32 devices in a mesh: row: 4 (over z), col: 8 (over y, x, core).
Axes of the slice: x: 2, y: 2, z: 4, core: 2. Of those that a mesh axis runs over, the one named last changes fastest.
Arguments:
- stored_blocks: float32 [4, 8, 2, 14, 256, 256], P('row', 'col'), may hold values from -0.0390625 to 0.0390625
- onsite: float32 [4, 8, 2, 256], P('row', 'col'), may hold values from 0.05 to 0.95
- bond_mask: int32 [4, 8, 2, 13], P('row', 'col'), may hold values 0 or 1
Outputs:
- purified: float32 [4, 8, 2, 14, 256, 256], P('row', 'col')
The draws below stay inside these ranges and needn't reach their ends.
All inputs are finite; a program needn't handle non-finite values. No bound on the sum of `bond_mask` on one device may be relied on, other than what follows from the above.
Results may differ from the reference program's by a relative error of at most 0.00024.
Values sent between devices are 32-bit elements; how exact they have to be, the bound alone decides.
No kernel may reach another device: no remote copies, remote signals or barrier semaphores. Data moves between devices by JAX's collectives and lax.ppermute only.
A program may use at most 448 MiB of HBM per device.

```python
import jax
import jax.numpy as jnp
from jax import lax

B = 256
SLOTS = 14
NOFF = 13
NX = 4
NY = 8
NZ = 2
NOCC = 8192


def touch_ends(result, key, low, top_value):
    longest = result.shape.index(max(result.shape))
    spots = []
    for shift in (0, 1):
        where = [jax.random.randint(jax.random.fold_in(key, axis), (), 0, length) for axis, length in enumerate(result.shape)]
        where[longest] = (where[longest] + shift) % result.shape[longest]
        spots.append(tuple(where))
    return result.at[spots[0]].set(low).at[spots[1]].set(top_value)


def levels(rng, extent, pieces, least, high):
    loudness, own = 1.0, jax.random.fold_in(rng, 6)
    for axis_at, shards_of in pieces:
        steps = jnp.exp(jax.random.uniform(jax.random.fold_in(own, axis_at), (shards_of,), jnp.float32, least / len(pieces), high / len(pieces)))
        loudness = loudness * jnp.repeat(steps, extent[axis_at] // shards_of).reshape([-1 if axis == axis_at else 1 for axis in range(len(extent))])
    return loudness


def normal_values(rng, extent, spread, most, shards=(), held_as=jnp.bfloat16):
    values = spread * jax.random.normal(rng, extent, jnp.float32)
    if shards:
        values = values * levels(rng, extent, shards, -0.22, 0.18)
    return jnp.clip(values, -most, most).astype(held_as)


def setup_inputs(seed: int = 0) -> dict:
    seeds = jax.random.split(jax.random.key(seed), 4)
    stored_blocks = normal_values(seeds[0], (NX, NY, NZ, SLOTS, B, B), ((88 * B) ** -0.5), 0.0390625, ((0, 4), (1, 8)), jnp.float32)
    onsite = jnp.clip(0.05 + 0.9 * jax.random.uniform(seeds[1], (NX, NY, NZ, B), jnp.float32) ** levels(seeds[1], (NX, NY, NZ, B), ((0, 4), (1, 8)), -0.2, 0.2), 0.05, 0.95)
    bond_mask = touch_ends((jax.random.randint(seeds[2], (NX, NY, NZ, NOFF), 0, 13) < 7).astype(jnp.int32), jax.random.fold_in(seeds[2], 1), 0, 1)
    return dict(stored_blocks=stored_blocks, onsite=onsite, bond_mask=bond_mask)


def offset_list():
    return [(step_x, step_y, step_z) for step_x in (-1, 0, 1) for step_y in (-1, 0, 1) for step_z in (-1, 0, 1) if (step_x, step_y, step_z) > (0, 0, 0)]


def slot_number(offset):
    return offset_list().index(offset) + 1


def shift_cells(array, step_x, step_y, step_z):
    moved = jnp.roll(array, (-step_x, -step_y), axis=(0, 1))
    if step_z == 1:
        moved = jnp.concatenate([moved[:, :, 1:], jnp.zeros_like(moved[:, :, :1])], axis=2)
    elif step_z == -1:
        moved = jnp.concatenate([jnp.zeros_like(moved[:, :, :1]), moved[:, :, :-1]], axis=2)
    return moved


def stored_at(blocks_list, offset):
    if offset == (0, 0, 0):
        return blocks_list[0]
    if offset > (0, 0, 0):
        return blocks_list[slot_number(offset)]
    mirror = (-offset[0], -offset[1], -offset[2])
    return jnp.swapaxes(shift_cells(blocks_list[slot_number(mirror)], offset[0], offset[1], offset[2]), 3, 4)


def reference(stored_blocks, onsite, bond_mask):
    offsets = offset_list()
    zplace = jnp.arange(NZ)
    leading = stored_blocks[:, :, :, 0]
    diagonal = 0.5 * (leading + jnp.swapaxes(leading, 3, 4)) + jnp.eye(B, dtype=jnp.float32) * onsite[..., None, :]
    blocks_list = [diagonal]
    keep_list = [jnp.ones(onsite.shape[:3], jnp.float32)]
    for position, offset in enumerate(offsets):
        inside = ((zplace + offset[2] >= 0) & (zplace + offset[2] < NZ)).astype(jnp.float32)
        keep_now = bond_mask[..., position].astype(jnp.float32) * inside[None, None, :]
        keep_list.append(keep_now)
        blocks_list.append(stored_blocks[:, :, :, position + 1] * keep_now[..., None, None])
    trace_one = jnp.sum(jnp.trace(diagonal, axis1=3, axis2=4))
    trace_two = jnp.sum(diagonal * diagonal)
    for blocks_now in blocks_list[1:]:
        trace_two = trace_two + 2.0 * jnp.sum(blocks_now * blocks_now)
    all_offsets = [(step_x, step_y, step_z) for step_x in (-1, 0, 1) for step_y in (-1, 0, 1) for step_z in (-1, 0, 1)]
    squares = []
    for target_offset in [(0, 0, 0)] + offsets:
        running = jnp.zeros_like(diagonal)
        for middle in all_offsets:
            remainder = (target_offset[0] - middle[0], target_offset[1] - middle[1], target_offset[2] - middle[2])
            if max(abs(remainder[0]), abs(remainder[1]), abs(remainder[2])) > 1:
                continue
            left_term = stored_at(blocks_list, middle)
            right_term = shift_cells(stored_at(blocks_list, remainder), middle[0], middle[1], middle[2])
            running = running + jnp.einsum("xyzab,xyzbc->xyzac", left_term, right_term, precision=lax.Precision.HIGHEST)
        squares.append(running)
    steering = jax.nn.sigmoid((jnp.abs(trace_two - NOCC) - jnp.abs(2.0 * trace_one - trace_two - NOCC)) / B)
    outputs = []
    for slot_id in range(len(blocks_list)):
        mixed = squares[slot_id] + 2.0 * steering * (blocks_list[slot_id] - squares[slot_id])
        outputs.append(keep_list[slot_id][..., None, None] * mixed)
    return jnp.stack(outputs, axis=3)
```

```python
import functools

import jax
import jax.numpy as jnp
from jax import lax
from jax.experimental import pallas as pl
from jax.experimental.pallas import tpu as pltpu
from jax.sharding import PartitionSpec as P


F32 = jnp.float32
BF16 = jnp.bfloat16
NN = ((1,), (0,))
NT = ((1,), (1,))
TN = ((0,), (0,))
IN_PLANE = {"C": (0, 0), "N": (0, 1), "S": (1, -1), "E": (1, 0), "D": (1, 1)}


def offset_list():
    steps = (-1, 0, 1)
    return [(i, j, k) for i in steps for j in steps for k in steps if (i, j, k) > (0, 0, 0)]


def slot_number(offset):
    return offset_list().index(offset) + 1


def panel_blocks(name, layers):
    side = IN_PLANE[name]
    found = []
    for low in range(layers):
        for high in range(layers):
            step = high - low
            if abs(step) <= 1 and (*side, step) > (0, 0, 0):
                found.append((low, high, slot_number((*side, step))))
    return found


def sym_rows(layers, size):
    return (layers * (layers - 1) // 2 + (layers + 1) // 2) * size + 8 * (layers // 2)


def rows_cols(size):
    return (
        lax.broadcasted_iota(jnp.int32, (size, size), 0),
        lax.broadcasted_iota(jnp.int32, (size, size), 1),
    )


def put_sym(ref, get, layers, size):
    row, col = rows_cols(size)
    at = 0
    for a in range(layers):
        for b in range(a + 1, layers):
            ref[at : at + size, :] = get(a, b)
            at += size
    marks = []
    for a in range(0, layers, 2):
        block = get(a, a)
        if a + 1 < layers:
            other = get(a + 1, a + 1)
            marks.append(jnp.sum(jnp.where(row == col, other, 0.0), axis=0, keepdims=True))
            block = jnp.where(row <= col, block, other)
        ref[at : at + size, :] = block
        at += size
    for mark in marks:
        ref[at : at + 8, :] = jnp.broadcast_to(mark, (8, size))
        at += 8


def take_sym(packed, layers, size):
    row, col = rows_cols(size)
    blocks = {}
    at = 0
    for a in range(layers):
        for b in range(a + 1, layers):
            blocks[a, b] = packed[at : at + size, :]
            at += size
    marks_at = at + (layers + 1) // 2 * size
    for a in range(0, layers, 2):
        block = packed[at : at + size, :]
        at += size
        if a + 1 < layers:
            flipped = block.T
            mark = packed[marks_at : marks_at + 1, :]
            marks_at += 8
            blocks[a, a] = jnp.where(row <= col, block, flipped)
            blocks[a + 1, a + 1] = jnp.where(row == col, mark, jnp.where(row < col, flipped, block))
        else:
            blocks[a, a] = block
    return blocks


def whole_sym(blocks, layers):
    rows = []
    for a in range(layers):
        rows.append(
            jnp.concatenate(
                [blocks[a, b] if a <= b else blocks[b, a].T for b in range(layers)], axis=1
            )
        )
    return jnp.concatenate(rows, axis=0)


def split(value):
    high = value.astype(BF16)
    return high, (value - high.astype(F32)).astype(BF16)


def dot3(a, b, dims):
    go = functools.partial(lax.dot_general, dimension_numbers=(dims, ((), ())), preferred_element_type=F32)
    return go(a[0], b[0]) + (go(a[0], b[1]) + go(a[1], b[0]))


def cut(pair, at, size):
    return tuple(part[at : at + size, :] for part in pair)


def sym_product(pair, layers, size, dims):
    blocks = {}
    for a in range(layers):
        if dims == NT:
            left = tuple(part[a * size : (a + 1) * size, :] for part in pair)
            right = tuple(part[a * size :, :] for part in pair)
        else:
            left = tuple(part[:, a * size : (a + 1) * size] for part in pair)
            right = tuple(part[:, a * size :] for part in pair)
        strip = dot3(left, right, dims)
        for b in range(a, layers):
            blocks[a, b] = strip[:, (b - a) * size : (b - a + 1) * size]
    return blocks


def kept(mask_ref, layer, slot):
    return mask_ref[layer, slot - 1] > 0


def load_panel(out_ref, held, first, name, layers, size, mask_ref, flip=False):
    blocks = panel_blocks(name, layers)
    if layers > 2 or name == "C":
        out_ref[...] = jnp.zeros(out_ref.shape, F32)
    for k, (low, high, slot) in enumerate(blocks):
        value = jnp.where(kept(mask_ref, low, slot), held[first + k], 0.0)
        if flip:
            low, high, value = high, low, value.T
        out_ref[low * size : (low + 1) * size, high * size : (high + 1) * size] = value
    return len(blocks)


def start_loads(stored_ref, held, sems, wanted):
    copies = [
        pltpu.make_async_copy(stored_ref.at[low, slot], held.at[k], sems.at[k])
        for k, (low, slot) in enumerate(wanted)
    ]
    for copy in copies:
        copy.start()
    return copies


def pack_t_wanted(layers):
    return (
        [(low, slot) for low, _, slot in panel_blocks("N", layers)]
        + [(layer, 0) for layer in range(layers)]
        + [(low, slot) for low, _, slot in panel_blocks("C", layers)]
    )


def pack_t_body(layers, size, mask_ref, stored_ref, onsite_ref, n_ref, packed_ref, c_ref, held, sems):
    for copy in start_loads(stored_ref, held, sems, pack_t_wanted(layers)):
        copy.wait()
    at = load_panel(n_ref, held, 0, "N", layers, size, mask_ref)
    row, col = rows_cols(size)
    c_ref[...] = jnp.zeros(c_ref.shape, F32)
    for layer in range(layers):
        block = held[at + layer]
        block = 0.5 * (block + block.T) + jnp.where(row == col, onsite_ref[layer : layer + 1, :], 0.0)
        c_ref[layer * size : (layer + 1) * size, layer * size : (layer + 1) * size] = block
    at += layers
    for k, (low, high, slot) in enumerate(panel_blocks("C", layers)):
        block = jnp.where(kept(mask_ref, low, slot), held[at + k], 0.0)
        c_ref[low * size : (low + 1) * size, high * size : (high + 1) * size] = block
        c_ref[high * size : (high + 1) * size, low * size : (low + 1) * size] = block.T
    put_sym(
        packed_ref,
        lambda a, b: c_ref[a * size : (a + 1) * size, b * size : (b + 1) * size],
        layers,
        size,
    )


def pack_e_wanted(layers):
    return [(low, slot) for name in "SED" for low, _, slot in panel_blocks(name, layers)]


def pack_e_body(layers, size, mask_ref, stored_ref, st_ref, e_ref, d_ref, held, sems):
    for copy in start_loads(stored_ref, held, sems, pack_e_wanted(layers)):
        copy.wait()
    at = load_panel(st_ref, held, 0, "S", layers, size, mask_ref, flip=True)
    at += load_panel(e_ref, held, at, "E", layers, size, mask_ref)
    load_panel(d_ref, held, at, "D", layers, size, mask_ref)


def up_body(layers, size, n_ref, d_ref, gc_ref, yc_ref):
    for panel, out_ref in ((d_ref, gc_ref), (n_ref, yc_ref)):
        blocks = sym_product(split(panel[...]), layers, size, TN)
        put_sym(out_ref, lambda a, b: blocks[a, b], layers, size)


def local_g_body(layers, size, n_ref, e_ref, d_ref, gc_ref, gn_ref, rs_ref, re_ref):
    n, e, d = split(n_ref[...]), split(e_ref[...]), split(d_ref[...])
    blocks = sym_product(e, layers, size, TN)
    put_sym(gc_ref, lambda a, b: blocks[a, b], layers, size)
    gn_ref[...] = dot3(e, d, TN)
    rs_ref[...] = dot3(n, e, TN)
    re_ref[...] = dot3(n, d, TN)


def local_y_body(
    layers, size, c_ref, n_ref, st_ref, e_ref, d_ref, yc_ref, yn_ref, ys_ref, ye_ref, yd_ref, sums_ref
):
    row, col = rows_cols(c_ref.shape[0])
    c_now = c_ref[...]
    trace = jnp.sum(jnp.where(row == col, c_now, 0.0))
    squares = jnp.sum(c_now * c_now)
    for ref in (n_ref, st_ref, e_ref, d_ref):
        value = ref[...]
        squares = squares + 2.0 * jnp.sum(value * value)
    line = lax.broadcasted_iota(jnp.int32, sums_ref.shape, 0)
    sums_ref[...] = jnp.where(line == 0, trace, squares)
    c, n, st, e, d = (split(ref[...]) for ref in (c_ref, n_ref, st_ref, e_ref, d_ref))
    yn_ref[...] = dot3(c, n, NN)
    ys_ref[...] = dot3(c, st, NT)
    ye_ref[...] = dot3(c, e, NN)
    yd_ref[...] = dot3(c, d, NN)
    terms = [
        sym_product(pair, layers, size, dims)
        for pair, dims in ((c, NT), (n, NT), (st, TN), (e, NT), (d, NT))
    ]
    put_sym(yc_ref, lambda a, b: sum(term[a, b] for term in terms), layers, size)


def g_body(layers, size, gc0_ref, gn0_ref, stu_ref, eu_ref, up_ref, gc_ref, gn_ref):
    stu, eu = split(stu_ref[...]), split(eu_ref[...])
    blocks = sym_product(stu, layers, size, NT)
    put_sym(gc_ref, lambda a, b: blocks[a, b], layers, size)
    gc_ref[...] += gc0_ref[...] + up_ref[...]
    gn_ref[...] = gn0_ref[...] + dot3(stu, eu, NN)


def r_body(layers, size, rs0_ref, re0_ref, stu_ref, eu_ref, cx_ref, nx_ref, rs_ref, re_ref):
    su, eu, nx = split(stu_ref[...].T), split(eu_ref[...]), split(nx_ref[...])
    cx = split(whole_sym(take_sym(cx_ref, layers, size), layers))
    rs_ref[...] = rs0_ref[...] + dot3(su, cx, NN) + dot3(eu, nx, NT)
    re_ref[...] = re0_ref[...] + dot3(su, nx, NN)


def middle_body(
    layers, size, n_ref, e_ref, d_ref, stu_ref, eu_ref, cu_ref, cx_ref, nx_ref, yn0_ref, ye0_ref, yd0_ref,
    yn_ref, ye_ref, yd_ref,
):
    n, e, d = split(n_ref[...]), split(e_ref[...]), split(d_ref[...])
    stu, eu, nx = split(stu_ref[...]), split(eu_ref[...]), split(nx_ref[...])
    cu = split(whole_sym(take_sym(cu_ref, layers, size), layers))
    yn_ref[...] = yn0_ref[...] + dot3(n, cu, NN) + dot3(e, stu, NN) + dot3(d, eu, NT)
    cx = split(whole_sym(take_sym(cx_ref, layers, size), layers))
    ye_ref[...] = ye0_ref[...] + dot3(n, stu, NT) + dot3(e, cx, NN) + dot3(d, nx, NT)
    yd_ref[...] = yd0_ref[...] + dot3(n, eu, NN) + dot3(e, nx, NN)


def last_body(
    layers, size, mask_ref, h_ref, c_ref, n_ref, st_ref, e_ref, d_ref,
    yc_ref, yn_ref, ys_ref, ye_ref, yd_ref, cxu_ref, ycu_ref, gc_ref, gn_ref, rs_ref, re_ref, out_ref,
):
    twice = 2.0 * h_ref[0]
    slots = out_ref.shape[1]

    def mixed(y, a):
        return y + twice * (a - y)

    c_blocks = take_sym(yc_ref[...] + ycu_ref[...] + gc_ref[...], layers, size)
    done = set()
    for layer in range(layers):
        here = slice(layer * size, (layer + 1) * size)
        out_ref[layer, 0] = mixed(c_blocks[layer, layer], c_ref[here, here])
        done.add((layer, 0))
    for low, high, slot in panel_blocks("C", layers):
        a = c_ref[low * size : (low + 1) * size, high * size : (high + 1) * size]
        out_ref[low, slot] = jnp.where(kept(mask_ref, low, slot), mixed(c_blocks[low, high], a), 0.0)
        done.add((low, slot))
    cxu = split(whole_sym(take_sym(cxu_ref, layers, size), layers))
    yd_ref[...] += dot3(split(d_ref[...]), cxu, NN)
    for name, a_ref, terms in (
        ("N", n_ref, (yn_ref, gn_ref)),
        ("S", st_ref, (ys_ref, rs_ref)),
        ("E", e_ref, (ye_ref, re_ref)),
        ("D", d_ref, (yd_ref,)),
    ):
        for low, high, slot in panel_blocks(name, layers):
            rows, cols = slice(low * size, (low + 1) * size), slice(high * size, (high + 1) * size)
            y = sum(ref[rows, cols] for ref in terms)
            a = a_ref[cols, rows].T if name == "S" else a_ref[rows, cols]
            out_ref[low, slot] = jnp.where(kept(mask_ref, low, slot), mixed(y, a), 0.0)
            done.add((low, slot))
    for layer in range(layers):
        for slot in range(slots):
            if (layer, slot) not in done:
                out_ref[layer, slot] = jnp.zeros((size, size), F32)


def call(body, layers, size, outs, spaces, products, scratch=(), limit=40):
    n = layers * size
    return pl.pallas_call(
        functools.partial(body, layers, size),
        out_shape=[jax.ShapeDtypeStruct(shape, F32) for shape in outs],
        in_specs=[pl.BlockSpec(memory_space=space) for space in spaces],
        out_specs=[pl.BlockSpec(memory_space=pltpu.VMEM)] * len(outs),
        scratch_shapes=list(scratch),
        compiler_params=pltpu.CompilerParams(vmem_limit_bytes=limit << 20),
        cost_estimate=pl.CostEstimate(
            flops=int(products * 6 * n**3), bytes_accessed=4 * n * n * (len(outs) + len(spaces)), transcendentals=0
        ),
    )


def passed_along(value, axis, by):
    peers = lax.axis_size(axis)
    return lax.ppermute(value, axis, [(i, (i + by) % peers) for i in range(peers)])


def summed(value, axis):
    peers = lax.axis_size(axis)
    if peers & (peers - 1):
        return value + sum(passed_along(value, axis, by) for by in range(1, peers))
    by = 1
    while by < peers:
        value = value + passed_along(value, axis, by)
        by *= 2
    return value


def shards(stored_blocks, onsite, bond_mask):
    stored, onsite, mask = stored_blocks[0, 0], onsite[0, 0], bond_mask[0, 0]
    layers, slots, size = stored.shape[:3]
    n = layers * size
    panel, packed = (n, n), (sym_rows(layers, size), size)
    vmem, smem, anywhere = pltpu.VMEM, pltpu.SMEM, pl.ANY

    def loads(count):
        return [pltpu.VMEM((count, size, size), F32), pltpu.SemaphoreType.DMA((count,))]

    go = functools.partial(call, layers=layers, size=size)
    N, Cp, C = go(
        pack_t_body, outs=[panel, packed, panel], spaces=[smem, anywhere, vmem], products=0.1,
        scratch=loads(len(pack_t_wanted(layers))), limit=16,
    )(mask, stored, onsite)
    N_x, Cp_x = passed_along(N, "row", -1), passed_along(Cp, "row", -1)
    St, E, D = go(
        pack_e_body, outs=[panel] * 3, spaces=[smem, anywhere], products=0.1,
        scratch=loads(len(pack_e_wanted(layers))), limit=16,
    )(mask, stored)
    St_u, E_u, Cp_u = (passed_along(value, "col", -1) for value in (St, E, Cp))
    gc_up, yc_up = go(up_body, outs=[packed] * 2, spaces=[vmem] * 2, products=2, limit=16)(N, D)
    gc_up, yc_up = passed_along(gc_up, "col", 1), passed_along(yc_up, "col", 1)
    gc, gn, rs, re = go(local_g_body, outs=[packed, panel, panel, panel], spaces=[vmem] * 3, products=4, limit=24)(N, E, D)
    yc, yn, ys, ye, yd, sums = go(
        local_y_body, outs=[packed] + [panel] * 4 + [(8, 128)], spaces=[vmem] * 5, products=8
    )(C, N, St, E, D)
    sums = summed(summed(sums, "row"), "col")
    gc, gn = go(g_body, outs=[packed, panel], spaces=[vmem] * 5, products=2, limit=24)(gc, gn, St_u, E_u, gc_up)
    gc, gn = passed_along(gc, "row", 1), passed_along(gn, "row", 1)
    Cp_xu = passed_along(Cp_x, "col", -1)
    rs, re = go(r_body, outs=[panel] * 2, spaces=[vmem] * 6, products=3, limit=24)(rs, re, St_u, E_u, Cp_x, N_x)
    rs, re = passed_along(rs, "col", 1), passed_along(re, "col", 1)
    yn, ye, yd = go(middle_body, outs=[panel] * 3, spaces=[vmem] * 11, products=8)(
        N, E, D, St_u, E_u, Cp_u, Cp_x, N_x, yn, ye, yd
    )
    cells = lax.axis_size("row") * lax.axis_size("col") * layers
    target = float(cells * size // 2)
    t1, t2 = sums[0, 0], sums[1, 0]
    steering = jax.nn.sigmoid((jnp.abs(t2 - target) - jnp.abs(2.0 * t1 - t2 - target)) / size)
    (out,) = go(last_body, outs=[(layers, slots, size, size)], spaces=[smem] * 2 + [vmem] * 16, products=1, limit=56)(
        mask, steering[None], C, N, St, E, D, yc, yn, ys, ye, yd, Cp_xu, yc_up, gc, gn, rs, re
    )
    return out[None, None]


def solution(mesh):
    in_specs = (
        P("row", "col", None, None, None, None),
        P("row", "col", None, None),
        P("row", "col", None, None),
    )
    out_specs = P("row", "col", None, None, None, None)
    return jax.shard_map(shards, mesh=mesh, in_specs=in_specs, out_specs=out_specs, check_vma=False)
```

```python
import functools

import jax
import jax.numpy as jnp
from jax import lax
from jax.experimental import pallas as pl
from jax.experimental.pallas import tpu as pltpu
from jax.sharding import PartitionSpec as P


F32 = jnp.float32
BF16 = jnp.bfloat16
NN = ((1,), (0,))
NT = ((1,), (1,))
TN = ((0,), (0,))
IN_PLANE = {"C": (0, 0), "N": (0, 1), "S": (1, -1), "E": (1, 0), "D": (1, 1)}


def offset_list():
    steps = (-1, 0, 1)
    return [(i, j, k) for i in steps for j in steps for k in steps if (i, j, k) > (0, 0, 0)]


def slot_number(offset):
    return offset_list().index(offset) + 1


def panel_blocks(name, layers):
    side = IN_PLANE[name]
    found = []
    for low in range(layers):
        for high in range(layers):
            step = high - low
            if abs(step) <= 1 and (*side, step) > (0, 0, 0):
                found.append((low, high, slot_number((*side, step))))
    return found


def sym_rows(layers, size):
    return (layers * (layers - 1) // 2 + (layers + 1) // 2) * size + 8 * (layers // 2)


def rows_cols(size):
    return (
        lax.broadcasted_iota(jnp.int32, (size, size), 0),
        lax.broadcasted_iota(jnp.int32, (size, size), 1),
    )


def put_sym(ref, get, layers, size):
    row, col = rows_cols(size)
    at = 0
    for a in range(layers):
        for b in range(a + 1, layers):
            ref[at : at + size, :] = get(a, b)
            at += size
    marks = []
    for a in range(0, layers, 2):
        block = get(a, a)
        if a + 1 < layers:
            other = get(a + 1, a + 1)
            marks.append(jnp.sum(jnp.where(row == col, other, 0.0), axis=0, keepdims=True))
            block = jnp.where(row <= col, block, other)
        ref[at : at + size, :] = block
        at += size
    for mark in marks:
        ref[at : at + 8, :] = jnp.broadcast_to(mark, (8, size))
        at += 8


def take_sym(packed, layers, size):
    row, col = rows_cols(size)
    blocks = {}
    at = 0
    for a in range(layers):
        for b in range(a + 1, layers):
            blocks[a, b] = packed[at : at + size, :]
            at += size
    marks_at = at + (layers + 1) // 2 * size
    for a in range(0, layers, 2):
        block = packed[at : at + size, :]
        at += size
        if a + 1 < layers:
            flipped = block.T
            mark = packed[marks_at : marks_at + 1, :]
            marks_at += 8
            blocks[a, a] = jnp.where(row <= col, block, flipped)
            blocks[a + 1, a + 1] = jnp.where(row == col, mark, jnp.where(row < col, flipped, block))
        else:
            blocks[a, a] = block
    return blocks


def whole_sym(blocks, layers):
    rows = []
    for a in range(layers):
        rows.append(
            jnp.concatenate(
                [blocks[a, b] if a <= b else blocks[b, a].T for b in range(layers)], axis=1
            )
        )
    return jnp.concatenate(rows, axis=0)


def split(value):
    high = value.astype(BF16)
    return high, (value - high.astype(F32)).astype(BF16)


def dot3(a, b, dims):
    go = functools.partial(lax.dot_general, dimension_numbers=(dims, ((), ())), preferred_element_type=F32)
    return go(a[0], b[0]) + (go(a[0], b[1]) + go(a[1], b[0]))


def cut(pair, at, size):
    return tuple(part[at : at + size, :] for part in pair)


def sym_product(pair, layers, size, dims):
    blocks = {}
    for a in range(layers):
        if dims == NT:
            left = tuple(part[a * size : (a + 1) * size, :] for part in pair)
            right = tuple(part[a * size :, :] for part in pair)
        else:
            left = tuple(part[:, a * size : (a + 1) * size] for part in pair)
            right = tuple(part[:, a * size :] for part in pair)
        strip = dot3(left, right, dims)
        for b in range(a, layers):
            blocks[a, b] = strip[:, (b - a) * size : (b - a + 1) * size]
    return blocks


def kept(mask_ref, layer, slot):
    return mask_ref[layer, slot - 1] > 0


def load_panel(out_ref, held, first, name, layers, size, mask_ref, flip=False):
    blocks = panel_blocks(name, layers)
    if layers > 2 or name == "C":
        out_ref[...] = jnp.zeros(out_ref.shape, F32)
    for k, (low, high, slot) in enumerate(blocks):
        value = jnp.where(kept(mask_ref, low, slot), held[first + k], 0.0)
        if flip:
            low, high, value = high, low, value.T
        out_ref[low * size : (low + 1) * size, high * size : (high + 1) * size] = value
    return len(blocks)


def start_loads(stored_ref, held, sems, wanted):
    copies = [
        pltpu.make_async_copy(stored_ref.at[low, slot], held.at[k], sems.at[k])
        for k, (low, slot) in enumerate(wanted)
    ]
    for copy in copies:
        copy.start()
    return copies


def pack_t_wanted(layers):
    return (
        [(low, slot) for low, _, slot in panel_blocks("N", layers)]
        + [(layer, 0) for layer in range(layers)]
        + [(low, slot) for low, _, slot in panel_blocks("C", layers)]
    )


def squares_of(refs):
    total = 0.0
    for ref in refs:
        value = ref[...]
        total = total + jnp.sum(value * value)
    return total


def pack_t_body(layers, size, mask_ref, stored_ref, onsite_ref, n_ref, packed_ref, c_ref, sums_ref, held, sems):
    for copy in start_loads(stored_ref, held, sems, pack_t_wanted(layers)):
        copy.wait()
    at = load_panel(n_ref, held, 0, "N", layers, size, mask_ref)
    row, col = rows_cols(size)
    c_ref[...] = jnp.zeros(c_ref.shape, F32)
    for layer in range(layers):
        block = held[at + layer]
        block = 0.5 * (block + block.T) + jnp.where(row == col, onsite_ref[layer : layer + 1, :], 0.0)
        c_ref[layer * size : (layer + 1) * size, layer * size : (layer + 1) * size] = block
    at += layers
    for k, (low, high, slot) in enumerate(panel_blocks("C", layers)):
        block = jnp.where(kept(mask_ref, low, slot), held[at + k], 0.0)
        c_ref[low * size : (low + 1) * size, high * size : (high + 1) * size] = block
        c_ref[high * size : (high + 1) * size, low * size : (low + 1) * size] = block.T
    put_sym(
        packed_ref,
        lambda a, b: c_ref[a * size : (a + 1) * size, b * size : (b + 1) * size],
        layers,
        size,
    )
    row, col = rows_cols(c_ref.shape[0])
    trace = jnp.sum(jnp.where(row == col, c_ref[...], 0.0))
    squares = squares_of([c_ref]) + 2.0 * squares_of([n_ref])
    line = lax.broadcasted_iota(jnp.int32, sums_ref.shape, 0)
    sums_ref[...] = jnp.where(line == 0, trace, squares)


def pack_e_wanted(layers):
    return [(low, slot) for name in "SED" for low, _, slot in panel_blocks(name, layers)]


def pack_e_body(layers, size, mask_ref, stored_ref, before_ref, st_ref, e_ref, d_ref, sums_ref, held, sems):
    for copy in start_loads(stored_ref, held, sems, pack_e_wanted(layers)):
        copy.wait()
    at = load_panel(st_ref, held, 0, "S", layers, size, mask_ref, flip=True)
    at += load_panel(e_ref, held, at, "E", layers, size, mask_ref)
    load_panel(d_ref, held, at, "D", layers, size, mask_ref)
    line = lax.broadcasted_iota(jnp.int32, sums_ref.shape, 0)
    sums_ref[...] = before_ref[...] + jnp.where(line == 0, 0.0, 2.0 * squares_of([st_ref, e_ref, d_ref]))


def own_sym_body(layers, size, panel_ref, out_ref):
    blocks = sym_product(split(panel_ref[...]), layers, size, TN)
    put_sym(out_ref, lambda a, b: blocks[a, b], layers, size)


def local_g_body(layers, size, n_ref, e_ref, d_ref, gc_ref, gn_ref, rs_ref, re_ref):
    n, e, d = split(n_ref[...]), split(e_ref[...]), split(d_ref[...])
    blocks = sym_product(e, layers, size, TN)
    put_sym(gc_ref, lambda a, b: blocks[a, b], layers, size)
    gn_ref[...] = dot3(e, d, TN)
    rs_ref[...] = dot3(n, e, TN)
    re_ref[...] = dot3(n, d, TN)


def local_y_body(layers, size, c_ref, n_ref, st_ref, e_ref, d_ref, yc_ref, yn_ref, ys_ref, ye_ref, yd_ref):
    c, n, st, e, d = (split(ref[...]) for ref in (c_ref, n_ref, st_ref, e_ref, d_ref))
    yn_ref[...] = dot3(c, n, NN)
    ys_ref[...] = dot3(c, st, NT)
    ye_ref[...] = dot3(c, e, NN)
    yd_ref[...] = dot3(c, d, NN)
    terms = [
        sym_product(pair, layers, size, dims)
        for pair, dims in ((c, NT), (n, NT), (st, TN), (e, NT), (d, NT))
    ]
    put_sym(yc_ref, lambda a, b: sum(term[a, b] for term in terms), layers, size)


def g_body(layers, size, gc0_ref, gn0_ref, stu_ref, eu_ref, up_ref, gc_ref, gn_ref):
    stu, eu = split(stu_ref[...]), split(eu_ref[...])
    blocks = sym_product(stu, layers, size, NT)
    put_sym(gc_ref, lambda a, b: blocks[a, b], layers, size)
    gc_ref[...] += gc0_ref[...] + up_ref[...]
    gn_ref[...] = gn0_ref[...] + dot3(stu, eu, NN)


def r_body(layers, size, rs0_ref, re0_ref, stu_ref, eu_ref, cx_ref, nx_ref, rs_ref, re_ref):
    su, eu, nx = split(stu_ref[...].T), split(eu_ref[...]), split(nx_ref[...])
    cx = split(whole_sym(take_sym(cx_ref, layers, size), layers))
    rs_ref[...] = rs0_ref[...] + dot3(su, cx, NN) + dot3(eu, nx, NT)
    re_ref[...] = re0_ref[...] + dot3(su, nx, NN)


def middle_body(
    layers, size, n_ref, e_ref, d_ref, stu_ref, eu_ref, cu_ref, cx_ref, nx_ref, yn0_ref, ye0_ref, yd0_ref,
    yn_ref, ye_ref, yd_ref,
):
    n, e, d = split(n_ref[...]), split(e_ref[...]), split(d_ref[...])
    stu, eu, nx = split(stu_ref[...]), split(eu_ref[...]), split(nx_ref[...])
    cu = split(whole_sym(take_sym(cu_ref, layers, size), layers))
    yn_ref[...] = yn0_ref[...] + dot3(n, cu, NN) + dot3(e, stu, NN) + dot3(d, eu, NT)
    cx = split(whole_sym(take_sym(cx_ref, layers, size), layers))
    ye_ref[...] = ye0_ref[...] + dot3(n, stu, NT) + dot3(e, cx, NN) + dot3(d, nx, NT)
    yd_ref[...] = yd0_ref[...] + dot3(n, eu, NN) + dot3(e, nx, NN)


def mix_body(
    layers, size, target, mask_ref, c_ref, n_ref, st_ref, e_ref, d_ref, yc_ref, yn_ref, ys_ref, ye_ref, yd_ref,
    cxu_ref, ycu_ref, *rest,
):
    *sums_refs, out_ref, pc_ref, pn_ref, ps_ref, pe_ref, scale_ref, held, zero, sems = rest
    sums = sum(ref[...] for ref in sums_refs)
    t1, t2 = sums[0:1, :], sums[1:2, :]
    twice = 2.0 * jax.nn.sigmoid((jnp.abs(t2 - target) - jnp.abs(2.0 * t1 - t2 - target)) / size)
    scale_ref[...] = jnp.broadcast_to(1.0 - twice, scale_ref.shape)
    slots = out_ref.shape[1]
    zero[...] = jnp.zeros(zero.shape, F32)
    written = {(layer, 0) for layer in range(layers)}
    for name in IN_PLANE:
        written |= {(low, slot) for low, _, slot in panel_blocks(name, layers)}
    copies = []
    for layer in range(layers):
        for slot in range(slots):
            if (layer, slot) not in written:
                copies.append(pltpu.make_async_copy(zero, out_ref.at[layer, slot], sems.at[len(copies)]))
                copies[-1].start()

    def mixed(y, a):
        return y + twice * (a - y)

    cxu = split(whole_sym(take_sym(cxu_ref, layers, size), layers))
    yd = yd_ref[...] + dot3(split(d_ref[...]), cxu, NN)
    for k, (low, high, slot) in enumerate(panel_blocks("D", layers)):
        rows, cols = slice(low * size, (low + 1) * size), slice(high * size, (high + 1) * size)
        held[k] = jnp.where(kept(mask_ref, low, slot), mixed(yd[rows, cols], d_ref[rows, cols]), 0.0)
        copies.append(pltpu.make_async_copy(held.at[k], out_ref.at[low, slot], sems.at[len(copies)]))
        copies[-1].start()
    c_blocks = take_sym(yc_ref[...] + ycu_ref[...], layers, size)
    put_sym(
        pc_ref,
        lambda a, b: mixed(c_blocks[a, b], c_ref[a * size : (a + 1) * size, b * size : (b + 1) * size]),
        layers,
        size,
    )
    for layer in range(layers):
        for name, y_ref, a_ref, p_ref in (
            ("N", yn_ref, n_ref, pn_ref),
            ("S", ys_ref, st_ref, ps_ref),
            ("E", ye_ref, e_ref, pe_ref),
        ):
            rows = slice(layer * size, (layer + 1) * size)
            for other in range(layers):
                cols = slice(other * size, (other + 1) * size)
                a = a_ref[cols, rows].T if name == "S" else a_ref[rows, cols]
                p_ref[rows, cols] = mixed(y_ref[rows, cols], a)
    for copy in copies:
        copy.wait()


def mix_body_for(target, layers, size, *refs):
    mix_body(layers, size, target, *refs)


def side_body(names, layers, size, mask_ref, _, scale_ref, *rest):
    refs, (out_ref, held, sems) = rest[: 2 * len(names)], rest[2 * len(names) :]
    scale = scale_ref[0:1, :]
    copies = []

    def send(value, low, slot):
        k = len(copies)
        held[k] = value
        copies.append(pltpu.make_async_copy(held.at[k], out_ref.at[low, slot], sems.at[k]))
        copies[-1].start()

    for at, name in enumerate(names):
        p_ref, late_ref = refs[2 * at], refs[2 * at + 1]
        if name == "C":
            blocks = take_sym(p_ref[...] + scale * late_ref[...], layers, size)
            for layer in range(layers):
                send(blocks[layer, layer], layer, 0)
        for low, high, slot in panel_blocks(name, layers):
            rows, cols = slice(low * size, (low + 1) * size), slice(high * size, (high + 1) * size)
            value = blocks[low, high] if name == "C" else p_ref[rows, cols] + scale * late_ref[rows, cols]
            send(jnp.where(kept(mask_ref, low, slot), value, 0.0), low, slot)
    for copy in copies:
        copy.wait()


def call(body, layers, size, outs, spaces, products, scratch=(), limit=40, out_spaces=None, aliases=None):
    n = layers * size
    return pl.pallas_call(
        functools.partial(body, layers, size),
        out_shape=[jax.ShapeDtypeStruct(shape, F32) for shape in outs],
        in_specs=[pl.BlockSpec(memory_space=space) for space in spaces],
        out_specs=[pl.BlockSpec(memory_space=space) for space in out_spaces or [pltpu.VMEM] * len(outs)],
        scratch_shapes=list(scratch),
        input_output_aliases=aliases or {},
        compiler_params=pltpu.CompilerParams(vmem_limit_bytes=limit << 20),
        cost_estimate=pl.CostEstimate(
            flops=int(products * 6 * n**3), bytes_accessed=4 * n * n * (len(outs) + len(spaces)), transcendentals=0
        ),
    )


def passed_along(value, axis, by):
    peers = lax.axis_size(axis)
    return lax.ppermute(value, axis, [(i, (i + by) % peers) for i in range(peers)])


def shards(stored_blocks, onsite, bond_mask):
    stored, onsite, mask = stored_blocks[0, 0], onsite[0, 0], bond_mask[0, 0]
    layers, slots, size = stored.shape[:3]
    n = layers * size
    panel, packed, sums = (n, n), (sym_rows(layers, size), size), (8, size)
    vmem, smem, hbm = pltpu.VMEM, pltpu.SMEM, pltpu.HBM

    def blocks(count):
        return [pltpu.VMEM((count, size, size), F32), pltpu.SemaphoreType.DMA((count,))]

    go = functools.partial(call, layers=layers, size=size)
    N, Cp, C, own = go(
        pack_t_body, outs=[panel, packed, panel, sums], spaces=[smem, hbm, vmem], products=0.1,
        scratch=blocks(len(pack_t_wanted(layers))), limit=16,
    )(mask, stored, onsite)
    N_x, Cp_x = passed_along(N, "row", -1), passed_along(Cp, "row", -1)
    St, E, D, own = go(
        pack_e_body, outs=[panel] * 3 + [sums], spaces=[smem, hbm, vmem], products=0.1,
        scratch=blocks(len(pack_e_wanted(layers))), limit=16,
    )(mask, stored, own)
    St_u, E_u = passed_along(St, "col", -1), passed_along(E, "col", -1)
    (gc_up,) = go(own_sym_body, outs=[packed], spaces=[vmem], products=1, limit=16)(D)
    gc_up = passed_along(gc_up, "col", 1)
    Cp_u = passed_along(Cp, "col", -1)
    (yc_up,) = go(own_sym_body, outs=[packed], spaces=[vmem], products=1, limit=16)(N)
    yc_up = passed_along(yc_up, "col", 1)
    own = own + sum(passed_along(own, "col", by) for by in range(1, lax.axis_size("col")))
    gc, gn, rs, re = go(local_g_body, outs=[packed, panel, panel, panel], spaces=[vmem] * 3, products=4, limit=24)(N, E, D)
    yc, yn, ys, ye, yd = go(local_y_body, outs=[packed] + [panel] * 4, spaces=[vmem] * 5, products=8)(C, N, St, E, D)
    gc, gn = go(g_body, outs=[packed, panel], spaces=[vmem] * 5, products=2, limit=24)(gc, gn, St_u, E_u, gc_up)
    gc = passed_along(gc, "row", 1)
    every = [own] + [passed_along(own, "row", by) for by in range(1, lax.axis_size("row"))]
    gn = passed_along(gn, "row", 1)
    Cp_xu = passed_along(Cp_x, "col", -1)
    rs, re = go(r_body, outs=[panel] * 2, spaces=[vmem] * 6, products=3, limit=24)(rs, re, St_u, E_u, Cp_x, N_x)
    rs, re = passed_along(rs, "col", 1), passed_along(re, "col", 1)
    yn, ye, yd = go(middle_body, outs=[panel] * 3, spaces=[vmem] * 11, products=8)(
        N, E, D, St_u, E_u, Cp_u, Cp_x, N_x, yn, ye, yd
    )
    cells = lax.axis_size("row") * lax.axis_size("col") * layers
    stack = (layers, slots, size, size)
    count = len(panel_blocks("D", layers))
    out, pc, pn, ps, pe, scale = go(
        functools.partial(mix_body_for, float(cells * size // 2)),
        outs=[stack, packed, panel, panel, panel, sums], out_spaces=[hbm] + [vmem] * 5,
        spaces=[smem] + [vmem] * (12 + len(every)), products=1,
        scratch=[pltpu.VMEM((count, size, size), F32), pltpu.VMEM((size, size), F32), pltpu.SemaphoreType.DMA((layers * slots,))],
    )(mask, C, N, St, E, D, yc, yn, ys, ye, yd, Cp_xu, yc_up, *every)
    for names, terms in ((("S", "E"), (ps, rs, pe, re)), (("C", "N"), (pc, gc, pn, gn))):
        count = sum(len(panel_blocks(name, layers)) for name in names) + layers * ("C" in names)
        (out,) = go(
            functools.partial(side_body, names), outs=[stack], out_spaces=[hbm], spaces=[smem, hbm] + [vmem] * 5,
            products=0.1, scratch=blocks(count), limit=16, aliases={1: 0},
        )(mask, out, scale, *terms)
    return out[None, None]


def solution(mesh):
    in_specs = (
        P("row", "col", None, None, None, None),
        P("row", "col", None, None),
        P("row", "col", None, None),
    )
    out_specs = P("row", "col", None, None, None, None)
    return jax.shard_map(shards, mesh=mesh, in_specs=in_specs, out_specs=out_specs, check_vma=False)
```

```python
import functools

import jax
import jax.numpy as jnp
from jax import lax
from jax.experimental import pallas as pl
from jax.experimental.pallas import tpu as pltpu
from jax.sharding import PartitionSpec as P


F32 = jnp.float32
BF16 = jnp.bfloat16
NN = ((1,), (0,))
NT = ((1,), (1,))
TN = ((0,), (0,))
IN_PLANE = {"C": (0, 0), "N": (0, 1), "S": (1, -1), "E": (1, 0), "D": (1, 1)}


def offset_list():
    steps = (-1, 0, 1)
    return [(i, j, k) for i in steps for j in steps for k in steps if (i, j, k) > (0, 0, 0)]


def slot_number(offset):
    return offset_list().index(offset) + 1


def panel_blocks(name, layers):
    side = IN_PLANE[name]
    found = []
    for low in range(layers):
        for high in range(layers):
            step = high - low
            if abs(step) <= 1 and (*side, step) > (0, 0, 0):
                found.append((low, high, slot_number((*side, step))))
    return found


def sym_rows(layers, size):
    blocks = layers * (layers - 1) // 2 + (layers + 1) // 2
    return -(-blocks // layers) * size + 8


def rows_cols(size):
    return (
        lax.broadcasted_iota(jnp.int32, (size, size), 0),
        lax.broadcasted_iota(jnp.int32, (size, size), 1),
    )


def block_slices(k, layers, size):
    row, col = k // layers * size, k % layers * size
    return slice(row, row + size), slice(col, col + size)


def sym_places(layers):
    above = [(a, b) for a in range(layers) for b in range(a + 1, layers)]
    pairs = list(range(0, layers, 2))
    return list(enumerate(above)), [(len(above) + k, k, a) for k, a in enumerate(pairs)]


def put_sym(ref, get, layers, size, first=0):
    row, col = rows_cols(size)
    above, pairs = sym_places(layers)
    last = first + sym_rows(layers, size) - 8

    def put(k, value):
        rows, cols = block_slices(k, layers, size)
        ref[first + rows.start : first + rows.stop, cols] = value

    ref[last : last + 8, :] = jnp.zeros((8, layers * size), F32)
    if len(above) + len(pairs) < (last - first) // size * layers:
        ref[last - size : last, :] = jnp.zeros((size, layers * size), F32)
    for k, (a, b) in above:
        put(k, get(a, b))
    for k, mark, a in pairs:
        block = get(a, a)
        if a + 1 < layers:
            other = get(a + 1, a + 1)
            line = jnp.sum(jnp.where(row == col, other, 0.0), axis=0, keepdims=True)
            ref[last : last + 8, mark * size : (mark + 1) * size] = jnp.broadcast_to(line, (8, size))
            block = jnp.where(row <= col, block, other)
        put(k, block)


def take_sym(packed, layers, size):
    row, col = rows_cols(size)
    above, pairs = sym_places(layers)
    last = sym_rows(layers, size) - 8
    blocks = {}
    for k, (a, b) in above:
        rows, cols = block_slices(k, layers, size)
        blocks[a, b] = packed[rows, cols]
    for k, mark, a in pairs:
        rows, cols = block_slices(k, layers, size)
        block = packed[rows, cols]
        if a + 1 < layers:
            flipped = block.T
            line = packed[last : last + 1, mark * size : (mark + 1) * size]
            blocks[a, a] = jnp.where(row <= col, block, flipped)
            blocks[a + 1, a + 1] = jnp.where(row == col, line, jnp.where(row < col, flipped, block))
        else:
            blocks[a, a] = block
    return blocks


def whole_sym(blocks, layers):
    rows = []
    for a in range(layers):
        rows.append(
            jnp.concatenate(
                [blocks[a, b] if a <= b else blocks[b, a].T for b in range(layers)], axis=1
            )
        )
    return jnp.concatenate(rows, axis=0)


def split(value):
    high = value.astype(BF16)
    return high, (value - high.astype(F32)).astype(BF16)


def dot3(a, b, dims):
    go = functools.partial(lax.dot_general, dimension_numbers=(dims, ((), ())), preferred_element_type=F32)
    return go(a[0], b[0]) + (go(a[0], b[1]) + go(a[1], b[0]))


def cut(pair, at, size):
    return tuple(part[at : at + size, :] for part in pair)


def sym_product(pair, layers, size, dims):
    blocks = {}
    for a in range(layers):
        if dims == NT:
            left = tuple(part[a * size : (a + 1) * size, :] for part in pair)
            right = tuple(part[a * size :, :] for part in pair)
        else:
            left = tuple(part[:, a * size : (a + 1) * size] for part in pair)
            right = tuple(part[:, a * size :] for part in pair)
        strip = dot3(left, right, dims)
        for b in range(a, layers):
            blocks[a, b] = strip[:, (b - a) * size : (b - a + 1) * size]
    return blocks


def kept(mask_ref, layer, slot):
    return mask_ref[layer, slot - 1] > 0


def load_panel(out_ref, held, first, name, layers, size, mask_ref, flip=False, top=0):
    blocks = panel_blocks(name, layers)
    if layers > 2:
        out_ref[top : top + layers * size, :] = jnp.zeros((layers * size, layers * size), F32)
    for k, (low, high, slot) in enumerate(blocks):
        value = jnp.where(kept(mask_ref, low, slot), held[first + k], 0.0)
        if flip:
            low, high, value = high, low, value.T
        out_ref[top + low * size : top + (low + 1) * size, high * size : (high + 1) * size] = value
    return len(blocks)


def start_loads(stored_ref, held, sems, wanted):
    copies = [
        pltpu.make_async_copy(stored_ref.at[low, slot], held.at[k], sems.at[k])
        for k, (low, slot) in enumerate(wanted)
    ]
    for copy in copies:
        copy.start()
    return copies


def squares_of(value):
    return jnp.sum(value * value)


def wanted_n(layers):
    return [(low, slot) for low, _, slot in panel_blocks("N", layers)]


def pack_n_body(layers, size, mask_ref, stored_ref, n_ref, held, sems):
    for copy in start_loads(stored_ref, held, sems, wanted_n(layers)):
        copy.wait()
    load_panel(n_ref, held, 0, "N", layers, size, mask_ref)


def wanted_rest(layers):
    return (
        [(layer, 0) for layer in range(layers)]
        + [(low, slot) for name in "CSED" for low, _, slot in panel_blocks(name, layers)]
    )


def pack_body(layers, size, mask_ref, stored_ref, onsite_ref, n_ref, packed_ref, down_ref, c_ref, d_ref, sums_ref, held, sems):
    n = layers * size
    copies = start_loads(stored_ref, held, sems, wanted_rest(layers))
    squares = squares_of(n_ref[...])
    row, col = rows_cols(size)
    at = layers + len(panel_blocks("C", layers))
    for copy in copies[:at]:
        copy.wait()
    c_ref[...] = jnp.zeros(c_ref.shape, F32)
    for layer in range(layers):
        block = held[layer]
        block = 0.5 * (block + block.T) + jnp.where(row == col, onsite_ref[layer : layer + 1, :], 0.0)
        c_ref[layer * size : (layer + 1) * size, layer * size : (layer + 1) * size] = block
    for k, (low, high, slot) in enumerate(panel_blocks("C", layers)):
        block = jnp.where(kept(mask_ref, low, slot), held[layers + k], 0.0)
        c_ref[low * size : (low + 1) * size, high * size : (high + 1) * size] = block
        c_ref[high * size : (high + 1) * size, low * size : (low + 1) * size] = block.T
    put_sym(
        packed_ref,
        lambda a, b: c_ref[a * size : (a + 1) * size, b * size : (b + 1) * size],
        layers,
        size,
    )
    down_ref[2 * n : 2 * n + sym_rows(layers, size), :] = packed_ref[...]
    for copy in copies[at:]:
        copy.wait()
    at += load_panel(down_ref, held, at, "S", layers, size, mask_ref, flip=True)
    at += load_panel(down_ref, held, at, "E", layers, size, mask_ref, top=n)
    load_panel(d_ref, held, at, "D", layers, size, mask_ref)
    row, col = rows_cols(n)
    c_now = c_ref[...]
    trace = jnp.sum(jnp.where(row == col, c_now, 0.0))
    squares = squares + squares_of(down_ref[: 2 * n, :]) + squares_of(d_ref[...])
    line = lax.broadcasted_iota(jnp.int32, sums_ref.shape, 0)
    sums_ref[...] = jnp.where(line == 0, trace, squares_of(c_now) + 2.0 * squares)


def up_body(layers, size, n_ref, d_ref, up_ref):
    for k, ref in enumerate((d_ref, n_ref)):
        blocks = sym_product(split(ref[...]), layers, size, TN)
        put_sym(up_ref, lambda a, b: blocks[a, b], layers, size, first=k * sym_rows(layers, size))


def local_g_body(layers, size, n_ref, down_ref, d_ref, g_ref, r_ref):
    n = layers * size
    n_now, e, d = split(n_ref[...]), split(down_ref[n : 2 * n, :]), split(d_ref[...])
    blocks = sym_product(e, layers, size, TN)
    g_ref[:n, :] = dot3(e, d, TN)
    put_sym(g_ref, lambda a, b: blocks[a, b], layers, size, first=n)
    r_ref[:n, :] = dot3(n_now, e, TN)
    r_ref[n:, :] = dot3(n_now, d, TN)


def local_y_body(layers, size, c_ref, n_ref, down_ref, d_ref, yc_ref, yn_ref, ys_ref, ye_ref, yd_ref):
    at = layers * size
    parts = (c_ref[...], n_ref[...], down_ref[:at, :], down_ref[at : 2 * at, :], d_ref[...])
    c, n, st, e, d = (split(part) for part in parts)
    yn_ref[...] = dot3(c, n, NN)
    ys_ref[...] = dot3(c, st, NT)
    ye_ref[...] = dot3(c, e, NN)
    yd_ref[...] = dot3(c, d, NN)
    terms = [
        sym_product(pair, layers, size, dims)
        for pair, dims in ((c, NT), (n, NT), (st, TN), (e, NT), (d, NT))
    ]
    put_sym(yc_ref, lambda a, b: sum(term[a, b] for term in terms), layers, size)


def g_body(layers, size, sums_ref, more_ref, g0_ref, below_ref, up_ref, total_ref, g_ref):
    n, tall = layers * size, sym_rows(layers, size)
    total_ref[...] = sums_ref[...] + more_ref[...]
    stu, eu = split(below_ref[:n, :]), split(below_ref[n : 2 * n, :])
    g_ref[:n, :] = g0_ref[:n, :] + dot3(stu, eu, NN)
    blocks = sym_product(stu, layers, size, NT)
    put_sym(g_ref, lambda a, b: blocks[a, b], layers, size, first=n)
    g_ref[n:, :] += g0_ref[n:, :] + up_ref[:tall, :]


def r_body(layers, size, r0_ref, below_ref, cx_ref, nx_ref, r_ref):
    n = layers * size
    su, eu, nx = split(below_ref[:n, :].T), split(below_ref[n : 2 * n, :]), split(nx_ref[...])
    cx = split(whole_sym(take_sym(cx_ref, layers, size), layers))
    r_ref[:n, :] = r0_ref[:n, :] + dot3(su, cx, NN) + dot3(eu, nx, NT)
    r_ref[n:, :] = r0_ref[n:, :] + dot3(su, nx, NN)


def middle_e_body(layers, size, after_ref, sums_ref, more_ref, n_ref, down_ref, d_ref, below_ref, cx_ref, nx_ref, ye0_ref, total_ref, ye_ref):
    at = layers * size
    total_ref[...] = sums_ref[...] + more_ref[...]
    n, e, d = split(n_ref[...]), split(down_ref[at : 2 * at, :]), split(d_ref[...])
    stu, nx = split(below_ref[:at, :]), split(nx_ref[...])
    cx = split(whole_sym(take_sym(cx_ref, layers, size), layers))
    ye_ref[...] = ye0_ref[...] + dot3(n, stu, NT) + dot3(e, cx, NN) + dot3(d, nx, NT)


def middle_n_body(
    layers, size, sums_ref, more_ref, n_ref, down_ref, d_ref, below_ref, nx_ref, yn0_ref, yd0_ref, total_ref, yn_ref, yd_ref
):
    at = layers * size
    total_ref[...] = sums_ref[...] + more_ref[...]
    n, e, d = split(n_ref[...]), split(down_ref[at : 2 * at, :]), split(d_ref[...])
    stu, eu, nx = split(below_ref[:at, :]), split(below_ref[at : 2 * at, :]), split(nx_ref[...])
    cu = split(whole_sym(take_sym(below_ref[2 * at :, :], layers, size), layers))
    yn_ref[...] = yn0_ref[...] + dot3(n, cu, NN) + dot3(e, stu, NN) + dot3(d, eu, NT)
    yd_ref[...] = yd0_ref[...] + dot3(n, eu, NN) + dot3(e, nx, NN)


def mix_body(
    layers, size, target, mask_ref, c_ref, n_ref, down_ref, d_ref, yc_ref, yn_ref, ys_ref, ye_ref, yd_ref,
    cxu_ref, up_ref, sums_ref, more_ref,
    out_ref, pc_ref, pn_ref, ps_ref, pe_ref, scale_ref, held, zero, sems,
):
    n, tall = layers * size, sym_rows(layers, size)
    sums = sums_ref[...] + more_ref[...]
    t1, t2 = sums[0:1, :], sums[1:2, :]
    twice = 2.0 * jax.nn.sigmoid((jnp.abs(t2 - target) - jnp.abs(2.0 * t1 - t2 - target)) / size)
    scale_ref[...] = jnp.broadcast_to(1.0 - twice, scale_ref.shape)
    slots = out_ref.shape[1]
    zero[...] = jnp.zeros(zero.shape, F32)
    written = {(layer, 0) for layer in range(layers)}
    for name in IN_PLANE:
        written |= {(low, slot) for low, _, slot in panel_blocks(name, layers)}
    copies = []
    for layer in range(layers):
        for slot in range(slots):
            if (layer, slot) not in written:
                copies.append(pltpu.make_async_copy(zero, out_ref.at[layer, slot], sems.at[len(copies)]))
                copies[-1].start()

    def mixed(y, a):
        return y + twice * (a - y)

    cxu = split(whole_sym(take_sym(cxu_ref, layers, size), layers))
    yd = yd_ref[...] + dot3(split(d_ref[...]), cxu, NN)
    for k, (low, high, slot) in enumerate(panel_blocks("D", layers)):
        rows, cols = slice(low * size, (low + 1) * size), slice(high * size, (high + 1) * size)
        held[k] = jnp.where(kept(mask_ref, low, slot), mixed(yd[rows, cols], d_ref[rows, cols]), 0.0)
        copies.append(pltpu.make_async_copy(held.at[k], out_ref.at[low, slot], sems.at[len(copies)]))
        copies[-1].start()
    c_blocks = take_sym(yc_ref[...] + up_ref[tall:, :], layers, size)
    put_sym(
        pc_ref,
        lambda a, b: mixed(c_blocks[a, b], c_ref[a * size : (a + 1) * size, b * size : (b + 1) * size]),
        layers,
        size,
    )
    for layer in range(layers):
        for name, y_ref, a_ref, p_ref in (
            ("N", yn_ref, n_ref, pn_ref),
            ("S", ys_ref, down_ref.at[:n, :], ps_ref),
            ("E", ye_ref, down_ref.at[n : 2 * n, :], pe_ref),
        ):
            rows = slice(layer * size, (layer + 1) * size)
            for other in range(layers):
                cols = slice(other * size, (other + 1) * size)
                a = a_ref[cols, rows].T if name == "S" else a_ref[rows, cols]
                p_ref[rows, cols] = mixed(y_ref[rows, cols], a)
    for copy in copies:
        copy.wait()


def mix_body_for(target, layers, size, *refs):
    mix_body(layers, size, target, *refs)


def side_body(names, layers, size, mask_ref, _, scale_ref, *rest):
    *p_refs, late_ref, out_ref, held, sems = rest
    n = layers * size
    scale = scale_ref[0:1, :]
    wide = jnp.concatenate([scale] * layers, axis=1)
    copies = []

    def send(value, low, slot):
        k = len(copies)
        held[k] = value
        copies.append(pltpu.make_async_copy(held.at[k], out_ref.at[low, slot], sems.at[k]))
        copies[-1].start()

    for at, name in enumerate(names):
        p_ref, top = p_refs[at], at * n
        if name == "C":
            blocks = take_sym(p_ref[...] + wide * late_ref[top:, :], layers, size)
            for layer in range(layers):
                send(blocks[layer, layer], layer, 0)
        for low, high, slot in panel_blocks(name, layers):
            rows, cols = slice(low * size, (low + 1) * size), slice(high * size, (high + 1) * size)
            value = blocks[low, high] if name == "C" else p_ref[rows, cols] + scale * late_ref[top + low * size : top + (low + 1) * size, cols]
            send(jnp.where(kept(mask_ref, low, slot), value, 0.0), low, slot)
    for copy in copies:
        copy.wait()


def call(body, layers, size, outs, spaces, products, scratch=(), limit=40, out_spaces=None, aliases=None):
    n = layers * size
    return pl.pallas_call(
        functools.partial(body, layers, size),
        out_shape=[jax.ShapeDtypeStruct(shape, F32) for shape in outs],
        in_specs=[pl.BlockSpec(memory_space=space) for space in spaces],
        out_specs=[pl.BlockSpec(memory_space=space) for space in out_spaces or [pltpu.VMEM] * len(outs)],
        scratch_shapes=list(scratch),
        input_output_aliases=aliases or {},
        compiler_params=pltpu.CompilerParams(vmem_limit_bytes=limit << 20),
        cost_estimate=pl.CostEstimate(
            flops=int(products * 6 * n**3), bytes_accessed=4 * n * n * (len(outs) + len(spaces)), transcendentals=0
        ),
    )


def passed_along(value, axis, by):
    peers = lax.axis_size(axis)
    return lax.ppermute(value, axis, [(i, (i + by) % peers) for i in range(peers)])


def swapped(value, axis, bit):
    peers = lax.axis_size(axis)
    return lax.ppermute(value, axis, [(i, i ^ bit) for i in range(peers)])


def rounds_of(axis):
    peers = lax.axis_size(axis)
    bits = [1 << k for k in range(peers.bit_length() - 1)]
    return [(axis, bit) for bit in bits[1:2] + bits[:1] + bits[2:]]


def shards(stored_blocks, onsite, bond_mask):
    stored, onsite, mask = stored_blocks[0, 0], onsite[0, 0], bond_mask[0, 0]
    layers, slots, size = stored.shape[:3]
    n, tall = layers * size, sym_rows(layers, size)
    panel, packed, sums = (n, n), (tall, n), (8, size)
    vmem, smem, hbm = pltpu.VMEM, pltpu.SMEM, pltpu.HBM

    def blocks(count):
        return [pltpu.VMEM((count, size, size), F32), pltpu.SemaphoreType.DMA((count,))]

    go = functools.partial(call, layers=layers, size=size)
    (N,) = go(
        pack_n_body, outs=[panel], spaces=[smem, hbm], products=0.1, scratch=blocks(len(wanted_n(layers))), limit=58
    )(mask, stored)
    N_x = passed_along(N, "row", -1)
    Cp, down, C, D, own = go(
        pack_body, outs=[packed, (2 * n + tall, n), panel, panel, sums], spaces=[smem, hbm, vmem, vmem], products=0.1,
        scratch=blocks(len(wanted_rest(layers))), limit=58,
    )(mask, stored, onsite, N)
    Cp_x = passed_along(Cp, "row", -1)
    below = passed_along(down, "col", -1)
    (up,) = go(up_body, outs=[(2 * tall, n)], spaces=[vmem] * 2, products=2, limit=16)(N, D)
    up = passed_along(up, "col", 1)

    if all(lax.axis_size(axis).bit_count() == 1 for axis in ("row", "col")):
        order = rounds_of("row") + rounds_of("col")
    else:
        order, own = [], lax.psum(own, ("row", "col"))
    hosts = 4
    plain = max(len(order) - hosts, 0)
    for axis, bit in order[:plain]:
        own = own + swapped(own, axis, bit)
    order = order[plain:]

    def arriving(value):
        return swapped(value, *order.pop(0)) if order else jnp.zeros_like(value)

    more = arriving(own)
    g0, r0 = go(local_g_body, outs=[(n + tall, n), (2 * n, n)], spaces=[vmem] * 3, products=4, limit=24)(N, down, D)
    yc, yn, ys, ye, yd = go(local_y_body, outs=[packed] + [panel] * 4, spaces=[vmem] * 4, products=8, limit=24)(C, N, down, D)
    own, g = go(g_body, outs=[sums, (n + tall, n)], spaces=[vmem] * 5, products=2, limit=16)(own, more, g0, below, up)
    g = passed_along(g, "row", 1)
    more = arriving(own)
    Cp_xu = passed_along(Cp_x, "col", -1)
    (r,) = go(r_body, outs=[(2 * n, n)], spaces=[vmem] * 4, products=3, limit=24)(r0, below, Cp_x, N_x)
    own, ye = go(middle_e_body, outs=[sums, panel], spaces=[hbm] + [vmem] * 9, products=3, limit=24)(
        r, own, more, N, down, D, below, Cp_x, N_x, ye
    )
    r = passed_along(r, "col", 1)
    more = arriving(own)
    own, yn, yd = go(middle_n_body, outs=[sums, panel, panel], spaces=[vmem] * 9, products=5, limit=24)(
        own, more, N, down, D, below, N_x, yn, yd
    )
    more = arriving(own)
    cells = lax.axis_size("row") * lax.axis_size("col") * layers
    stack = (layers, slots, size, size)
    count = len(panel_blocks("D", layers))
    out, pc, pn, ps, pe, scale = go(
        functools.partial(mix_body_for, float(cells * size // 2)),
        outs=[stack, packed, panel, panel, panel, sums], out_spaces=[hbm] + [vmem] * 5,
        spaces=[smem] + [vmem] * 13, products=1, limit=24,
        scratch=[pltpu.VMEM((count, size, size), F32), pltpu.VMEM((size, size), F32), pltpu.SemaphoreType.DMA((layers * slots,))],
    )(mask, C, N, down, D, yc, yn, ys, ye, yd, Cp_xu, up, own, more)
    for names, terms in ((("S", "E"), (ps, pe, r)), (("N", "C"), (pn, pc, g))):
        count = sum(len(panel_blocks(name, layers)) for name in names) + layers * ("C" in names)
        (out,) = go(
            functools.partial(side_body, names), outs=[stack], out_spaces=[hbm], spaces=[smem, hbm] + [vmem] * 4,
            products=0.1, scratch=blocks(count), limit=16, aliases={1: 0},
        )(mask, out, scale, *terms)
    return out[None, None]


def solution(mesh):
    in_specs = (
        P("row", "col", None, None, None, None),
        P("row", "col", None, None),
        P("row", "col", None, None),
    )
    out_specs = P("row", "col", None, None, None, None)
    return jax.shard_map(shards, mesh=mesh, in_specs=in_specs, out_specs=out_specs, check_vma=False)
```

```python
import functools

import jax
import jax.numpy as jnp
from jax import lax
from jax.experimental import pallas as pl
from jax.experimental.pallas import tpu as pltpu
from jax.sharding import PartitionSpec as P


F32 = jnp.float32
BF16 = jnp.bfloat16
NN = ((1,), (0,))
NT = ((1,), (1,))
TN = ((0,), (0,))
IN_PLANE = {"C": (0, 0), "N": (0, 1), "S": (1, -1), "E": (1, 0), "D": (1, 1)}


def offset_list():
    steps = (-1, 0, 1)
    return [(i, j, k) for i in steps for j in steps for k in steps if (i, j, k) > (0, 0, 0)]


def slot_number(offset):
    return offset_list().index(offset) + 1


def panel_blocks(name, layers):
    side = IN_PLANE[name]
    found = []
    for low in range(layers):
        for high in range(layers):
            step = high - low
            if abs(step) <= 1 and (*side, step) > (0, 0, 0):
                found.append((low, high, slot_number((*side, step))))
    return found


def sym_rows(layers, size):
    blocks = layers * (layers - 1) // 2 + (layers + 1) // 2
    return -(-blocks // layers) * size + 8


def rows_cols(size):
    return (
        lax.broadcasted_iota(jnp.int32, (size, size), 0),
        lax.broadcasted_iota(jnp.int32, (size, size), 1),
    )


def block_slices(k, layers, size):
    row, col = k // layers * size, k % layers * size
    return slice(row, row + size), slice(col, col + size)


def sym_places(layers):
    above = [(a, b) for a in range(layers) for b in range(a + 1, layers)]
    pairs = list(range(0, layers, 2))
    return list(enumerate(above)), [(len(above) + k, k, a) for k, a in enumerate(pairs)]


def put_sym(ref, get, layers, size, first=0):
    row, col = rows_cols(size)
    above, pairs = sym_places(layers)
    last = first + sym_rows(layers, size) - 8

    def put(k, value):
        rows, cols = block_slices(k, layers, size)
        ref[first + rows.start : first + rows.stop, cols] = value

    ref[last : last + 8, :] = jnp.zeros((8, layers * size), F32)
    if len(above) + len(pairs) < (last - first) // size * layers:
        ref[last - size : last, :] = jnp.zeros((size, layers * size), F32)
    for k, (a, b) in above:
        put(k, get(a, b))
    for k, mark, a in pairs:
        block = get(a, a)
        if a + 1 < layers:
            other = get(a + 1, a + 1)
            line = jnp.sum(jnp.where(row == col, other, 0.0), axis=0, keepdims=True)
            ref[last : last + 8, mark * size : (mark + 1) * size] = jnp.broadcast_to(line, (8, size))
            block = jnp.where(row <= col, block, other)
        put(k, block)


def take_sym(packed, layers, size):
    row, col = rows_cols(size)
    above, pairs = sym_places(layers)
    last = sym_rows(layers, size) - 8
    blocks = {}
    for k, (a, b) in above:
        rows, cols = block_slices(k, layers, size)
        blocks[a, b] = packed[rows, cols]
    for k, mark, a in pairs:
        rows, cols = block_slices(k, layers, size)
        block = packed[rows, cols]
        if a + 1 < layers:
            flipped = block.T
            line = packed[last : last + 1, mark * size : (mark + 1) * size]
            blocks[a, a] = jnp.where(row <= col, block, flipped)
            blocks[a + 1, a + 1] = jnp.where(row == col, line, jnp.where(row < col, flipped, block))
        else:
            blocks[a, a] = block
    return blocks


def whole_sym(blocks, layers):
    rows = []
    for a in range(layers):
        rows.append(
            jnp.concatenate(
                [blocks[a, b] if a <= b else blocks[b, a].T for b in range(layers)], axis=1
            )
        )
    return jnp.concatenate(rows, axis=0)


def split(value):
    high = value.astype(BF16)
    return high, (value - high.astype(F32)).astype(BF16)


def dot3(a, b, dims):
    go = functools.partial(lax.dot_general, dimension_numbers=(dims, ((), ())), preferred_element_type=F32)
    return go(a[0], b[0]) + (go(a[0], b[1]) + go(a[1], b[0]))


def cut(pair, at, size):
    return tuple(part[at : at + size, :] for part in pair)


def sym_product(pair, layers, size, dims):
    blocks = {}
    for a in range(layers):
        if dims == NT:
            left = tuple(part[a * size : (a + 1) * size, :] for part in pair)
            right = tuple(part[a * size :, :] for part in pair)
        else:
            left = tuple(part[:, a * size : (a + 1) * size] for part in pair)
            right = tuple(part[:, a * size :] for part in pair)
        strip = dot3(left, right, dims)
        for b in range(a, layers):
            blocks[a, b] = strip[:, (b - a) * size : (b - a + 1) * size]
    return blocks


def kept(mask_ref, layer, slot):
    return mask_ref[layer, slot - 1] > 0


def load_panel(out_ref, held, first, name, layers, size, mask_ref, flip=False, top=0):
    blocks = panel_blocks(name, layers)
    if layers > 2:
        out_ref[top : top + layers * size, :] = jnp.zeros((layers * size, layers * size), F32)
    for k, (low, high, slot) in enumerate(blocks):
        value = jnp.where(kept(mask_ref, low, slot), held[first + k], 0.0)
        if flip:
            low, high, value = high, low, value.T
        out_ref[top + low * size : top + (low + 1) * size, high * size : (high + 1) * size] = value
    return len(blocks)


def start_loads(stored_ref, held, sems, wanted):
    copies = [
        pltpu.make_async_copy(stored_ref.at[low, slot], held.at[k], sems.at[k])
        for k, (low, slot) in enumerate(wanted)
    ]
    for copy in copies:
        copy.start()
    return copies


def squares_of(value):
    return jnp.sum(value * value)


def wanted(layers):
    return [(layer, 0) for layer in range(layers)] + [
        (low, slot) for name in "CSEND" for low, _, slot in panel_blocks(name, layers)
    ]


def pack_body(
    layers, size, mask_ref, stored_ref, onsite_ref, t_ref, packed_ref, c_ref, down_ref, d_ref, sums_ref,
    held, sems, mask, mask_sem, onsite, onsite_sem,
):
    n = layers * size
    small = [
        pltpu.make_async_copy(mask_ref, mask, mask_sem),
        pltpu.make_async_copy(onsite_ref, onsite, onsite_sem),
    ]
    for copy in small:
        copy.start()
    copies = start_loads(stored_ref, held, sems, wanted(layers))
    for copy in small:
        copy.wait()
    row, col = rows_cols(size)
    c_ref[...] = jnp.zeros(c_ref.shape, F32)
    for layer in range(layers):
        copies[layer].wait()
        block = held[layer]
        block = 0.5 * (block + block.T) + jnp.where(row == col, onsite[layer : layer + 1, :], 0.0)
        c_ref[layer * size : (layer + 1) * size, layer * size : (layer + 1) * size] = block
    at = layers
    for low, high, slot in panel_blocks("C", layers):
        copies[at].wait()
        block = jnp.where(kept(mask, low, slot), held[at], 0.0)
        c_ref[low * size : (low + 1) * size, high * size : (high + 1) * size] = block
        c_ref[high * size : (high + 1) * size, low * size : (low + 1) * size] = block.T
        at += 1
    put_sym(
        packed_ref,
        lambda a, b: c_ref[a * size : (a + 1) * size, b * size : (b + 1) * size],
        layers,
        size,
    )
    t_ref[n:, :] = packed_ref[...]
    squares = 0.0
    for name, ref, top in (("S", down_ref, 0), ("E", down_ref, n), ("N", t_ref, 0), ("D", d_ref, 0)):
        count = len(panel_blocks(name, layers))
        for copy in copies[at : at + count]:
            copy.wait()
        load_panel(ref, held, at, name, layers, size, mask, flip=name == "S", top=top)
        squares = squares + squares_of(ref[top : top + n, :])
        at += count
    row, col = rows_cols(n)
    c_now = c_ref[...]
    trace = jnp.sum(jnp.where(row == col, c_now, 0.0))
    line = lax.broadcasted_iota(jnp.int32, sums_ref.shape, 0)
    sums = jnp.where((line == 0) | (line == 4), trace, squares_of(c_now) + 2.0 * squares)
    sums_ref[...] = sums
    last = t_ref.shape[0] - 8
    line = lax.broadcasted_iota(jnp.int32, (8, size), 0)
    for at in range(layers):
        cols = slice(at * size, (at + 1) * size)
        t_ref[last:, cols] = jnp.where(line < 4, t_ref[last:, cols], sums)


def squares_of(value):
    return jnp.sum(value * value)


def up_body(layers, size, n_ref, d_ref, up_ref):
    for k, ref in enumerate((d_ref, n_ref)):
        blocks = sym_product(split(ref[: layers * size, :]), layers, size, TN)
        put_sym(up_ref, lambda a, b: blocks[a, b], layers, size, first=k * sym_rows(layers, size))


def local_g_body(layers, size, _, t_ref, down_ref, d_ref, g_ref, r_ref):
    n = layers * size
    n_now, e, d = split(t_ref[:n, :]), split(down_ref[n:, :]), split(d_ref[...])
    blocks = sym_product(e, layers, size, TN)
    g_ref[:n, :] = dot3(e, d, TN)
    put_sym(g_ref, lambda a, b: blocks[a, b], layers, size, first=n)
    r_ref[:n, :] = dot3(n_now, e, TN)
    r_ref[n:, :] = dot3(n_now, d, TN)


def local_y_body(
    layers, size, _, c_ref, t_ref, down_ref, d_ref, out_ref, yc_ref, yn_ref, ys_ref, ye_ref, yd_ref, zero, sems
):
    at = layers * size
    zero[...] = jnp.zeros(zero.shape, F32)
    written = set(wanted(layers))
    copies = []
    for layer in range(layers):
        for slot in range(out_ref.shape[1]):
            if (layer, slot) not in written:
                copies.append(pltpu.make_async_copy(zero, out_ref.at[layer, slot], sems.at[len(copies)]))
                copies[-1].start()
    parts = (c_ref[...], t_ref[:at, :], down_ref[:at, :], down_ref[at:, :], d_ref[...])
    c, n, st, e, d = (split(part) for part in parts)
    yn_ref[...] = dot3(c, n, NN)
    ys_ref[...] = dot3(c, st, NT)
    ye_ref[...] = dot3(c, e, NN)
    yd_ref[...] = dot3(c, d, NN)
    terms = [
        sym_product(pair, layers, size, dims)
        for pair, dims in ((c, NT), (n, NT), (st, TN), (e, NT), (d, NT))
    ]
    put_sym(yc_ref, lambda a, b: sum(term[a, b] for term in terms), layers, size)
    for copy in copies:
        copy.wait()


def g_body(layers, size, _, sums_ref, g0_ref, below_ref, up_ref, packed_ref, tx_ref, *rest):
    *more_refs, total_ref, g_ref, both_ref = rest
    n, tall = layers * size, sym_rows(layers, size)
    last = n + tall - 8
    beside = tx_ref[last:, :size]
    line = lax.broadcasted_iota(jnp.int32, (8, size), 0)
    total = sums_ref[...] + jnp.where(line == 0, beside[4:5, :], beside[5:6, :])
    for ref in more_refs:
        total = total + ref[...]
    total_ref[...] = total
    both_ref[:tall, :] = packed_ref[...]
    both_ref[tall:, :] = tx_ref[n:, :]
    stu, eu = split(below_ref[:n, :]), split(below_ref[n:, :])
    g_ref[:n, :] = g0_ref[:n, :] + dot3(stu, eu, NN)
    blocks = sym_product(stu, layers, size, NT)
    put_sym(g_ref, lambda a, b: blocks[a, b], layers, size, first=n)
    g_ref[n:, :] += g0_ref[n:, :] + up_ref[:tall, :]


def r_body(layers, size, _, r0_ref, below_ref, tx_ref, rs_ref, re_ref):
    n = layers * size
    su, eu, nx = split(below_ref[:n, :].T), split(below_ref[n:, :]), split(tx_ref[:n, :])
    cx = split(whole_sym(take_sym(tx_ref[n:, :], layers, size), layers))
    rs_ref[...] = r0_ref[:n, :] + dot3(su, cx, NN) + dot3(eu, nx, NT)
    re_ref[...] = r0_ref[n:, :] + dot3(su, nx, NN)


def middle_e_body(
    layers, size, _, sums_ref, more_ref, t_ref, down_ref, d_ref, below_ref, tx_ref, ye0_ref, total_ref, ye_ref
):
    at = layers * size
    total_ref[...] = sums_ref[...] + more_ref[...]
    n, e, d = split(t_ref[:at, :]), split(down_ref[at:, :]), split(d_ref[...])
    stu, nx = split(below_ref[:at, :]), split(tx_ref[:at, :])
    cx = split(whole_sym(take_sym(tx_ref[at:, :], layers, size), layers))
    ye_ref[...] = ye0_ref[...] + dot3(n, stu, NT) + dot3(e, cx, NN) + dot3(d, nx, NT)


def middle_n_body(
    layers, size, _, sums_ref, more_ref, t_ref, down_ref, d_ref, below_ref, both_ref, tx_ref, yn0_ref, yd0_ref,
    total_ref, yn_ref, yd_ref,
):
    total_ref[...] = sums_ref[...] + more_ref[...]
    at, tall = layers * size, sym_rows(layers, size)
    n, e, d = split(t_ref[:at, :]), split(down_ref[at:, :]), split(d_ref[...])
    stu, eu, nx = split(below_ref[:at, :]), split(below_ref[at:, :]), split(tx_ref[:at, :])
    cu = split(whole_sym(take_sym(both_ref[:tall, :], layers, size), layers))
    cxu = split(whole_sym(take_sym(both_ref[tall:, :], layers, size), layers))
    yn_ref[...] = yn0_ref[...] + dot3(n, cu, NN) + dot3(e, stu, NN) + dot3(d, eu, NT)
    yd_ref[...] = yd0_ref[...] + dot3(n, eu, NN) + dot3(e, nx, NN) + dot3(d, cxu, NN)


def twice_h(target, size, sums_ref, more_ref):
    sums = sums_ref[...] + more_ref[...]
    t1, t2 = sums[0:1, :], sums[1:2, :]
    return 2.0 * jax.nn.sigmoid((jnp.abs(t2 - target) - jnp.abs(2.0 * t1 - t2 - target)) / size)


class Sender:
    def __init__(self, mask_ref, out_ref, held, sems):
        self.mask_ref, self.out_ref, self.held, self.sems = mask_ref, out_ref, held, sems
        self.copies = []

    def send(self, value, low, slot):
        k = len(self.copies)
        self.held[k] = jnp.where(kept(self.mask_ref, low, slot), value, 0.0) if slot else value
        self.copies.append(pltpu.make_async_copy(self.held.at[k], self.out_ref.at[low, slot], self.sems.at[k]))
        self.copies[-1].start()

    def wait(self):
        for copy in self.copies:
            copy.wait()


def last_e_body(
    target, layers, size, mask_ref, _, sums_ref, more_ref, ys_ref, ye_ref, yd_ref, down_ref, d_ref, rs_ref, re_ref,
    out_ref, held, sems,
):
    n = layers * size
    twice = twice_h(target, size, sums_ref, more_ref)
    sender = Sender(mask_ref, out_ref, held, sems)
    for name, a_ref, *terms in (
        ("D", d_ref, yd_ref),
        ("S", down_ref.at[:n, :], ys_ref, rs_ref),
        ("E", down_ref.at[n:, :], ye_ref, re_ref),
    ):
        for low, high, slot in panel_blocks(name, layers):
            rows, cols = slice(low * size, (low + 1) * size), slice(high * size, (high + 1) * size)
            y = sum(ref[rows, cols] for ref in terms)
            a = a_ref[cols, rows].T if name == "S" else a_ref[rows, cols]
            sender.send(y + twice * (a - y), low, slot)
    sender.wait()


def last_c_body(
    target, layers, size, mask_ref, _, sums_ref, more_ref, yc_ref, yn_ref, up_ref, c_ref, t_ref, g_ref, out_ref, held, sems
):
    n, tall = layers * size, sym_rows(layers, size)
    twice = twice_h(target, size, sums_ref, more_ref)
    sender = Sender(mask_ref, out_ref, held, sems)
    for low, high, slot in panel_blocks("N", layers):
        rows, cols = slice(low * size, (low + 1) * size), slice(high * size, (high + 1) * size)
        y = yn_ref[rows, cols] + g_ref[rows, cols]
        sender.send(y + twice * (t_ref[rows, cols] - y), low, slot)
    blocks = take_sym(yc_ref[...] + up_ref[tall:, :] + g_ref[n:, :], layers, size)
    for low, high, slot in panel_blocks("C", layers) + [(layer, layer, 0) for layer in range(layers)]:
        rows, cols = slice(low * size, (low + 1) * size), slice(high * size, (high + 1) * size)
        y = blocks[low, high]
        sender.send(y + twice * (c_ref[rows, cols] - y), low, slot)
    sender.wait()


def call(body, layers, size, outs, spaces, scratch=(), limit=24, out_spaces=None, aliases=None):
    return pl.pallas_call(
        functools.partial(body, layers, size),
        out_shape=[jax.ShapeDtypeStruct(shape, F32) for shape in outs],
        in_specs=[pl.BlockSpec(memory_space=space) for space in spaces],
        out_specs=[pl.BlockSpec(memory_space=space) for space in out_spaces or [pltpu.VMEM] * len(outs)],
        scratch_shapes=list(scratch),
        input_output_aliases=aliases or {},
        compiler_params=pltpu.CompilerParams(vmem_limit_bytes=limit << 20),
    )


def passed_along(value, axis, by):
    peers = lax.axis_size(axis)
    return lax.ppermute(value, axis, [(i, (i + by) % peers) for i in range(peers)])


def swapped(value, axis, bit):
    peers = lax.axis_size(axis)
    return lax.ppermute(value, axis, [(i, i ^ bit) for i in range(peers)])


def shards(stored_blocks, onsite, bond_mask):
    stored, onsite, mask = stored_blocks[0, 0], onsite[0, 0], bond_mask[0, 0]
    layers, slots, size = stored.shape[:3]
    n, tall = layers * size, sym_rows(layers, size)
    panel, packed, sums = (n, n), (tall, n), (8, size)
    vmem, smem, hbm = pltpu.VMEM, pltpu.SMEM, pltpu.HBM

    def blocks(count):
        return [pltpu.VMEM((count, size, size), F32), pltpu.SemaphoreType.DMA((count,))]

    go = functools.partial(call, layers=layers, size=size)
    stored, onsite, mask_hbm = (pltpu.with_memory_space_constraint(value, hbm) for value in (stored, onsite, mask))
    T, Cp, C, down, D, own = go(
        pack_body, outs=[(n + tall, n), packed, panel, (2 * n, n), panel, sums], spaces=[hbm] * 3,
        scratch=blocks(len(wanted(layers)))
        + [pltpu.SMEM(mask.shape, mask.dtype), pltpu.SemaphoreType.DMA, pltpu.VMEM(onsite.shape, F32), pltpu.SemaphoreType.DMA],
    )(mask_hbm, stored, onsite)
    T_x = passed_along(T, "row", -1)
    below = passed_along(down, "col", -1)
    (up,) = go(up_body, outs=[(2 * tall, n)], spaces=[vmem] * 2)(T, D)
    up_in = passed_along(up, "col", 1)
    more = [passed_along(own, "row", -by) for by in range(2, lax.axis_size("row"))]
    g0, r0 = go(local_g_body, outs=[(n + tall, n), (2 * n, n)], spaces=[hbm] + [vmem] * 3)(up, T, down, D)
    out, yc, yn, ys, ye, yd = go(
        local_y_body, outs=[(layers, slots, size, size), packed] + [panel] * 4, spaces=[hbm] + [vmem] * 4,
        out_spaces=[hbm] + [vmem] * 5, scratch=[pltpu.VMEM((size, size), F32), pltpu.SemaphoreType.DMA((layers * slots,))],
    )(g0, C, T, down, D)
    own, g, both = go(g_body, outs=[sums, (n + tall, n), (2 * tall, n)], spaces=[hbm] + [vmem] * (6 + len(more)))(
        yc, own, g0, below, up_in, Cp, T_x, *more
    )
    g_in = passed_along(g, "row", 1)
    both_u = passed_along(both, "col", -1)

    peers = lax.axis_size("col")
    bits = [1 << k for k in range(peers.bit_length() - 1)]
    bits = bits[:1] + bits[2:] + bits[1:2]
    if peers.bit_count() > 1:
        own = own + sum(passed_along(own, "col", by) for by in range(1, peers))
        bits = []
    while len(bits) > 3:
        own = own + swapped(own, "col", bits.pop(0))

    def arriving(value):
        return swapped(value, "col", bits.pop(0)) if bits else jnp.zeros_like(value)

    more = arriving(own)
    rs, re = go(r_body, outs=[panel, panel], spaces=[hbm] + [vmem] * 3)(g, r0, below, T_x)
    rs_in, re_in = passed_along(rs, "col", 1), passed_along(re, "col", 1)
    own, ye = go(middle_e_body, outs=[sums, panel], spaces=[hbm] + [vmem] * 8)(rs, own, more, T, down, D, below, T_x, ye)
    more = arriving(own)
    own, yn, yd = go(middle_n_body, outs=[sums, panel, panel], spaces=[hbm] + [vmem] * 10)(
        ye, own, more, T, down, D, below, both_u, T_x, yn, yd
    )
    more = arriving(own)
    cells = lax.axis_size("row") * lax.axis_size("col") * layers
    target = float(cells * size // 2)

    def finish(body, out, names, *terms):
        count = sum(len(panel_blocks(name, layers)) for name in names) + layers * ("C" in names)
        return go(
            functools.partial(body, target), outs=[out.shape], out_spaces=[hbm], spaces=[smem, hbm] + [vmem] * (2 + len(terms)),
            scratch=blocks(count), aliases={1: 0},
        )(mask, out, own, more, *terms)[0]

    out = finish(last_e_body, out, "SED", ys, ye, yd, down, D, rs_in, re_in)
    out = finish(last_c_body, out, "NC", yc, yn, up_in, C, T, g_in)
    return out[None, None]


def solution(mesh):
    in_specs = (
        P("row", "col", None, None, None, None),
        P("row", "col", None, None),
        P("row", "col", None, None),
    )
    out_specs = P("row", "col", None, None, None, None)
    return jax.shard_map(shards, mesh=mesh, in_specs=in_specs, out_specs=out_specs, check_vma=False)
```

```python
import functools

import jax
import jax.numpy as jnp
from jax import lax
from jax.experimental import pallas as pl
from jax.experimental.pallas import tpu as pltpu
from jax.sharding import PartitionSpec as P


F32 = jnp.float32
BF16 = jnp.bfloat16
NN = ((1,), (0,))
NT = ((1,), (1,))
TN = ((0,), (0,))
IN_PLANE = {"C": (0, 0), "N": (0, 1), "S": (1, -1), "E": (1, 0), "D": (1, 1)}


def offset_list():
    steps = (-1, 0, 1)
    return [(i, j, k) for i in steps for j in steps for k in steps if (i, j, k) > (0, 0, 0)]


def slot_number(offset):
    return offset_list().index(offset) + 1


def panel_blocks(name, layers):
    side = IN_PLANE[name]
    found = []
    for low in range(layers):
        for high in range(layers):
            step = high - low
            if abs(step) <= 1 and (*side, step) > (0, 0, 0):
                found.append((low, high, slot_number((*side, step))))
    return found


def sym_rows(layers, size):
    blocks = layers * (layers - 1) // 2 + (layers + 1) // 2
    return -(-blocks // layers) * size + 8


def rows_cols(size):
    return (
        lax.broadcasted_iota(jnp.int32, (size, size), 0),
        lax.broadcasted_iota(jnp.int32, (size, size), 1),
    )


def block_slices(k, layers, size):
    row, col = k // layers * size, k % layers * size
    return slice(row, row + size), slice(col, col + size)


def sym_places(layers):
    above = [(a, b) for a in range(layers) for b in range(a + 1, layers)]
    pairs = list(range(0, layers, 2))
    return list(enumerate(above)), [(len(above) + k, k, a) for k, a in enumerate(pairs)]


def put_sym(ref, get, layers, size, first=0):
    row, col = rows_cols(size)
    above, pairs = sym_places(layers)
    last = first + sym_rows(layers, size) - 8

    def put(k, value):
        rows, cols = block_slices(k, layers, size)
        ref[first + rows.start : first + rows.stop, cols] = value

    ref[last : last + 8, :] = jnp.zeros((8, layers * size), F32)
    if len(above) + len(pairs) < (last - first) // size * layers:
        ref[last - size : last, :] = jnp.zeros((size, layers * size), F32)
    for k, (a, b) in above:
        put(k, get(a, b))
    for k, mark, a in pairs:
        block = get(a, a)
        if a + 1 < layers:
            other = get(a + 1, a + 1)
            line = jnp.sum(jnp.where(row == col, other, 0.0), axis=0, keepdims=True)
            ref[last : last + 8, mark * size : (mark + 1) * size] = jnp.broadcast_to(line, (8, size))
            block = jnp.where(row <= col, block, other)
        put(k, block)


def take_sym(packed, layers, size):
    row, col = rows_cols(size)
    above, pairs = sym_places(layers)
    last = sym_rows(layers, size) - 8
    blocks = {}
    for k, (a, b) in above:
        rows, cols = block_slices(k, layers, size)
        blocks[a, b] = packed[rows, cols]
    for k, mark, a in pairs:
        rows, cols = block_slices(k, layers, size)
        block = packed[rows, cols]
        if a + 1 < layers:
            flipped = block.T
            line = packed[last : last + 1, mark * size : (mark + 1) * size]
            blocks[a, a] = jnp.where(row <= col, block, flipped)
            blocks[a + 1, a + 1] = jnp.where(row == col, line, jnp.where(row < col, flipped, block))
        else:
            blocks[a, a] = block
    return blocks


def whole_sym(blocks, layers):
    rows = []
    for a in range(layers):
        rows.append(
            jnp.concatenate(
                [blocks[a, b] if a <= b else blocks[b, a].T for b in range(layers)], axis=1
            )
        )
    return jnp.concatenate(rows, axis=0)


def split(value):
    high = value.astype(BF16)
    return high, (value - high.astype(F32)).astype(BF16)


def dot3(a, b, dims):
    go = functools.partial(lax.dot_general, dimension_numbers=(dims, ((), ())), preferred_element_type=F32)
    return go(a[0], b[0]) + (go(a[0], b[1]) + go(a[1], b[0]))


def cut(pair, at, size):
    return tuple(part[at : at + size, :] for part in pair)


def sym_product(pair, layers, size, dims):
    blocks = {}
    for a in range(layers):
        if dims == NT:
            left = tuple(part[a * size : (a + 1) * size, :] for part in pair)
            right = tuple(part[a * size :, :] for part in pair)
        else:
            left = tuple(part[:, a * size : (a + 1) * size] for part in pair)
            right = tuple(part[:, a * size :] for part in pair)
        strip = dot3(left, right, dims)
        for b in range(a, layers):
            blocks[a, b] = strip[:, (b - a) * size : (b - a + 1) * size]
    return blocks


def kept(mask_ref, layer, slot):
    return mask_ref[layer, slot - 1] > 0


def load_panel(out_ref, held, first, name, layers, size, mask_ref, flip=False, top=0):
    if layers > 2:
        out_ref[top : top + layers * size, :] = jnp.zeros((layers * size, layers * size), F32)
    for k, (low, high, slot) in enumerate(panel_blocks(name, layers)):
        value = jnp.where(kept(mask_ref, low, slot), held[first + k], 0.0)
        if flip:
            low, high, value = high, low, value.T
        out_ref[top + low * size : top + (low + 1) * size, high * size : (high + 1) * size] = value


def start_loads(stored_ref, held, sems, wanted):
    copies = [
        pltpu.make_async_copy(stored_ref.at[low, slot], held.at[k], sems.at[k])
        for k, (low, slot) in enumerate(wanted)
    ]
    for copy in copies:
        copy.start()
    return copies


def squares_of(value):
    return jnp.sum(value * value)


def wanted(names, layers):
    return [(layer, 0) for layer in range(layers) if "C" in names] + [
        (low, slot) for name in names for low, _, slot in panel_blocks(name, layers)
    ]


def pack_body(
    layers, size, mask_ref, stored_ref, onsite_ref, t_ref, packed_ref, c_ref, down_ref, d_ref, sums_ref,
    held, sems, mask, mask_sem, onsite, onsite_sem,
):
    n = layers * size
    small = [
        pltpu.make_async_copy(mask_ref, mask, mask_sem),
        pltpu.make_async_copy(onsite_ref, onsite, onsite_sem),
    ]
    for copy in small:
        copy.start()
    copies = start_loads(stored_ref, held, sems, wanted("CSEND", layers))
    for copy in small:
        copy.wait()
    row, col = rows_cols(size)
    c_ref[...] = jnp.zeros(c_ref.shape, F32)
    for layer in range(layers):
        copies[layer].wait()
        block = held[layer]
        block = 0.5 * (block + block.T) + jnp.where(row == col, onsite[layer : layer + 1, :], 0.0)
        c_ref[layer * size : (layer + 1) * size, layer * size : (layer + 1) * size] = block
    at = layers
    for low, high, slot in panel_blocks("C", layers):
        copies[at].wait()
        block = jnp.where(kept(mask, low, slot), held[at], 0.0)
        c_ref[low * size : (low + 1) * size, high * size : (high + 1) * size] = block
        c_ref[high * size : (high + 1) * size, low * size : (low + 1) * size] = block.T
        at += 1
    put_sym(
        packed_ref,
        lambda a, b: c_ref[a * size : (a + 1) * size, b * size : (b + 1) * size],
        layers,
        size,
    )
    t_ref[n:, :] = packed_ref[...]
    squares = 0.0
    for name, ref, top in (("S", down_ref, 0), ("E", down_ref, n), ("N", t_ref, 0), ("D", d_ref, 0)):
        count = len(panel_blocks(name, layers))
        for copy in copies[at : at + count]:
            copy.wait()
        load_panel(ref, held, at, name, layers, size, mask, flip=name == "S", top=top)
        squares = squares + squares_of(ref[top : top + n, :])
        at += count
    row, col = rows_cols(n)
    c_now = c_ref[...]
    trace = jnp.sum(jnp.where(row == col, c_now, 0.0))
    line = lax.broadcasted_iota(jnp.int32, sums_ref.shape, 0)
    sums_ref[...] = jnp.where(line % 4 == 0, trace, squares_of(c_now) + 2.0 * squares)


def squares_of(value):
    return jnp.sum(value * value)


def wanted(names, layers):
    return [(layer, 0) for layer in range(layers) if "C" in names] + [
        (low, slot) for name in names for low, _, slot in panel_blocks(name, layers)
    ]


def pack_t_body(
    layers, size, mask_ref, stored_ref, onsite_ref, t_ref, packed_ref, c_ref, sums_ref,
    held, sems, mask, mask_sem, onsite, onsite_sem,
):
    n = layers * size
    small = [
        pltpu.make_async_copy(mask_ref, mask, mask_sem),
        pltpu.make_async_copy(onsite_ref, onsite, onsite_sem),
    ]
    for copy in small:
        copy.start()
    copies = start_loads(stored_ref, held, sems, wanted("CN", layers))
    for copy in small:
        copy.wait()
    row, col = rows_cols(size)
    c_ref[...] = jnp.zeros(c_ref.shape, F32)
    for layer in range(layers):
        copies[layer].wait()
        block = held[layer]
        block = 0.5 * (block + block.T) + jnp.where(row == col, onsite[layer : layer + 1, :], 0.0)
        c_ref[layer * size : (layer + 1) * size, layer * size : (layer + 1) * size] = block
    at = layers
    for low, high, slot in panel_blocks("C", layers):
        copies[at].wait()
        block = jnp.where(kept(mask, low, slot), held[at], 0.0)
        c_ref[low * size : (low + 1) * size, high * size : (high + 1) * size] = block
        c_ref[high * size : (high + 1) * size, low * size : (low + 1) * size] = block.T
        at += 1
    put_sym(
        packed_ref,
        lambda a, b: c_ref[a * size : (a + 1) * size, b * size : (b + 1) * size],
        layers,
        size,
    )
    t_ref[n:, :] = packed_ref[...]
    for copy in copies[at:]:
        copy.wait()
    load_panel(t_ref, held, at, "N", layers, size, mask)
    row, col = rows_cols(n)
    c_now = c_ref[...]
    trace = jnp.sum(jnp.where(row == col, c_now, 0.0))
    line = lax.broadcasted_iota(jnp.int32, sums_ref.shape, 0)
    sums_ref[...] = jnp.where(line % 4 == 0, trace, squares_of(c_now) + 2.0 * squares_of(t_ref[:n, :]))


def pack_e_body(layers, size, mask_ref, stored_ref, before_ref, st_ref, e_ref, d_ref, sums_ref, held, sems, mask, mask_sem):
    small = pltpu.make_async_copy(mask_ref, mask, mask_sem)
    small.start()
    copies = start_loads(stored_ref, held, sems, wanted("SED", layers))
    small.wait()
    at = 0
    squares = 0.0
    for name, ref in (("S", st_ref), ("E", e_ref), ("D", d_ref)):
        count = len(panel_blocks(name, layers))
        for copy in copies[at : at + count]:
            copy.wait()
        load_panel(ref, held, at, name, layers, size, mask, flip=name == "S")
        squares = squares + squares_of(ref[...])
        at += count
    line = lax.broadcasted_iota(jnp.int32, sums_ref.shape, 0)
    sums_ref[...] = before_ref[...] + jnp.where(line % 4 == 0, 0.0, 2.0 * squares)


def squares_of(value):
    return jnp.sum(value * value)


def up_body(layers, size, panel_ref, up_ref):
    blocks = sym_product(split(panel_ref[: layers * size, :]), layers, size, TN)
    put_sym(up_ref, lambda a, b: blocks[a, b], layers, size)


def local_g_body(layers, size, _, sums_ref, more_ref, t_ref, down_ref, d_ref, total_ref, g_ref, r_ref, yc_up_ref):
    n = layers * size
    total_ref[...] = sums_ref[...] + more_ref[...]
    n_now, e, d = split(t_ref[:n, :]), split(down_ref[n:, :]), split(d_ref[...])
    blocks = sym_product(e, layers, size, TN)
    g_ref[:n, :] = dot3(e, d, TN)
    put_sym(g_ref, lambda a, b: blocks[a, b], layers, size, first=n)
    r_ref[:n, :] = dot3(n_now, e, TN)
    r_ref[n:, :] = dot3(n_now, d, TN)
    blocks = sym_product(n_now, layers, size, TN)
    put_sym(yc_up_ref, lambda a, b: blocks[a, b], layers, size)


def local_y_body(
    layers, size, _, sums_ref, more_ref, c_ref, t_ref, down_ref, d_ref,
    total_ref, out_ref, yc_ref, yn_ref, ys_ref, ye_ref, yd_ref, zero, sems,
):
    total_ref[...] = sums_ref[...] + more_ref[...]
    zero[...] = jnp.zeros(zero.shape, F32)
    written = set(wanted(IN_PLANE, layers))
    copies = []
    for layer in range(layers):
        for slot in range(out_ref.shape[1]):
            if (layer, slot) not in written:
                copies.append(pltpu.make_async_copy(zero, out_ref.at[layer, slot], sems.at[len(copies)]))
                copies[-1].start()
    at = layers * size
    parts = (c_ref[...], t_ref[:at, :], down_ref[:at, :], down_ref[at:, :], d_ref[...])
    c, n, st, e, d = (split(part) for part in parts)
    yn_ref[...] = dot3(c, n, NN)
    ys_ref[...] = dot3(c, st, NT)
    ye_ref[...] = dot3(c, e, NN)
    yd_ref[...] = dot3(c, d, NN)
    terms = [
        sym_product(pair, layers, size, dims)
        for pair, dims in ((c, NT), (n, NT), (st, TN), (e, NT), (d, NT))
    ]
    put_sym(yc_ref, lambda a, b: sum(term[a, b] for term in terms), layers, size)
    for copy in copies:
        copy.wait()


def copy_body(layers, size, _, __, from_ref, to_ref):
    to_ref[...] = from_ref[...]


def g_body(layers, size, _, sums_ref, more_ref, g0_ref, below_ref, up_ref, total_ref, g_ref):
    n, last = layers * size, g_ref.shape[0] - 8
    total = sums_ref[...] + more_ref[...]
    total_ref[...] = total
    stu, eu = split(below_ref[:n, :]), split(below_ref[n:, :])
    g_ref[:n, :] = g0_ref[:n, :] + dot3(stu, eu, NN)
    blocks = sym_product(stu, layers, size, NT)
    put_sym(g_ref, lambda a, b: blocks[a, b], layers, size, first=n)
    g_ref[n:, :] += g0_ref[n:, :] + up_ref[...]
    line = lax.broadcasted_iota(jnp.int32, total.shape, 0)
    for at in range(layers):
        cols = slice(at * size, (at + 1) * size)
        g_ref[last:, cols] = jnp.where(line < 4, g_ref[last:, cols], total)


def both_body(layers, size, _, packed_ref, tx_ref, both_ref):
    n, tall = layers * size, sym_rows(layers, size)
    both_ref[:tall, :] = packed_ref[...]
    both_ref[tall:, :] = tx_ref[n:, :]


def early_body(layers, size, _, t_ref, e_ref, d_ref, below_ref, yn0_ref, ye0_ref, yd0_ref, yn_ref, ye_ref, yd_ref, su_ref):
    at = layers * size
    su_ref[...] = below_ref[:at, :].T
    n, e, d = split(t_ref[:at, :]), split(e_ref[at:, :]), split(d_ref[...])
    stu, eu = split(below_ref[:at, :]), split(below_ref[at:, :])
    yn_ref[...] = yn0_ref[...] + dot3(e, stu, NN) + dot3(d, eu, NT)
    ye_ref[...] = ye0_ref[...] + dot3(n, stu, NT)
    yd_ref[...] = yd0_ref[...] + dot3(n, eu, NN)


def r_body(layers, size, _, __, r0_ref, su_ref, below_ref, tx_ref, rs_ref, re_ref):
    n = layers * size
    su, eu, nx = split(su_ref[...]), split(below_ref[n:, :]), split(tx_ref[:n, :])
    cx = split(whole_sym(take_sym(tx_ref[n:, :], layers, size), layers))
    rs_ref[...] = r0_ref[:n, :] + dot3(su, cx, NN) + dot3(eu, nx, NT)
    re_ref[...] = r0_ref[n:, :] + dot3(su, nx, NN)


def middle_body(layers, size, _, e_ref, d_ref, tx_ref, ye0_ref, yd0_ref, ye_ref, yd_ref):
    at = layers * size
    e, d, nx = split(e_ref[at:, :]), split(d_ref[...]), split(tx_ref[:at, :])
    cx = split(whole_sym(take_sym(tx_ref[at:, :], layers, size), layers))
    ye_ref[...] = ye0_ref[...] + dot3(e, cx, NN) + dot3(d, nx, NT)
    yd_ref[...] = yd0_ref[...] + dot3(e, nx, NN)


def middle_c_body(layers, size, sums_ref, t_ref, d_ref, both_ref, yn0_ref, yd0_ref, total_ref, yn_ref, yd_ref):
    at, tall = layers * size, sym_rows(layers, size)
    total_ref[...] = sums_ref[...]
    n, d = split(t_ref[:at, :]), split(d_ref[...])
    cu = split(whole_sym(take_sym(both_ref[:tall, :], layers, size), layers))
    cxu = split(whole_sym(take_sym(both_ref[tall:, :], layers, size), layers))
    yn_ref[...] = yn0_ref[...] + dot3(n, cu, NN)
    yd_ref[...] = yd0_ref[...] + dot3(d, cxu, NN)


def twice_h(target, size, sums):
    t1, t2 = sums[0:1, :], sums[1:2, :]
    return 2.0 * jax.nn.sigmoid((jnp.abs(t2 - target) - jnp.abs(2.0 * t1 - t2 - target)) / size)


class Sender:
    def __init__(self, mask_ref, out_ref, held, sems):
        self.mask_ref, self.out_ref, self.held, self.sems = mask_ref, out_ref, held, sems
        self.copies = []

    def send(self, value, low, slot):
        k = len(self.copies)
        self.held[k] = jnp.where(kept(self.mask_ref, low, slot), value, 0.0) if slot else value
        self.copies.append(pltpu.make_async_copy(self.held.at[k], self.out_ref.at[low, slot], self.sems.at[k]))
        self.copies[-1].start()

    def wait(self):
        for copy in self.copies:
            copy.wait()


def last_body(
    target, layers, size, mask_ref, _, c_ref, t_ref, down_ref, d_ref,
    yc_ref, yn_ref, ys_ref, ye_ref, yd_ref, yc_in_ref, rs_ref, re_ref, g_ref, *rest,
):
    *sums_refs, out_ref, held, sems = rest
    n, last = layers * size, g_ref.shape[0] - 8
    line = lax.broadcasted_iota(jnp.int32, (8, size), 0)
    beside = g_ref[last:, :size]
    sums = jnp.where(line == 0, beside[4:5, :], beside[5:6, :])
    twice = twice_h(target, size, sum((ref[...] for ref in sums_refs), start=sums))
    sender = Sender(mask_ref, out_ref, held, sems)
    for name, a_ref, *terms in (
        ("D", d_ref, yd_ref),
        ("E", down_ref.at[n:, :], ye_ref, re_ref),
        ("S", down_ref.at[:n, :], ys_ref, rs_ref),
        ("N", t_ref.at[:n, :], yn_ref, g_ref),
    ):
        for low, high, slot in panel_blocks(name, layers):
            rows, cols = slice(low * size, (low + 1) * size), slice(high * size, (high + 1) * size)
            y = sum(ref[rows, cols] for ref in terms)
            a = a_ref[cols, rows].T if name == "S" else a_ref[rows, cols]
            sender.send(y + twice * (a - y), low, slot)
    blocks = take_sym(yc_ref[...] + yc_in_ref[...] + g_ref[n:, :], layers, size)
    for low, high, slot in panel_blocks("C", layers) + [(layer, layer, 0) for layer in range(layers)]:
        rows, cols = slice(low * size, (low + 1) * size), slice(high * size, (high + 1) * size)
        y = blocks[low, high]
        sender.send(y + twice * (c_ref[rows, cols] - y), low, slot)
    sender.wait()


def call(body, layers, size, outs, spaces, scratch=(), limit=24, out_spaces=None, aliases=None):
    return pl.pallas_call(
        functools.partial(body, layers, size),
        out_shape=[jax.ShapeDtypeStruct(shape, F32) for shape in outs],
        in_specs=[pl.BlockSpec(memory_space=space) for space in spaces],
        out_specs=[pl.BlockSpec(memory_space=space) for space in out_spaces or [pltpu.VMEM] * len(outs)],
        scratch_shapes=list(scratch),
        input_output_aliases=aliases or {},
        compiler_params=pltpu.CompilerParams(vmem_limit_bytes=limit << 20),
    )


def passed_along(value, axis, by):
    peers = lax.axis_size(axis)
    return lax.ppermute(value, axis, [(i, (i + by) % peers) for i in range(peers)])


def swapped(value, axis, bit):
    peers = lax.axis_size(axis)
    return lax.ppermute(value, axis, [(i, i ^ bit) for i in range(peers)])


def shards(stored_blocks, onsite, bond_mask):
    stored, onsite, mask = stored_blocks[0, 0], onsite[0, 0], bond_mask[0, 0]
    layers, slots, size = stored.shape[:3]
    n, tall = layers * size, sym_rows(layers, size)
    panel, packed, sums = (n, n), (tall, n), (8, size)
    vmem, smem, hbm = pltpu.VMEM, pltpu.SMEM, pltpu.HBM

    def blocks(count):
        return [pltpu.VMEM((count, size, size), F32), pltpu.SemaphoreType.DMA((count,))]

    go = functools.partial(call, layers=layers, size=size)
    stored, onsite, mask_hbm = (pltpu.with_memory_space_constraint(value, hbm) for value in (stored, onsite, mask))

    peers = lax.axis_size("col")
    bits = [1 << k for k in range(peers.bit_length() - 1)]
    bits = bits[:1] + bits[2:] + bits[1:2]

    def arriving(value):
        return swapped(value, "col", bits.pop(0)) if bits else jnp.zeros_like(value)

    T, Cp, C, down, D, own = go(
        pack_body, outs=[(n + tall, n), packed, panel, (2 * n, n), panel, sums], spaces=[hbm] * 3,
        scratch=blocks(len(wanted(IN_PLANE, layers)))
        + [pltpu.SMEM(mask.shape, mask.dtype), pltpu.SemaphoreType.DMA, pltpu.VMEM(onsite.shape, F32), pltpu.SemaphoreType.DMA],
    )(mask_hbm, stored, onsite)
    T_x = passed_along(T, "row", -1)
    below = passed_along(down, "col", -1)
    (gc,) = go(up_body, outs=[packed], spaces=[vmem])(D)
    gc_in = passed_along(gc, "col", 1)
    if peers.bit_count() > 1:
        own = own + sum(passed_along(own, "col", by) for by in range(1, peers))
        bits = []
    while len(bits) > 3:
        own = own + arriving(own)
    more = arriving(own)
    own, g0, r0, yc_up = go(local_g_body, outs=[sums, (n + tall, n), (2 * n, n), packed], spaces=[hbm] + [vmem] * 5)(
        gc, own, more, T, down, D
    )
    more = arriving(own)
    own, out, yc, yn, ys, ye, yd = go(
        local_y_body, outs=[sums, (layers, slots, size, size), packed] + [panel] * 4, spaces=[hbm] + [vmem] * 6,
        out_spaces=[vmem, hbm] + [vmem] * 5, scratch=[pltpu.VMEM((size, size), F32), pltpu.SemaphoreType.DMA((layers * slots,))],
    )(g0, own, more, C, T, down, D)
    more = arriving(own)
    (yc_up,) = go(copy_body, outs=[packed], spaces=[hbm] * 2 + [vmem])(yc, below, yc_up)
    yc_in = passed_along(yc_up, "col", 1)
    own, g = go(g_body, outs=[sums, (n + tall, n)], spaces=[hbm] + [vmem] * 5)(yc_up, own, more, g0, below, gc_in)
    g_in = passed_along(g, "row", 1)
    yn, ye, yd, S_u = go(early_body, outs=[panel] * 4, spaces=[hbm] + [vmem] * 7)(g, T, down, D, below, yn, ye, yd)
    (both,) = go(both_body, outs=[(2 * tall, n)], spaces=[hbm] + [vmem] * 2)(yn, Cp, T_x)
    both_u = passed_along(both, "col", -1)
    rs, re = go(r_body, outs=[panel, panel], spaces=[hbm] * 2 + [vmem] * 4)(both, yc_in, r0, S_u, below, T_x)
    rs_in, re_in = passed_along(rs, "col", 1), passed_along(re, "col", 1)
    ye, yd = go(middle_body, outs=[panel] * 2, spaces=[hbm] + [vmem] * 5)(rs, down, D, T_x, ye, yd)
    own, yn, yd = go(middle_c_body, outs=[sums, panel, panel], spaces=[vmem] * 6)(own, T, D, both_u, yn, yd)
    every = [own] + [passed_along(own, "row", -by) for by in range(1, lax.axis_size("row") - 1)]
    cells = lax.axis_size("row") * lax.axis_size("col") * layers
    target = float(cells * size // 2)
    (out,) = go(
        functools.partial(last_body, target), outs=[out.shape], out_spaces=[hbm],
        spaces=[smem, hbm] + [vmem] * (13 + len(every)), scratch=blocks(len(wanted(IN_PLANE, layers))), aliases={1: 0},
    )(mask, out, C, T, down, D, yc, yn, ys, ye, yd, yc_in, rs_in, re_in, g_in, *every)
    return out[None, None]


def solution(mesh):
    in_specs = (
        P("row", "col", None, None, None, None),
        P("row", "col", None, None),
        P("row", "col", None, None),
    )
    out_specs = P("row", "col", None, None, None, None)
    return jax.shard_map(shards, mesh=mesh, in_specs=in_specs, out_specs=out_specs, check_vma=False)
```

```python
import functools

import jax
import jax.numpy as jnp
from jax import lax
from jax.experimental import pallas as pl
from jax.experimental.pallas import tpu as pltpu
from jax.sharding import PartitionSpec as P


F32 = jnp.float32
BF16 = jnp.bfloat16
NN = ((1,), (0,))
NT = ((1,), (1,))
TN = ((0,), (0,))
IN_PLANE = {"C": (0, 0), "N": (0, 1), "S": (1, -1), "E": (1, 0), "D": (1, 1)}


def offset_list():
    steps = (-1, 0, 1)
    return [(i, j, k) for i in steps for j in steps for k in steps if (i, j, k) > (0, 0, 0)]


def slot_number(offset):
    return offset_list().index(offset) + 1


def panel_blocks(name, layers):
    side = IN_PLANE[name]
    found = []
    for low in range(layers):
        for high in range(layers):
            step = high - low
            if abs(step) <= 1 and (*side, step) > (0, 0, 0):
                found.append((low, high, slot_number((*side, step))))
    return found


def sym_rows(layers, size):
    blocks = layers * (layers - 1) // 2 + (layers + 1) // 2
    return -(-blocks // layers) * size + 8


def rows_cols(size):
    return (
        lax.broadcasted_iota(jnp.int32, (size, size), 0),
        lax.broadcasted_iota(jnp.int32, (size, size), 1),
    )


def block_slices(k, layers, size):
    row, col = k // layers * size, k % layers * size
    return slice(row, row + size), slice(col, col + size)


def sym_places(layers):
    above = [(a, b) for a in range(layers) for b in range(a + 1, layers)]
    pairs = list(range(0, layers, 2))
    return list(enumerate(above)), [(len(above) + k, k, a) for k, a in enumerate(pairs)]


def put_sym(ref, get, layers, size, first=0):
    row, col = rows_cols(size)
    above, pairs = sym_places(layers)
    last = first + sym_rows(layers, size) - 8

    def put(k, value):
        rows, cols = block_slices(k, layers, size)
        ref[first + rows.start : first + rows.stop, cols] = value

    ref[last : last + 8, :] = jnp.zeros((8, layers * size), F32)
    if len(above) + len(pairs) < (last - first) // size * layers:
        ref[last - size : last, :] = jnp.zeros((size, layers * size), F32)
    for k, (a, b) in above:
        put(k, get(a, b))
    for k, mark, a in pairs:
        block = get(a, a)
        if a + 1 < layers:
            other = get(a + 1, a + 1)
            line = jnp.sum(jnp.where(row == col, other, 0.0), axis=0, keepdims=True)
            ref[last : last + 8, mark * size : (mark + 1) * size] = jnp.broadcast_to(line, (8, size))
            block = jnp.where(row <= col, block, other)
        put(k, block)


def take_sym(packed, layers, size):
    row, col = rows_cols(size)
    above, pairs = sym_places(layers)
    last = sym_rows(layers, size) - 8
    blocks = {}
    for k, (a, b) in above:
        rows, cols = block_slices(k, layers, size)
        blocks[a, b] = packed[rows, cols]
    for k, mark, a in pairs:
        rows, cols = block_slices(k, layers, size)
        block = packed[rows, cols]
        if a + 1 < layers:
            flipped = block.T
            line = packed[last : last + 1, mark * size : (mark + 1) * size]
            blocks[a, a] = jnp.where(row <= col, block, flipped)
            blocks[a + 1, a + 1] = jnp.where(row == col, line, jnp.where(row < col, flipped, block))
        else:
            blocks[a, a] = block
    return blocks


def whole_sym(blocks, layers):
    rows = []
    for a in range(layers):
        rows.append(
            jnp.concatenate(
                [blocks[a, b] if a <= b else blocks[b, a].T for b in range(layers)], axis=1
            )
        )
    return jnp.concatenate(rows, axis=0)


def split(value):
    high = value.astype(BF16)
    return high, (value - high.astype(F32)).astype(BF16)


def dot3(a, b, dims):
    go = functools.partial(lax.dot_general, dimension_numbers=(dims, ((), ())), preferred_element_type=F32)
    return go(a[0], b[0]) + (go(a[0], b[1]) + go(a[1], b[0]))


def cut(pair, at, size):
    return tuple(part[at : at + size, :] for part in pair)


def sym_product(pair, layers, size, dims):
    blocks = {}
    for a in range(layers):
        if dims == NT:
            left = tuple(part[a * size : (a + 1) * size, :] for part in pair)
            right = tuple(part[a * size :, :] for part in pair)
        else:
            left = tuple(part[:, a * size : (a + 1) * size] for part in pair)
            right = tuple(part[:, a * size :] for part in pair)
        strip = dot3(left, right, dims)
        for b in range(a, layers):
            blocks[a, b] = strip[:, (b - a) * size : (b - a + 1) * size]
    return blocks


def kept(mask_ref, layer, slot):
    return mask_ref[layer, slot - 1] > 0


def load_panel(out_ref, held, first, name, layers, size, mask_ref, top=0):
    if layers > 2:
        out_ref[top : top + layers * size, :] = jnp.zeros((layers * size, layers * size), F32)
    squares = 0.0
    for k, (low, high, slot) in enumerate(panel_blocks(name, layers)):
        value = jnp.where(kept(mask_ref, low, slot), held[first + k], 0.0)
        out_ref[top + low * size : top + (low + 1) * size, high * size : (high + 1) * size] = value
        squares = squares + squares_of(value)
    return squares


def start_loads(stored_ref, held, sems, wanted):
    copies = [
        pltpu.make_async_copy(stored_ref.at[low, slot], held.at[k], sems.at[k])
        for k, (low, slot) in enumerate(wanted)
    ]
    for copy in copies:
        copy.start()
    return copies


def lanes(value):
    return jnp.sum(value.reshape(-1, 8, value.shape[-1]), axis=0)


def squares_of(value):
    return lanes(value * value)


def wanted(names, layers):
    return [(layer, 0) for layer in range(layers) if "C" in names] + [
        (low, slot) for name in names for low, _, slot in panel_blocks(name, layers)
    ]


def pack_e_body(layers, size, mask_ref, stored_ref, down_ref, sums_ref, held, sems, mask, mask_sem):
    n = layers * size
    small = pltpu.make_async_copy(mask_ref, mask, mask_sem)
    small.start()
    copies = start_loads(stored_ref, held, sems, wanted("SE", layers))
    small.wait()
    at = 0
    squares = 0.0
    for name, top in (("S", 0), ("E", n)):
        count = len(panel_blocks(name, layers))
        for copy in copies[at : at + count]:
            copy.wait()
        squares = squares + load_panel(down_ref, held, at, name, layers, size, mask, top=top)
        at += count
    sums_ref[...] = 2.0 * squares


def pack_t_body(
    layers, size, mask_ref, stored_ref, onsite_ref, before_ref, t_ref, packed_ref, c_ref, sums_ref,
    held, sems, mask, mask_sem, onsite, onsite_sem,
):
    n = layers * size
    small = [
        pltpu.make_async_copy(mask_ref, mask, mask_sem),
        pltpu.make_async_copy(onsite_ref, onsite, onsite_sem),
    ]
    for copy in small:
        copy.start()
    copies = start_loads(stored_ref, held, sems, wanted("CN", layers))
    for copy in small:
        copy.wait()
    row, col = rows_cols(size)
    if layers > 2:
        c_ref[...] = jnp.zeros(c_ref.shape, F32)
    trace = squares = 0.0
    for layer in range(layers):
        copies[layer].wait()
        block = held[layer]
        diagonal = jnp.where(row == col, onsite[layer : layer + 1, :], 0.0)
        trace = trace + lanes(jnp.where(row == col, block, 0.0) + diagonal)
        block = 0.5 * (block + block.T) + diagonal
        squares = squares + squares_of(block)
        c_ref[layer * size : (layer + 1) * size, layer * size : (layer + 1) * size] = block
    at = layers
    for low, high, slot in panel_blocks("C", layers):
        copies[at].wait()
        block = jnp.where(kept(mask, low, slot), held[at], 0.0)
        squares = squares + 2.0 * squares_of(block)
        c_ref[low * size : (low + 1) * size, high * size : (high + 1) * size] = block
        c_ref[high * size : (high + 1) * size, low * size : (low + 1) * size] = block.T
        at += 1
    put_sym(
        packed_ref,
        lambda a, b: c_ref[a * size : (a + 1) * size, b * size : (b + 1) * size],
        layers,
        size,
    )
    t_ref[n:, :] = packed_ref[...]
    for copy in copies[at:]:
        copy.wait()
    sums_ref[:8, :] = trace
    squares = squares + 2.0 * load_panel(t_ref, held, at, "N", layers, size, mask)
    sums_ref[8:, :] = before_ref[...] + squares


def pack_d_body(layers, size, mask_ref, stored_ref, before_ref, d_ref, up_ref, sums_ref, held, sems, mask, mask_sem):
    small = pltpu.make_async_copy(mask_ref, mask, mask_sem)
    small.start()
    copies = start_loads(stored_ref, held, sems, wanted("D", layers))
    small.wait()
    for copy in copies:
        copy.wait()
    sums_ref[:8, :] = before_ref[:8, :]
    sums_ref[8:, :] = before_ref[8:, :] + 2.0 * load_panel(d_ref, held, 0, "D", layers, size, mask)
    blocks = sym_product(split(d_ref[...]), layers, size, TN)
    put_sym(up_ref, lambda a, b: blocks[a, b], layers, size)


def local_g_body(layers, size, _, sums_ref, more_ref, t_ref, down_ref, d_ref, total_ref, g_ref, r_ref, yc_up_ref):
    n = layers * size
    total_ref[...] = sums_ref[...] + more_ref[...]
    n_now, e, d = split(t_ref[:n, :]), split(down_ref[n:, :]), split(d_ref[...])
    blocks = sym_product(e, layers, size, TN)
    g_ref[:n, :] = dot3(e, d, TN)
    put_sym(g_ref, lambda a, b: blocks[a, b], layers, size, first=n)
    r_ref[:n, :] = dot3(n_now, e, TN)
    r_ref[n:, :] = dot3(n_now, d, TN)
    blocks = sym_product(n_now, layers, size, TN)
    put_sym(yc_up_ref, lambda a, b: blocks[a, b], layers, size)


def local_y_body(
    layers, size, _, sums_ref, more_ref, c_ref, t_ref, down_ref, d_ref,
    total_ref, out_ref, yc_ref, yn_ref, ys_ref, ye_ref, yd_ref, zero, sems,
):
    total_ref[...] = sums_ref[...] + more_ref[...]
    zero[...] = jnp.zeros(zero.shape, F32)
    written = set(wanted(IN_PLANE, layers))
    copies = []
    for layer in range(layers):
        for slot in range(out_ref.shape[1]):
            if (layer, slot) not in written:
                copies.append(pltpu.make_async_copy(zero, out_ref.at[layer, slot], sems.at[len(copies)]))
                copies[-1].start()
    at = layers * size
    parts = (c_ref[...], t_ref[:at, :], down_ref[:at, :], down_ref[at:, :], d_ref[...])
    c, n, s, e, d = (split(part) for part in parts)
    yn_ref[...] = dot3(c, n, NN)
    ys_ref[...] = dot3(c, s, NN)
    ye_ref[...] = dot3(c, e, NN)
    yd_ref[...] = dot3(c, d, NN)
    terms = [
        sym_product(pair, layers, size, dims)
        for pair, dims in ((c, NT), (n, NT), (s, NT), (e, NT), (d, NT))
    ]
    put_sym(yc_ref, lambda a, b: sum(term[a, b] for term in terms), layers, size)
    for copy in copies:
        copy.wait()


def copy_body(layers, size, _, __, from_ref, to_ref):
    to_ref[...] = from_ref[...]


def g_body(layers, size, _, sums_ref, more_ref, g0_ref, below_ref, up_ref, total_ref, g_ref):
    n, last = layers * size, g_ref.shape[0] - 8
    parts = sums_ref[...] + more_ref[...]
    line = lax.broadcasted_iota(jnp.int32, total_ref.shape, 0)
    total = jnp.where(line % 4 == 0, jnp.sum(parts[:8, :]), jnp.sum(parts[8:, :]))
    total_ref[...] = total
    stu, eu = split(below_ref[:n, :].T), split(below_ref[n:, :])
    g_ref[:n, :] = g0_ref[:n, :] + dot3(stu, eu, NN)
    blocks = sym_product(stu, layers, size, NT)
    put_sym(g_ref, lambda a, b: blocks[a, b], layers, size, first=n)
    g_ref[n:, :] += g0_ref[n:, :] + up_ref[...]
    for at in range(layers):
        cols = slice(at * size, (at + 1) * size)
        g_ref[last:, cols] = jnp.where(line < 4, g_ref[last:, cols], total)


def both_body(layers, size, _, packed_ref, tx_ref, both_ref):
    n, tall = layers * size, sym_rows(layers, size)
    both_ref[:tall, :] = packed_ref[...]
    both_ref[tall:, :] = tx_ref[n:, :]


def early_body(layers, size, _, t_ref, e_ref, d_ref, below_ref, yn0_ref, ye0_ref, yd0_ref, yn_ref, ye_ref, yd_ref):
    at = layers * size
    n, e, d = split(t_ref[:at, :]), split(e_ref[at:, :]), split(d_ref[...])
    su, eu = split(below_ref[:at, :]), split(below_ref[at:, :])
    yn_ref[...] = yn0_ref[...] + dot3(e, su, NT) + dot3(d, eu, NT)
    ye_ref[...] = ye0_ref[...] + dot3(n, su, NN)
    yd_ref[...] = yd0_ref[...] + dot3(n, eu, NN)


def r_body(layers, size, _, __, r0_ref, below_ref, tx_ref, rs_ref, re_ref):
    n = layers * size
    su, eu, nx = split(below_ref[:n, :]), split(below_ref[n:, :]), split(tx_ref[:n, :])
    cx = split(whole_sym(take_sym(tx_ref[n:, :], layers, size), layers))
    rs_ref[...] = r0_ref[:n, :] + dot3(su, cx, NN) + dot3(eu, nx, NT)
    re_ref[...] = r0_ref[n:, :] + dot3(su, nx, NN)


def middle_body(layers, size, _, e_ref, d_ref, tx_ref, ye0_ref, yd0_ref, ye_ref, yd_ref):
    at = layers * size
    e, d, nx = split(e_ref[at:, :]), split(d_ref[...]), split(tx_ref[:at, :])
    cx = split(whole_sym(take_sym(tx_ref[at:, :], layers, size), layers))
    ye_ref[...] = ye0_ref[...] + dot3(e, cx, NN) + dot3(d, nx, NT)
    yd_ref[...] = yd0_ref[...] + dot3(e, nx, NN)


def middle_c_body(layers, size, sums_ref, t_ref, d_ref, both_ref, yn0_ref, yd0_ref, total_ref, yn_ref, yd_ref):
    at, tall = layers * size, sym_rows(layers, size)
    total_ref[...] = sums_ref[...]
    n, d = split(t_ref[:at, :]), split(d_ref[...])
    cu = split(whole_sym(take_sym(both_ref[:tall, :], layers, size), layers))
    cxu = split(whole_sym(take_sym(both_ref[tall:, :], layers, size), layers))
    yn_ref[...] = yn0_ref[...] + dot3(n, cu, NN)
    yd_ref[...] = yd0_ref[...] + dot3(d, cxu, NN)


def twice_h(target, size, sums):
    t1, t2 = sums[0:1, :], sums[1:2, :]
    return 2.0 * jax.nn.sigmoid((jnp.abs(t2 - target) - jnp.abs(2.0 * t1 - t2 - target)) / size)


class Sender:
    def __init__(self, mask_ref, out_ref, held, sems):
        self.mask_ref, self.out_ref, self.held, self.sems = mask_ref, out_ref, held, sems
        self.copies = []

    def send(self, value, low, slot):
        k = len(self.copies)
        self.held[k] = jnp.where(kept(self.mask_ref, low, slot), value, 0.0) if slot else value
        self.copies.append(pltpu.make_async_copy(self.held.at[k], self.out_ref.at[low, slot], self.sems.at[k]))
        self.copies[-1].start()

    def send_panel(self, name, twice, a_ref, terms, layers, size):
        for low, high, slot in panel_blocks(name, layers):
            rows, cols = slice(low * size, (low + 1) * size), slice(high * size, (high + 1) * size)
            y = sum(ref[rows, cols] for ref in terms)
            self.send(y + twice * (a_ref[rows, cols] - y), low, slot)

    def wait(self):
        for copy in self.copies:
            copy.wait()


def last_c_body(
    target, layers, size, mask_ref, _, c_ref, t_ref, down_ref, d_ref, yc_ref, yn_ref, ys_ref, yd_ref, yc_in_ref, rs_ref, g_ref,
    *rest,
):
    *sums_refs, out_ref, twice_ref, held, sems = rest
    n, last = layers * size, g_ref.shape[0] - 8
    line = lax.broadcasted_iota(jnp.int32, (8, size), 0)
    beside = g_ref[last:, :size]
    sums = jnp.where(line == 0, beside[4:5, :], beside[5:6, :])
    twice = twice_h(target, size, sum((ref[...] for ref in sums_refs), start=sums))
    twice_ref[...] = jnp.broadcast_to(twice, twice_ref.shape)
    sender = Sender(mask_ref, out_ref, held, sems)
    for name, a_ref, *terms in (
        ("D", d_ref, yd_ref),
        ("N", t_ref.at[:n, :], yn_ref, g_ref),
        ("S", down_ref.at[:n, :], ys_ref, rs_ref),
    ):
        sender.send_panel(name, twice, a_ref, terms, layers, size)
    blocks = take_sym(yc_ref[...] + yc_in_ref[...] + g_ref[n:, :], layers, size)
    for low, high, slot in panel_blocks("C", layers) + [(layer, layer, 0) for layer in range(layers)]:
        rows, cols = slice(low * size, (low + 1) * size), slice(high * size, (high + 1) * size)
        y = blocks[low, high]
        sender.send(y + twice * (c_ref[rows, cols] - y), low, slot)
    sender.wait()


def last_e_body(layers, size, mask_ref, _, twice_ref, down_ref, ye_ref, re_ref, out_ref, held, sems):
    sender = Sender(mask_ref, out_ref, held, sems)
    sender.send_panel("E", twice_ref[0:1, :], down_ref.at[layers * size :, :], [ye_ref, re_ref], layers, size)
    sender.wait()


def call(body, layers, size, outs, spaces, scratch=(), limit=24, out_spaces=None, aliases=None):
    return pl.pallas_call(
        functools.partial(body, layers, size),
        out_shape=[jax.ShapeDtypeStruct(shape, F32) for shape in outs],
        in_specs=[pl.BlockSpec(memory_space=space) for space in spaces],
        out_specs=[pl.BlockSpec(memory_space=space) for space in out_spaces or [pltpu.VMEM] * len(outs)],
        scratch_shapes=list(scratch),
        input_output_aliases=aliases or {},
        compiler_params=pltpu.CompilerParams(vmem_limit_bytes=limit << 20),
    )


def passed_along(value, axis, by):
    peers = lax.axis_size(axis)
    return lax.ppermute(value, axis, [(i, (i + by) % peers) for i in range(peers)])


def swapped(value, axis, bit):
    peers = lax.axis_size(axis)
    return lax.ppermute(value, axis, [(i, i ^ bit) for i in range(peers)])


def shards(stored_blocks, onsite, bond_mask):
    stored, onsite, mask = stored_blocks[0, 0], onsite[0, 0], bond_mask[0, 0]
    layers, slots, size = stored.shape[:3]
    n, tall = layers * size, sym_rows(layers, size)
    panel, packed, sums, total = (n, n), (tall, n), (16, size), (8, size)
    vmem, smem, hbm = pltpu.VMEM, pltpu.SMEM, pltpu.HBM

    def blocks(count):
        return [pltpu.VMEM((count, size, size), F32), pltpu.SemaphoreType.DMA((count,))]

    go = functools.partial(call, layers=layers, size=size)
    stored, onsite, mask_hbm = (pltpu.with_memory_space_constraint(value, hbm) for value in (stored, onsite, mask))

    peers = lax.axis_size("col")
    bits = [1 << k for k in range(peers.bit_length() - 1)]
    bits = bits[:1] + bits[2:] + bits[1:2]

    def arriving(value):
        return swapped(value, "col", bits.pop(0)) if bits else jnp.zeros_like(value)

    small = [pltpu.SMEM(mask.shape, mask.dtype), pltpu.SemaphoreType.DMA]
    down, own = go(
        pack_e_body, outs=[(2 * n, n), total], spaces=[hbm] * 2, scratch=blocks(len(wanted("SE", layers))) + small
    )(mask_hbm, stored)
    below = passed_along(down, "col", -1)
    T, Cp, C, own = go(
        pack_t_body, outs=[(n + tall, n), packed, panel, sums], spaces=[hbm] * 3 + [vmem],
        scratch=blocks(len(wanted("CN", layers))) + small + [pltpu.VMEM(onsite.shape, F32), pltpu.SemaphoreType.DMA],
    )(mask_hbm, stored, onsite, own)
    T_x = passed_along(T, "row", -1)
    D, gc, own = go(
        pack_d_body, outs=[panel, packed, sums], spaces=[hbm] * 2 + [vmem], scratch=blocks(len(wanted("D", layers))) + small
    )(mask_hbm, stored, own)
    gc_in = passed_along(gc, "col", 1)
    if peers.bit_count() > 1:
        own = own + sum(passed_along(own, "col", by) for by in range(1, peers))
        bits = []
    while len(bits) > 3:
        own = own + arriving(own)
    more = arriving(own)
    own, g0, r0, yc_up = go(local_g_body, outs=[sums, (n + tall, n), (2 * n, n), packed], spaces=[hbm] + [vmem] * 5)(
        gc, own, more, T, down, D
    )
    more = arriving(own)
    own, out, yc, yn, ys, ye, yd = go(
        local_y_body, outs=[sums, (layers, slots, size, size), packed] + [panel] * 4, spaces=[hbm] + [vmem] * 6,
        out_spaces=[vmem, hbm] + [vmem] * 5, scratch=[pltpu.VMEM((size, size), F32), pltpu.SemaphoreType.DMA((layers * slots,))],
    )(g0, own, more, C, T, down, D)
    more = arriving(own)
    (yc_up,) = go(copy_body, outs=[packed], spaces=[hbm] * 2 + [vmem])(yc, below, yc_up)
    yc_in = passed_along(yc_up, "col", 1)
    own, g = go(g_body, outs=[total, (n + tall, n)], spaces=[hbm] + [vmem] * 5)(yc_up, own, more, g0, below, gc_in)
    g_in = passed_along(g, "row", 1)
    (both,) = go(both_body, outs=[(2 * tall, n)], spaces=[hbm] + [vmem] * 2)(g, Cp, T_x)
    both_u = passed_along(both, "col", -1)
    rs, re = go(r_body, outs=[panel, panel], spaces=[hbm] * 2 + [vmem] * 3)(both, yc_in, r0, below, T_x)
    rs_in, re_in = passed_along(rs, "col", 1), passed_along(re, "col", 1)
    yn, ye, yd = go(early_body, outs=[panel] * 3, spaces=[hbm] + [vmem] * 7)(rs, T, down, D, below, yn, ye, yd)
    ye, yd = go(middle_body, outs=[panel] * 2, spaces=[hbm] + [vmem] * 5)(yn, down, D, T_x, ye, yd)
    own, yn, yd = go(middle_c_body, outs=[total, panel, panel], spaces=[vmem] * 6)(own, T, D, both_u, yn, yd)
    every = [own] + [passed_along(own, "row", -by) for by in range(1, lax.axis_size("row") - 1)]
    cells = lax.axis_size("row") * lax.axis_size("col") * layers
    target = float(cells * size // 2)
    out, twice = go(
        functools.partial(last_c_body, target), outs=[out.shape, total], out_spaces=[hbm, vmem],
        spaces=[smem, hbm] + [vmem] * (11 + len(every)), scratch=blocks(len(wanted("CNSD", layers))), aliases={1: 0},
    )(mask, out, C, T, down, D, yc, yn, ys, yd, yc_in, rs_in, g_in, *every)
    (out,) = go(
        last_e_body, outs=[out.shape], out_spaces=[hbm], spaces=[smem, hbm] + [vmem] * 4,
        scratch=blocks(len(wanted("E", layers))), aliases={1: 0},
    )(mask, out, twice, down, ye, re_in)
    return out[None, None]


def solution(mesh):
    in_specs = (
        P("row", "col", None, None, None, None),
        P("row", "col", None, None),
        P("row", "col", None, None),
    )
    out_specs = P("row", "col", None, None, None, None)
    return jax.shard_map(shards, mesh=mesh, in_specs=in_specs, out_specs=out_specs, check_vma=False)
```

```python
import functools

import jax
import jax.numpy as jnp
from jax import lax
from jax.experimental import pallas as pl
from jax.experimental.pallas import tpu as pltpu
from jax.sharding import PartitionSpec as P


F32 = jnp.float32
BF16 = jnp.bfloat16
NN = ((1,), (0,))
NT = ((1,), (1,))
TN = ((0,), (0,))
IN_PLANE = {"C": (0, 0), "N": (0, 1), "S": (1, -1), "E": (1, 0), "D": (1, 1)}


def offset_list():
    steps = (-1, 0, 1)
    return [(i, j, k) for i in steps for j in steps for k in steps if (i, j, k) > (0, 0, 0)]


def slot_number(offset):
    return offset_list().index(offset) + 1


def panel_blocks(name, layers):
    side = IN_PLANE[name]
    found = []
    for low in range(layers):
        for high in range(layers):
            step = high - low
            if abs(step) <= 1 and (*side, step) > (0, 0, 0):
                found.append((low, high, slot_number((*side, step))))
    return found


def sym_rows(layers, size):
    blocks = layers * (layers - 1) // 2 + (layers + 1) // 2
    return -(-blocks // layers) * size + 8


def rows_cols(size):
    return (
        lax.broadcasted_iota(jnp.int32, (size, size), 0),
        lax.broadcasted_iota(jnp.int32, (size, size), 1),
    )


def block_slices(k, layers, size):
    row, col = k // layers * size, k % layers * size
    return slice(row, row + size), slice(col, col + size)


def sym_places(layers):
    above = [(a, b) for a in range(layers) for b in range(a + 1, layers)]
    pairs = list(range(0, layers, 2))
    return list(enumerate(above)), [(len(above) + k, k, a) for k, a in enumerate(pairs)]


def put_sym(ref, get, layers, size, first=0):
    row, col = rows_cols(size)
    above, pairs = sym_places(layers)
    last = first + sym_rows(layers, size) - 8

    def put(k, value):
        rows, cols = block_slices(k, layers, size)
        ref[first + rows.start : first + rows.stop, cols] = value

    ref[last : last + 8, :] = jnp.zeros((8, layers * size), F32)
    if len(above) + len(pairs) < (last - first) // size * layers:
        ref[last - size : last, :] = jnp.zeros((size, layers * size), F32)
    for k, (a, b) in above:
        put(k, get(a, b))
    for k, mark, a in pairs:
        block = get(a, a)
        if a + 1 < layers:
            other = get(a + 1, a + 1)
            line = jnp.sum(jnp.where(row == col, other, 0.0), axis=0, keepdims=True)
            ref[last : last + 8, mark * size : (mark + 1) * size] = jnp.broadcast_to(line, (8, size))
            block = jnp.where(row <= col, block, other)
        put(k, block)


def take_sym(packed, layers, size):
    row, col = rows_cols(size)
    above, pairs = sym_places(layers)
    last = sym_rows(layers, size) - 8
    blocks = {}
    for k, (a, b) in above:
        rows, cols = block_slices(k, layers, size)
        blocks[a, b] = packed[rows, cols]
    for k, mark, a in pairs:
        rows, cols = block_slices(k, layers, size)
        block = packed[rows, cols]
        if a + 1 < layers:
            flipped = block.T
            line = packed[last : last + 1, mark * size : (mark + 1) * size]
            blocks[a, a] = jnp.where(row <= col, block, flipped)
            blocks[a + 1, a + 1] = jnp.where(row == col, line, jnp.where(row < col, flipped, block))
        else:
            blocks[a, a] = block
    return blocks


def whole_sym(blocks, layers):
    rows = []
    for a in range(layers):
        rows.append(
            jnp.concatenate(
                [blocks[a, b] if a <= b else blocks[b, a].T for b in range(layers)], axis=1
            )
        )
    return jnp.concatenate(rows, axis=0)


def split(value):
    high = value.astype(BF16)
    return high, (value - high.astype(F32)).astype(BF16)


def dot3(a, b, dims):
    go = functools.partial(lax.dot_general, dimension_numbers=(dims, ((), ())), preferred_element_type=F32)
    return go(a[0], b[0]) + (go(a[0], b[1]) + go(a[1], b[0]))


def cut(pair, at, size):
    return tuple(part[at : at + size, :] for part in pair)


def sym_product(pair, layers, size, dims):
    blocks = {}
    for a in range(layers):
        if dims == NT:
            left = tuple(part[a * size : (a + 1) * size, :] for part in pair)
            right = tuple(part[a * size :, :] for part in pair)
        else:
            left = tuple(part[:, a * size : (a + 1) * size] for part in pair)
            right = tuple(part[:, a * size :] for part in pair)
        strip = dot3(left, right, dims)
        for b in range(a, layers):
            blocks[a, b] = strip[:, (b - a) * size : (b - a + 1) * size]
    return blocks


def kept(mask_ref, layer, slot):
    return mask_ref[layer, slot - 1] > 0


def start_panel(stored_ref, out_ref, sems, first, name, layers, size, top=0):
    copies = []
    for k, (low, high, slot) in enumerate(panel_blocks(name, layers)):
        place = out_ref.at[pl.ds(top + low * size, size), pl.ds(high * size, size)]
        copies.append(pltpu.make_async_copy(stored_ref.at[low, slot], place, sems.at[first + k]))
        copies[-1].start()
    return copies


def end_panel(copies, out_ref, name, layers, size, mask_ref, top=0):
    blocks = panel_blocks(name, layers)
    for low in range(layers):
        for high in range(layers):
            if (low, high) not in [block[:2] for block in blocks]:
                out_ref[top + low * size : top + (low + 1) * size, high * size : (high + 1) * size] = jnp.zeros((size, size), F32)
    for copy, (low, high, slot) in zip(copies, blocks, strict=True):
        copy.wait()

        @pl.when(jnp.logical_not(kept(mask_ref, low, slot)))
        def _(low=low, high=high):
            out_ref[top + low * size : top + (low + 1) * size, high * size : (high + 1) * size] = jnp.zeros((size, size), F32)


def start_loads(stored_ref, held, sems, wanted):
    copies = [
        pltpu.make_async_copy(stored_ref.at[low, slot], held.at[k], sems.at[k])
        for k, (low, slot) in enumerate(wanted)
    ]
    for copy in copies:
        copy.start()
    return copies


def lanes(value):
    return jnp.sum(value.reshape(-1, 8, value.shape[-1]), axis=0)


def squares_of(value):
    return lanes(value * value)


def wanted(names, layers):
    return [(layer, 0) for layer in range(layers) if "C" in names] + [
        (low, slot) for name in names for low, _, slot in panel_blocks(name, layers)
    ]


def pack_e_body(layers, size, mask_ref, stored_ref, down_ref, sems, mask, mask_sem):
    n = layers * size
    small = pltpu.make_async_copy(mask_ref, mask, mask_sem)
    small.start()
    first = start_panel(stored_ref, down_ref, sems, 0, "S", layers, size)
    second = start_panel(stored_ref, down_ref, sems, len(first), "E", layers, size, top=n)
    small.wait()
    end_panel(first, down_ref, "S", layers, size, mask)
    end_panel(second, down_ref, "E", layers, size, mask, top=n)


def pack_t_body(layers, size, mask_ref, stored_ref, onsite_ref, _, t_ref, held, sems, mask, mask_sem, onsite, onsite_sem):
    n = layers * size
    small = [
        pltpu.make_async_copy(mask_ref, mask, mask_sem),
        pltpu.make_async_copy(onsite_ref, onsite, onsite_sem),
    ]
    for copy in small:
        copy.start()
    copies = start_loads(stored_ref, held, sems, wanted("C", layers))
    panel = start_panel(stored_ref, t_ref, sems, len(copies), "N", layers, size)
    for copy in small:
        copy.wait()
    row, col = rows_cols(size)
    blocks = {}
    for layer in range(layers):
        copies[layer].wait()
        block = held[layer]
        blocks[layer, layer] = 0.5 * (block + block.T) + jnp.where(row == col, onsite[layer : layer + 1, :], 0.0)
    for k, (low, high, slot) in enumerate(panel_blocks("C", layers), start=layers):
        copies[k].wait()
        blocks[low, high] = jnp.where(kept(mask, low, slot), held[k], 0.0)
    put_sym(t_ref, lambda a, b: blocks.get((a, b), jnp.zeros((size, size), F32)), layers, size, first=n)
    end_panel(panel, t_ref, "N", layers, size, mask)


def pack_d_body(layers, size, mask_ref, stored_ref, _, d_ref, up_ref, sems, mask, mask_sem):
    small = pltpu.make_async_copy(mask_ref, mask, mask_sem)
    small.start()
    copies = start_panel(stored_ref, d_ref, sems, 0, "D", layers, size)
    small.wait()
    end_panel(copies, d_ref, "D", layers, size, mask)
    blocks = sym_product(split(d_ref[...]), layers, size, TN)
    put_sym(up_ref, lambda a, b: blocks[a, b], layers, size)


def sums_body(layers, size, mask_ref, _, down_ref, t_ref, d_ref, packed_ref, c_ref, keep_ref, sums_ref):
    n = layers * size
    packed_ref[...] = t_ref[n:, :]
    c_ref[...] = whole_sym(take_sym(t_ref[n:, :], layers, size), layers)
    keep_ref[...] = jnp.zeros(keep_ref.shape, F32)
    slots = keep_ref.shape[0] // layers
    for low, slot in wanted(IN_PLANE, layers):
        here = 1.0 if slot == 0 else jnp.where(kept(mask_ref, low, slot), 1.0, 0.0)
        keep_ref[low * slots + slot : low * slots + slot + 1, :] = jnp.full((1, size), here, F32)
    row, col = rows_cols(size)
    trace = 0.0
    for layer in range(layers):
        here = slice(layer * size, (layer + 1) * size)
        trace = trace + lanes(jnp.where(row == col, c_ref[here, here], 0.0))
    sums_ref[:8, :] = trace
    squares = squares_of(c_ref[...])
    for ref in (down_ref.at[:n, :], down_ref.at[n:, :], t_ref.at[:n, :], d_ref):
        squares = squares + 2.0 * squares_of(ref[...])
    sums_ref[8:, :] = sum(squares[:, at * size : (at + 1) * size] for at in range(layers))


def local_g_body(layers, size, _, sums_ref, more_ref, t_ref, down_ref, d_ref, total_ref, g_ref, r_ref, yc_up_ref):
    n = layers * size
    total_ref[...] = sums_ref[...] + more_ref[...]
    n_now, e, d = split(t_ref[:n, :]), split(down_ref[n:, :]), split(d_ref[...])
    blocks = sym_product(e, layers, size, TN)
    g_ref[:n, :] = dot3(e, d, TN)
    put_sym(g_ref, lambda a, b: blocks[a, b], layers, size, first=n)
    r_ref[:n, :] = dot3(n_now, e, TN)
    r_ref[n:, :] = dot3(n_now, d, TN)
    blocks = sym_product(n_now, layers, size, TN)
    put_sym(yc_up_ref, lambda a, b: blocks[a, b], layers, size)


def local_y_body(
    layers, size, _, sums_ref, more_ref, c_ref, t_ref, down_ref, d_ref,
    total_ref, out_ref, yc_ref, yn_ref, ys_ref, ye_ref, yd_ref, zero, sems,
):
    total_ref[...] = sums_ref[...] + more_ref[...]
    zero[...] = jnp.zeros(zero.shape, F32)
    written = set(wanted(IN_PLANE, layers))
    copies = []
    for layer in range(layers):
        for slot in range(out_ref.shape[1]):
            if (layer, slot) not in written:
                copies.append(pltpu.make_async_copy(zero, out_ref.at[layer, slot], sems.at[len(copies)]))
                copies[-1].start()
    at = layers * size
    parts = (c_ref[...], t_ref[:at, :], down_ref[:at, :], down_ref[at:, :], d_ref[...])
    c, n, s, e, d = (split(part) for part in parts)
    yn_ref[...] = dot3(c, n, NN)
    ys_ref[...] = dot3(c, s, NN)
    ye_ref[...] = dot3(c, e, NN)
    yd_ref[...] = dot3(c, d, NN)
    terms = [
        sym_product(pair, layers, size, dims)
        for pair, dims in ((c, NT), (n, NT), (s, NT), (e, NT), (d, NT))
    ]
    put_sym(yc_ref, lambda a, b: sum(term[a, b] for term in terms), layers, size)
    for copy in copies:
        copy.wait()


def copy_body(layers, size, _, __, from_ref, to_ref):
    to_ref[...] = from_ref[...]


def g_body(layers, size, _, sums_ref, more_ref, g0_ref, below_ref, up_ref, total_ref, g_ref):
    n, last = layers * size, g_ref.shape[0] - 8
    parts = sums_ref[...] + more_ref[...]
    line = lax.broadcasted_iota(jnp.int32, total_ref.shape, 0)
    total = jnp.where(line % 4 == 0, jnp.sum(parts[:8, :]), jnp.sum(parts[8:, :]))
    total_ref[...] = total
    stu, eu = split(below_ref[:n, :].T), split(below_ref[n:, :])
    g_ref[:n, :] = g0_ref[:n, :] + dot3(stu, eu, NN)
    blocks = sym_product(stu, layers, size, NT)
    put_sym(g_ref, lambda a, b: blocks[a, b], layers, size, first=n)
    g_ref[n:, :] += g0_ref[n:, :] + up_ref[...]
    for at in range(layers):
        cols = slice(at * size, (at + 1) * size)
        g_ref[last:, cols] = jnp.where(line < 4, g_ref[last:, cols], total)


def early_body(layers, size, _, t_ref, e_ref, d_ref, below_ref, cu_ref, yn0_ref, ye0_ref, yd0_ref, yn_ref, ye_ref, yd_ref):
    at = layers * size
    n, e, d = split(t_ref[:at, :]), split(e_ref[at:, :]), split(d_ref[...])
    su, eu = split(below_ref[:at, :]), split(below_ref[at:, :])
    cu = split(whole_sym(take_sym(cu_ref, layers, size), layers))
    yn_ref[...] = yn0_ref[...] + dot3(e, su, NT) + dot3(d, eu, NT) + dot3(n, cu, NN)
    ye_ref[...] = ye0_ref[...] + dot3(n, su, NN)
    yd_ref[...] = yd0_ref[...] + dot3(n, eu, NN)


def r_body(layers, size, _, __, r0_ref, below_ref, tx_ref, rs_ref, re_ref):
    n = layers * size
    su, eu, nx = split(below_ref[:n, :]), split(below_ref[n:, :]), split(tx_ref[:n, :])
    cx = split(whole_sym(take_sym(tx_ref[n:, :], layers, size), layers))
    rs_ref[...] = r0_ref[:n, :] + dot3(su, cx, NN) + dot3(eu, nx, NT)
    re_ref[...] = r0_ref[n:, :] + dot3(su, nx, NN)


def hand_body(layers, size, _, __, tx_ref, cx_ref):
    cx_ref[...] = tx_ref[layers * size :, :]


def middle_body(layers, size, _, e_ref, d_ref, tx_ref, ye0_ref, yd0_ref, ye_ref, yd_ref):
    at = layers * size
    e, d, nx = split(e_ref[at:, :]), split(d_ref[...]), split(tx_ref[:at, :])
    cx = split(whole_sym(take_sym(tx_ref[at:, :], layers, size), layers))
    ye_ref[...] = ye0_ref[...] + dot3(e, cx, NN) + dot3(d, nx, NT)
    yd_ref[...] = yd0_ref[...] + dot3(e, nx, NN)


def middle_c_body(layers, size, _, sums_ref, d_ref, cxu_ref, yd0_ref, total_ref, yd_ref):
    total_ref[...] = sums_ref[...]
    cxu = split(whole_sym(take_sym(cxu_ref, layers, size), layers))
    yd_ref[...] = yd0_ref[...] + dot3(split(d_ref[...]), cxu, NN)


def twice_h(target, size, sums):
    t1, t2 = sums[0:1, :], sums[1:2, :]
    return 2.0 * jax.nn.sigmoid((jnp.abs(t2 - target) - jnp.abs(2.0 * t1 - t2 - target)) / size)


class Sender:
    def __init__(self, twice, keep_ref, out_ref, held, sems):
        self.twice, self.keep_ref, self.out_ref, self.held, self.sems = twice, keep_ref, out_ref, held, sems
        self.copies = []

    def send(self, y, a, low, slot):
        k, at = len(self.copies), low * self.out_ref.shape[1] + slot
        self.held[k] = self.keep_ref[at : at + 1, :] * (y + self.twice * (a - y))
        self.copies.append(pltpu.make_async_copy(self.held.at[k], self.out_ref.at[low, slot], self.sems.at[k]))
        self.copies[-1].start()

    def send_panel(self, name, a_ref, terms, layers, size):
        for low, high, slot in panel_blocks(name, layers):
            rows, cols = slice(low * size, (low + 1) * size), slice(high * size, (high + 1) * size)
            self.send(sum(ref[rows, cols] for ref in terms), a_ref[rows, cols], low, slot)

    def wait(self):
        for copy in self.copies:
            copy.wait()


def last_c_body(
    target, layers, size, keep_ref, _, c_ref, t_ref, s_ref, d_ref, yc_ref, yn_ref, ys_ref, yd_ref, yc_in_ref, rs_ref, g_ref, *rest
):
    *sums_refs, out_ref, twice_ref, held, sems = rest
    n, last = layers * size, g_ref.shape[0] - 8
    line = lax.broadcasted_iota(jnp.int32, (8, size), 0)
    beside = g_ref[last:, :size]
    sums = jnp.where(line == 0, beside[4:5, :], beside[5:6, :])
    twice = twice_h(target, size, sum((ref[...] for ref in sums_refs), start=sums))
    twice_ref[...] = jnp.broadcast_to(twice, twice_ref.shape)
    sender = Sender(twice, keep_ref, out_ref, held, sems)
    sender.send_panel("D", d_ref, [yd_ref], layers, size)
    sender.send_panel("S", s_ref, [ys_ref, rs_ref], layers, size)
    sender.send_panel("N", t_ref, [yn_ref, g_ref], layers, size)
    blocks = take_sym(yc_ref[...] + yc_in_ref[...] + g_ref[n:, :], layers, size)
    for low, high, slot in panel_blocks("C", layers) + [(layer, layer, 0) for layer in range(layers)]:
        rows, cols = slice(low * size, (low + 1) * size), slice(high * size, (high + 1) * size)
        sender.send(blocks[low, high], c_ref[rows, cols], low, slot)
    sender.wait()


def last_e_body(layers, size, keep_ref, _, twice_ref, down_ref, ye_ref, re_ref, out_ref, held, sems):
    sender = Sender(twice_ref[0:1, :], keep_ref, out_ref, held, sems)
    sender.send_panel("E", down_ref.at[layers * size :, :], [ye_ref, re_ref], layers, size)
    sender.wait()


def call(body, layers, size, outs, spaces, scratch=(), limit=24, out_spaces=None, aliases=None):
    return pl.pallas_call(
        functools.partial(body, layers, size),
        out_shape=[jax.ShapeDtypeStruct(shape, F32) for shape in outs],
        in_specs=[pl.BlockSpec(memory_space=space) for space in spaces],
        out_specs=[pl.BlockSpec(memory_space=space) for space in out_spaces or [pltpu.VMEM] * len(outs)],
        scratch_shapes=list(scratch),
        input_output_aliases=aliases or {},
        compiler_params=pltpu.CompilerParams(vmem_limit_bytes=limit << 20),
    )


def passed_along(value, axis, by):
    peers = lax.axis_size(axis)
    return lax.ppermute(value, axis, [(i, (i + by) % peers) for i in range(peers)])


def swapped(value, axis, bit):
    peers = lax.axis_size(axis)
    return lax.ppermute(value, axis, [(i, i ^ bit) for i in range(peers)])


def shards(stored_blocks, onsite, bond_mask):
    stored, onsite, mask = stored_blocks[0, 0], onsite[0, 0], bond_mask[0, 0]
    layers, slots, size = stored.shape[:3]
    n, tall = layers * size, sym_rows(layers, size)
    panel, packed, sums, total = (n, n), (tall, n), (16, size), (8, size)
    vmem, smem, hbm = pltpu.VMEM, pltpu.SMEM, pltpu.HBM

    def blocks(count):
        return [pltpu.VMEM((count, size, size), F32), pltpu.SemaphoreType.DMA((count,))]

    go = functools.partial(call, layers=layers, size=size)
    stored, onsite, mask_hbm = (pltpu.with_memory_space_constraint(value, hbm) for value in (stored, onsite, mask))

    peers = lax.axis_size("col")
    bits = [1 << k for k in range(peers.bit_length() - 1)]
    bits = bits[:1] + bits[2:] + bits[1:2]

    def arriving(value):
        return swapped(value, "col", bits.pop(0)) if bits else jnp.zeros_like(value)

    small = [pltpu.SMEM(mask.shape, mask.dtype), pltpu.SemaphoreType.DMA]
    count = {name: len(wanted(name, layers)) for name in IN_PLANE}
    (down,) = go(
        pack_e_body, outs=[(2 * n, n)], spaces=[hbm] * 2, scratch=[pltpu.SemaphoreType.DMA((count["S"] + count["E"],))] + small
    )(mask_hbm, stored)
    below = passed_along(down, "col", -1)
    (T,) = go(
        pack_t_body, outs=[(n + tall, n)], spaces=[hbm] * 4,
        scratch=[pltpu.VMEM((count["C"], size, size), F32), pltpu.SemaphoreType.DMA((count["C"] + count["N"],))]
        + small + [pltpu.VMEM(onsite.shape, F32), pltpu.SemaphoreType.DMA],
    )(mask_hbm, stored, onsite, down)
    T_x = passed_along(T, "row", -1)
    D, gc = go(
        pack_d_body, outs=[panel, packed], spaces=[hbm] * 3, scratch=[pltpu.SemaphoreType.DMA((count["D"],))] + small
    )(mask_hbm, stored, T)
    gc_in = passed_along(gc, "col", 1)
    Cp, C, keep, own = go(sums_body, outs=[packed, panel, (layers * slots, size), sums], spaces=[smem, hbm] + [vmem] * 3)(
        mask, gc, down, T, D
    )
    if peers.bit_count() > 1:
        own = own + sum(passed_along(own, "col", by) for by in range(1, peers))
        bits = []
    while len(bits) > 3:
        own = own + arriving(own)
    more = arriving(own)
    own, g0, r0, yc_up = go(local_g_body, outs=[sums, (n + tall, n), (2 * n, n), packed], spaces=[hbm] + [vmem] * 5)(
        gc, own, more, T, down, D
    )
    more = arriving(own)
    own, out, yc, yn, ys, ye, yd = go(
        local_y_body, outs=[sums, (layers, slots, size, size), packed] + [panel] * 4, spaces=[hbm] + [vmem] * 6,
        out_spaces=[vmem, hbm] + [vmem] * 5, scratch=[pltpu.VMEM((size, size), F32), pltpu.SemaphoreType.DMA((layers * slots,))],
    )(g0, own, more, C, T, down, D)
    more = arriving(own)
    (yc_up,) = go(copy_body, outs=[packed], spaces=[hbm] * 2 + [vmem])(yc, below, yc_up)
    yc_in = passed_along(yc_up, "col", 1)
    own, g = go(g_body, outs=[total, (n + tall, n)], spaces=[hbm] + [vmem] * 5)(yc_up, own, more, g0, below, gc_in)
    g_in = passed_along(g, "row", 1)
    Cp_u = passed_along(Cp, "col", -1)
    rs, re = go(r_body, outs=[panel, panel], spaces=[hbm] * 2 + [vmem] * 3)(g, yc_in, r0, below, T_x)
    rs_in, re_in = passed_along(rs, "col", 1), passed_along(re, "col", 1)
    (Cp_x,) = go(hand_body, outs=[packed], spaces=[hbm] * 2 + [vmem])(rs, Cp_u, T_x)
    Cp_xu = passed_along(Cp_x, "col", -1)
    yn, ye, yd = go(early_body, outs=[panel] * 3, spaces=[hbm] + [vmem] * 8)(Cp_x, T, down, D, below, Cp_u, yn, ye, yd)
    ye, yd = go(middle_body, outs=[panel, panel], spaces=[hbm] + [vmem] * 5)(yn, down, D, T_x, ye, yd)
    own, yd = go(middle_c_body, outs=[total, panel], spaces=[hbm] + [vmem] * 4)(ye, own, D, Cp_xu, yd)
    every = [own] + [passed_along(own, "row", -by) for by in range(1, lax.axis_size("row") - 1)]
    cells = lax.axis_size("row") * lax.axis_size("col") * layers
    target = float(cells * size // 2)
    out, twice = go(
        functools.partial(last_c_body, target), outs=[out.shape, total], out_spaces=[hbm, vmem],
        spaces=[vmem, hbm] + [vmem] * (11 + len(every)), scratch=blocks(len(wanted("CNSD", layers))), aliases={1: 0},
    )(keep, out, C, T, down, D, yc, yn, ys, yd, yc_in, rs_in, g_in, *every)
    (out,) = go(
        last_e_body, outs=[out.shape], out_spaces=[hbm], spaces=[vmem, hbm] + [vmem] * 4,
        scratch=blocks(count["E"]), aliases={1: 0},
    )(keep, out, twice, down, ye, re_in)
    return out[None, None]


def solution(mesh):
    in_specs = (
        P("row", "col", None, None, None, None),
        P("row", "col", None, None),
        P("row", "col", None, None),
    )
    out_specs = P("row", "col", None, None, None, None)
    return jax.shard_map(shards, mesh=mesh, in_specs=in_specs, out_specs=out_specs, check_vma=False)
```

```python
import functools

import jax
import jax.numpy as jnp
from jax import lax
from jax.experimental import pallas as pl
from jax.experimental.pallas import tpu as pltpu
from jax.sharding import PartitionSpec as P


F32 = jnp.float32
BF16 = jnp.bfloat16
NN = ((1,), (0,))
NT = ((1,), (1,))
TN = ((0,), (0,))
IN_PLANE = {"C": (0, 0), "N": (0, 1), "S": (1, -1), "E": (1, 0), "D": (1, 1)}


def offset_list():
    steps = (-1, 0, 1)
    return [(i, j, k) for i in steps for j in steps for k in steps if (i, j, k) > (0, 0, 0)]


def slot_number(offset):
    return offset_list().index(offset) + 1


def panel_blocks(name, layers):
    side = IN_PLANE[name]
    found = []
    for low in range(layers):
        for high in range(layers):
            step = high - low
            if abs(step) <= 1 and (*side, step) > (0, 0, 0):
                found.append((low, high, slot_number((*side, step))))
    return found


def sym_rows(layers, size):
    blocks = layers * (layers - 1) // 2 + (layers + 1) // 2
    return -(-blocks // layers) * size + 8


def rows_cols(size):
    return (
        lax.broadcasted_iota(jnp.int32, (size, size), 0),
        lax.broadcasted_iota(jnp.int32, (size, size), 1),
    )


def block_slices(k, layers, size):
    row, col = k // layers * size, k % layers * size
    return slice(row, row + size), slice(col, col + size)


def sym_places(layers):
    above = [(a, b) for a in range(layers) for b in range(a + 1, layers)]
    pairs = list(range(0, layers, 2))
    return list(enumerate(above)), [(len(above) + k, k, a) for k, a in enumerate(pairs)]


def put_sym(ref, get, layers, size, first=0):
    row, col = rows_cols(size)
    above, pairs = sym_places(layers)
    last = first + sym_rows(layers, size) - 8

    def put(k, value):
        rows, cols = block_slices(k, layers, size)
        ref[first + rows.start : first + rows.stop, cols] = value

    ref[last : last + 8, :] = jnp.zeros((8, layers * size), F32)
    if len(above) + len(pairs) < (last - first) // size * layers:
        ref[last - size : last, :] = jnp.zeros((size, layers * size), F32)
    for k, (a, b) in above:
        put(k, get(a, b))
    for k, mark, a in pairs:
        block = get(a, a)
        if a + 1 < layers:
            other = get(a + 1, a + 1)
            line = jnp.sum(jnp.where(row == col, other, 0.0), axis=0, keepdims=True)
            ref[last : last + 8, mark * size : (mark + 1) * size] = jnp.broadcast_to(line, (8, size))
            block = jnp.where(row <= col, block, other)
        put(k, block)


def take_sym(packed, layers, size):
    row, col = rows_cols(size)
    above, pairs = sym_places(layers)
    last = sym_rows(layers, size) - 8
    blocks = {}
    for k, (a, b) in above:
        rows, cols = block_slices(k, layers, size)
        blocks[a, b] = packed[rows, cols]
    for k, mark, a in pairs:
        rows, cols = block_slices(k, layers, size)
        block = packed[rows, cols]
        if a + 1 < layers:
            flipped = block.T
            line = packed[last : last + 1, mark * size : (mark + 1) * size]
            blocks[a, a] = jnp.where(row <= col, block, flipped)
            blocks[a + 1, a + 1] = jnp.where(row == col, line, jnp.where(row < col, flipped, block))
        else:
            blocks[a, a] = block
    return blocks


def whole_sym(blocks, layers):
    rows = []
    for a in range(layers):
        rows.append(
            jnp.concatenate(
                [blocks[a, b] if a <= b else blocks[b, a].T for b in range(layers)], axis=1
            )
        )
    return jnp.concatenate(rows, axis=0)


def split(value):
    high = value.astype(BF16)
    return high, (value - high.astype(F32)).astype(BF16)


def dot3(a, b, dims):
    go = functools.partial(lax.dot_general, dimension_numbers=(dims, ((), ())), preferred_element_type=F32)
    return go(a[0], b[0]) + (go(a[0], b[1]) + go(a[1], b[0]))


def cut(pair, at, size):
    return tuple(part[at : at + size, :] for part in pair)


def sym_product(pair, layers, size, dims):
    blocks = {}
    for a in range(layers):
        if dims == NT:
            left = tuple(part[a * size : (a + 1) * size, :] for part in pair)
            right = tuple(part[a * size :, :] for part in pair)
        else:
            left = tuple(part[:, a * size : (a + 1) * size] for part in pair)
            right = tuple(part[:, a * size :] for part in pair)
        strip = dot3(left, right, dims)
        for b in range(a, layers):
            blocks[a, b] = strip[:, (b - a) * size : (b - a + 1) * size]
    return blocks


def kept(mask_ref, layer, slot):
    return mask_ref[layer, slot - 1] > 0


def start_panel(stored_ref, out_ref, sems, first, name, layers, size, top=0):
    copies = []
    for k, (low, high, slot) in enumerate(panel_blocks(name, layers)):
        place = out_ref.at[pl.ds(top + low * size, size), pl.ds(high * size, size)]
        copies.append(pltpu.make_async_copy(stored_ref.at[low, slot], place, sems.at[first + k]))
        copies[-1].start()
    return copies


def end_panel(copies, out_ref, name, layers, size, mask_ref, top=0):
    blocks = panel_blocks(name, layers)
    for low in range(layers):
        for high in range(layers):
            if (low, high) not in [block[:2] for block in blocks]:
                out_ref[top + low * size : top + (low + 1) * size, high * size : (high + 1) * size] = jnp.zeros((size, size), F32)
    for copy, (low, high, slot) in zip(copies, blocks, strict=True):
        copy.wait()

        @pl.when(jnp.logical_not(kept(mask_ref, low, slot)))
        def _(low=low, high=high):
            out_ref[top + low * size : top + (low + 1) * size, high * size : (high + 1) * size] = jnp.zeros((size, size), F32)


def start_loads(stored_ref, held, sems, wanted):
    copies = [
        pltpu.make_async_copy(stored_ref.at[low, slot], held.at[k], sems.at[k])
        for k, (low, slot) in enumerate(wanted)
    ]
    for copy in copies:
        copy.start()
    return copies


def lanes(value):
    return jnp.sum(value.reshape(-1, 8, value.shape[-1]), axis=0)


def squares_of(value):
    return lanes(value * value)


def wanted(names, layers):
    return [(layer, 0) for layer in range(layers) if "C" in names] + [
        (low, slot) for name in names for low, _, slot in panel_blocks(name, layers)
    ]


def pack_body(
    layers, size, mask_ref, stored_ref, onsite_ref, t_ref, down_ref, held, sems, mask, mask_sem, onsite, onsite_sem
):
    n = layers * size
    small = [
        pltpu.make_async_copy(mask_ref, mask, mask_sem),
        pltpu.make_async_copy(onsite_ref, onsite, onsite_sem),
    ]
    for copy in small:
        copy.start()
    copies = start_loads(stored_ref, held, sems, wanted("C", layers))
    panels = []
    at = len(copies)
    for name, ref, top in (("N", t_ref, 0), ("S", down_ref, 0), ("E", down_ref, n)):
        panels.append((start_panel(stored_ref, ref, sems, at, name, layers, size, top=top), ref, name, top))
        at += len(panels[-1][0])
    for copy in small:
        copy.wait()
    row, col = rows_cols(size)
    blocks = {}
    for layer in range(layers):
        copies[layer].wait()
        block = held[layer]
        blocks[layer, layer] = 0.5 * (block + block.T) + jnp.where(row == col, onsite[layer : layer + 1, :], 0.0)
    for k, (low, high, slot) in enumerate(panel_blocks("C", layers), start=layers):
        copies[k].wait()
        blocks[low, high] = jnp.where(kept(mask, low, slot), held[k], 0.0)
    put_sym(t_ref, lambda a, b: blocks.get((a, b), jnp.zeros((size, size), F32)), layers, size, first=n)
    for started, ref, name, top in panels:
        end_panel(started, ref, name, layers, size, mask, top=top)


def pack_d_body(layers, size, mask_ref, stored_ref, _, d_ref, up_ref, sems, mask, mask_sem):
    small = pltpu.make_async_copy(mask_ref, mask, mask_sem)
    small.start()
    copies = start_panel(stored_ref, d_ref, sems, 0, "D", layers, size)
    small.wait()
    end_panel(copies, d_ref, "D", layers, size, mask)
    blocks = sym_product(split(d_ref[...]), layers, size, TN)
    put_sym(up_ref, lambda a, b: blocks[a, b], layers, size)


def sums_body(layers, size, mask_ref, _, down_ref, t_ref, d_ref, packed_ref, c_ref, keep_ref, sums_ref):
    n = layers * size
    packed_ref[...] = t_ref[n:, :]
    c_ref[...] = whole_sym(take_sym(t_ref[n:, :], layers, size), layers)
    keep_ref[...] = jnp.zeros(keep_ref.shape, F32)
    slots = keep_ref.shape[0] // layers
    for low, slot in wanted(IN_PLANE, layers):
        here = 1.0 if slot == 0 else jnp.where(kept(mask_ref, low, slot), 1.0, 0.0)
        keep_ref[low * slots + slot : low * slots + slot + 1, :] = jnp.full((1, size), here, F32)
    row, col = rows_cols(size)
    trace = 0.0
    for layer in range(layers):
        here = slice(layer * size, (layer + 1) * size)
        trace = trace + lanes(jnp.where(row == col, c_ref[here, here], 0.0))
    sums_ref[:8, :] = trace
    squares = squares_of(c_ref[...])
    for ref in (down_ref.at[:n, :], down_ref.at[n:, :], t_ref.at[:n, :], d_ref):
        squares = squares + 2.0 * squares_of(ref[...])
    sums_ref[8:, :] = sum(squares[:, at * size : (at + 1) * size] for at in range(layers))


def local_g_body(layers, size, _, sums_ref, more_ref, t_ref, down_ref, d_ref, total_ref, g_ref, r_ref, yc_up_ref):
    n = layers * size
    total_ref[...] = sums_ref[...] + more_ref[...]
    n_now, e, d = split(t_ref[:n, :]), split(down_ref[n:, :]), split(d_ref[...])
    blocks = sym_product(e, layers, size, TN)
    g_ref[:n, :] = dot3(e, d, TN)
    put_sym(g_ref, lambda a, b: blocks[a, b], layers, size, first=n)
    r_ref[:n, :] = dot3(n_now, e, TN)
    r_ref[n:, :] = dot3(n_now, d, TN)
    blocks = sym_product(n_now, layers, size, TN)
    put_sym(yc_up_ref, lambda a, b: blocks[a, b], layers, size)


def local_y_body(
    layers, size, _, sums_ref, more_ref, c_ref, t_ref, down_ref, d_ref,
    total_ref, out_ref, yc_ref, yn_ref, ys_ref, ye_ref, yd_ref, zero, sems,
):
    total_ref[...] = sums_ref[...] + more_ref[...]
    zero[...] = jnp.zeros(zero.shape, F32)
    written = set(wanted(IN_PLANE, layers))
    copies = []
    for layer in range(layers):
        for slot in range(out_ref.shape[1]):
            if (layer, slot) not in written:
                copies.append(pltpu.make_async_copy(zero, out_ref.at[layer, slot], sems.at[len(copies)]))
                copies[-1].start()
    at = layers * size
    parts = (c_ref[...], t_ref[:at, :], down_ref[:at, :], down_ref[at:, :], d_ref[...])
    c, n, s, e, d = (split(part) for part in parts)
    yn_ref[...] = dot3(c, n, NN)
    ys_ref[...] = dot3(c, s, NN)
    ye_ref[...] = dot3(c, e, NN)
    yd_ref[...] = dot3(c, d, NN)
    terms = [
        sym_product(pair, layers, size, dims)
        for pair, dims in ((c, NT), (n, NT), (s, NT), (e, NT), (d, NT))
    ]
    put_sym(yc_ref, lambda a, b: sum(term[a, b] for term in terms), layers, size)
    for copy in copies:
        copy.wait()


def copy_body(layers, size, _, __, from_ref, to_ref):
    to_ref[...] = from_ref[...]


def yc_body(layers, size, _, __, from_ref, to_ref):
    tall = from_ref.shape[0]
    to_ref[:tall, :] = from_ref[...]
    to_ref[tall:, :] = jnp.zeros((8, layers * size), F32)


def g_body(layers, size, _, sums_ref, more_ref, g0_ref, below_ref, up_ref, total_ref, g_ref):
    n, last = layers * size, g_ref.shape[0] - 8
    parts = sums_ref[...] + more_ref[...]
    line = lax.broadcasted_iota(jnp.int32, total_ref.shape, 0)
    total = jnp.where(line % 4 == 0, jnp.sum(parts[:8, :]), jnp.sum(parts[8:, :]))
    total_ref[...] = total
    stu, eu = split(below_ref[:n, :].T), split(below_ref[n:, :])
    g_ref[:n, :] = g0_ref[:n, :] + dot3(stu, eu, NN)
    blocks = sym_product(stu, layers, size, NT)
    put_sym(g_ref, lambda a, b: blocks[a, b], layers, size, first=n)
    g_ref[n:, :] += g0_ref[n:, :] + up_ref[...]
    for at in range(layers):
        cols = slice(at * size, (at + 1) * size)
        g_ref[last:, cols] = jnp.where(line < 4, g_ref[last:, cols], total)


def early_body(layers, size, _, t_ref, e_ref, d_ref, below_ref, cu_ref, yn0_ref, ye0_ref, yd0_ref, yn_ref, ye_ref, yd_ref):
    at = layers * size
    n, e, d = split(t_ref[:at, :]), split(e_ref[at:, :]), split(d_ref[...])
    su, eu = split(below_ref[:at, :]), split(below_ref[at:, :])
    cu = split(whole_sym(take_sym(cu_ref, layers, size), layers))
    yn_ref[...] = yn0_ref[...] + dot3(e, su, NT) + dot3(d, eu, NT) + dot3(n, cu, NN)
    ye_ref[...] = ye0_ref[...] + dot3(n, su, NN)
    yd_ref[...] = yd0_ref[...] + dot3(n, eu, NN)


def r_body(layers, size, _, r0_ref, below_ref, tx_ref, rs_ref, re_ref):
    n = layers * size
    su, eu, nx = split(below_ref[:n, :]), split(below_ref[n:, :]), split(tx_ref[:n, :])
    cx = split(whole_sym(take_sym(tx_ref[n:, :], layers, size), layers))
    rs_ref[...] = r0_ref[:n, :] + dot3(su, cx, NN) + dot3(eu, nx, NT)
    re_ref[...] = r0_ref[n:, :] + dot3(su, nx, NN)


def hand_body(layers, size, _, __, tx_ref, cx_ref):
    cx_ref[...] = tx_ref[layers * size :, :]


def middle_body(layers, size, _, e_ref, d_ref, tx_ref, ye0_ref, yd0_ref, ye_ref, yd_ref):
    at = layers * size
    e, d, nx = split(e_ref[at:, :]), split(d_ref[...]), split(tx_ref[:at, :])
    cx = split(whole_sym(take_sym(tx_ref[at:, :], layers, size), layers))
    ye_ref[...] = ye0_ref[...] + dot3(e, cx, NN) + dot3(d, nx, NT)
    yd_ref[...] = yd0_ref[...] + dot3(e, nx, NN)


def middle_c_body(layers, size, _, sums_ref, d_ref, cxu_ref, yd0_ref, total_ref, yd_ref):
    total_ref[...] = sums_ref[...]
    cxu = split(whole_sym(take_sym(cxu_ref, layers, size), layers))
    yd_ref[...] = yd0_ref[...] + dot3(split(d_ref[...]), cxu, NN)


def twice_h(target, size, sums):
    t1, t2 = sums[0:1, :], sums[1:2, :]
    return 2.0 * jax.nn.sigmoid((jnp.abs(t2 - target) - jnp.abs(2.0 * t1 - t2 - target)) / size)


class Sender:
    def __init__(self, twice, keep_ref, out_ref, held, sems):
        self.twice, self.keep_ref, self.out_ref, self.held, self.sems = twice, keep_ref, out_ref, held, sems
        self.copies = []

    def send(self, y, a, low, slot):
        k, at = len(self.copies), low * self.out_ref.shape[1] + slot
        self.held[k] = self.keep_ref[at : at + 1, :] * (y + self.twice * (a - y))
        self.copies.append(pltpu.make_async_copy(self.held.at[k], self.out_ref.at[low, slot], self.sems.at[k]))
        self.copies[-1].start()

    def send_panel(self, name, a_ref, terms, layers, size):
        for low, high, slot in panel_blocks(name, layers):
            rows, cols = slice(low * size, (low + 1) * size), slice(high * size, (high + 1) * size)
            self.send(sum(ref[rows, cols] for ref in terms), a_ref[rows, cols], low, slot)

    def wait(self):
        for copy in self.copies:
            copy.wait()


def last_c_body(
    target, layers, size, keep_ref, _, c_ref, t_ref, e_ref, d_ref, yc_ref, yn_ref, ye_ref, yd_ref, yc_in_ref, re_ref, g_ref, *rest
):
    *sums_refs, out_ref, twice_ref, held, sems = rest
    n, last = layers * size, g_ref.shape[0] - 8
    line = lax.broadcasted_iota(jnp.int32, (8, size), 0)
    beside = g_ref[last:, :size]
    sums = jnp.where(line == 0, beside[4:5, :], beside[5:6, :])
    twice = twice_h(target, size, sum((ref[...] for ref in sums_refs), start=sums))
    twice_ref[...] = jnp.broadcast_to(twice, twice_ref.shape)
    sender = Sender(twice, keep_ref, out_ref, held, sems)
    sender.send_panel("D", d_ref, [yd_ref], layers, size)
    sender.send_panel("E", e_ref.at[n:, :], [ye_ref, re_ref], layers, size)
    sender.send_panel("N", t_ref, [yn_ref, g_ref], layers, size)
    blocks = take_sym(yc_ref[...] + yc_in_ref[: yc_ref.shape[0], :] + g_ref[n:, :], layers, size)
    for low, high, slot in panel_blocks("C", layers) + [(layer, layer, 0) for layer in range(layers)]:
        rows, cols = slice(low * size, (low + 1) * size), slice(high * size, (high + 1) * size)
        sender.send(blocks[low, high], c_ref[rows, cols], low, slot)
    sender.wait()


def last_s_body(layers, size, keep_ref, _, twice_ref, down_ref, ys_ref, rs_ref, out_ref, held, sems):
    sender = Sender(twice_ref[0:1, :], keep_ref, out_ref, held, sems)
    sender.send_panel("S", down_ref, [ys_ref, rs_ref], layers, size)
    sender.wait()


def call(body, layers, size, outs, spaces, scratch=(), limit=24, out_spaces=None, aliases=None):
    return pl.pallas_call(
        functools.partial(body, layers, size),
        out_shape=[jax.ShapeDtypeStruct(shape, F32) for shape in outs],
        in_specs=[pl.BlockSpec(memory_space=space) for space in spaces],
        out_specs=[pl.BlockSpec(memory_space=space) for space in out_spaces or [pltpu.VMEM] * len(outs)],
        scratch_shapes=list(scratch),
        input_output_aliases=aliases or {},
        compiler_params=pltpu.CompilerParams(vmem_limit_bytes=limit << 20),
    )


def passed_along(value, axis, by):
    peers = lax.axis_size(axis)
    return lax.ppermute(value, axis, [(i, (i + by) % peers) for i in range(peers)])


def swapped(value, axis, bit):
    peers = lax.axis_size(axis)
    return lax.ppermute(value, axis, [(i, i ^ bit) for i in range(peers)])


def shards(stored_blocks, onsite, bond_mask):
    stored, onsite, mask = stored_blocks[0, 0], onsite[0, 0], bond_mask[0, 0]
    layers, slots, size = stored.shape[:3]
    n, tall = layers * size, sym_rows(layers, size)
    panel, packed, sums, total = (n, n), (tall, n), (16, size), (8, size)
    vmem, smem, hbm = pltpu.VMEM, pltpu.SMEM, pltpu.HBM

    def blocks(count):
        return [pltpu.VMEM((count, size, size), F32), pltpu.SemaphoreType.DMA((count,))]

    go = functools.partial(call, layers=layers, size=size)
    stored, onsite, mask_hbm = (pltpu.with_memory_space_constraint(value, hbm) for value in (stored, onsite, mask))

    peers = lax.axis_size("col")
    bits = [1 << k for k in range(peers.bit_length() - 1)]
    bits = bits[:1] + bits[2:] + bits[1:2]

    def arriving(value):
        return swapped(value, "col", bits.pop(0)) if bits else jnp.zeros_like(value)

    small = [pltpu.SMEM(mask.shape, mask.dtype), pltpu.SemaphoreType.DMA]
    count = {name: len(wanted(name, layers)) for name in IN_PLANE}
    T, down = go(
        pack_body, outs=[(n + tall, n), (2 * n, n)], spaces=[hbm] * 3,
        scratch=[pltpu.VMEM((count["C"], size, size), F32), pltpu.SemaphoreType.DMA((len(wanted("CNSE", layers)),))]
        + small + [pltpu.VMEM(onsite.shape, F32), pltpu.SemaphoreType.DMA],
    )(mask_hbm, stored, onsite)
    T_x = passed_along(T, "row", -1)
    below = passed_along(down, "col", -1)
    D, gc = go(
        pack_d_body, outs=[panel, packed], spaces=[hbm] * 3, scratch=[pltpu.SemaphoreType.DMA((count["D"],))] + small
    )(mask_hbm, stored, T)
    gc_in = passed_along(gc, "col", 1)
    Cp, C, keep, own = go(sums_body, outs=[packed, panel, (layers * slots, size), sums], spaces=[smem, hbm] + [vmem] * 3)(
        mask, gc, down, T, D
    )
    if peers.bit_count() > 1:
        own = own + sum(passed_along(own, "col", by) for by in range(1, peers))
        bits = []
    while len(bits) > 3:
        own = own + arriving(own)
    more = arriving(own)
    own, g0, r0, yc_up = go(local_g_body, outs=[sums, (n + tall, n), (2 * n, n), packed], spaces=[hbm] + [vmem] * 5)(
        gc, own, more, T, down, D
    )
    more = arriving(own)
    own, out, yc, yn, ys, ye, yd = go(
        local_y_body, outs=[sums, (layers, slots, size, size), packed] + [panel] * 4, spaces=[hbm] + [vmem] * 6,
        out_spaces=[vmem, hbm] + [vmem] * 5, scratch=[pltpu.VMEM((size, size), F32), pltpu.SemaphoreType.DMA((layers * slots,))],
    )(g0, own, more, C, T, down, D)
    more = arriving(own)
    (yc_up,) = go(yc_body, outs=[(tall + 8, n)], spaces=[hbm] * 2 + [vmem])(yc, below, yc_up)
    yc_in = passed_along(yc_up, "col", 1)
    own, g = go(g_body, outs=[total, (n + tall, n)], spaces=[hbm] + [vmem] * 5)(yc_up, own, more, g0, below, gc_in)
    g_in = passed_along(g, "row", 1)
    Cp_u = passed_along(Cp, "col", -1)
    rs, re = go(r_body, outs=[panel, panel], spaces=[hbm] + [vmem] * 3)(g, r0, below, T_x)
    (rs,) = go(copy_body, outs=[panel], spaces=[hbm] * 2 + [vmem])(yc_in, re, rs)
    rs_in, re_in = passed_along(rs, "col", 1), passed_along(re, "col", 1)
    (Cp_x,) = go(hand_body, outs=[packed], spaces=[hbm] * 2 + [vmem])(rs, Cp_u, T_x)
    Cp_xu = passed_along(Cp_x, "col", -1)
    yn, ye, yd = go(early_body, outs=[panel] * 3, spaces=[hbm] + [vmem] * 8)(Cp_x, T, down, D, below, Cp_u, yn, ye, yd)
    ye, yd = go(middle_body, outs=[panel, panel], spaces=[hbm] + [vmem] * 5)(yn, down, D, T_x, ye, yd)
    own, yd = go(middle_c_body, outs=[total, panel], spaces=[hbm] + [vmem] * 4)(ye, own, D, Cp_xu, yd)
    every = [own] + [passed_along(own, "row", -by) for by in range(1, lax.axis_size("row") - 1)]
    cells = lax.axis_size("row") * lax.axis_size("col") * layers
    target = float(cells * size // 2)
    out, twice = go(
        functools.partial(last_c_body, target), outs=[out.shape, total], out_spaces=[hbm, vmem],
        spaces=[vmem, hbm] + [vmem] * (11 + len(every)), scratch=blocks(len(wanted("CNED", layers))), aliases={1: 0},
    )(keep, out, C, T, down, D, yc, yn, ye, yd, yc_in, re_in, g_in, *every)
    (out,) = go(
        last_s_body, outs=[out.shape], out_spaces=[hbm], spaces=[vmem, hbm] + [vmem] * 4,
        scratch=blocks(count["S"]), aliases={1: 0},
    )(keep, out, twice, down, ys, rs_in)
    return out[None, None]


def solution(mesh):
    in_specs = (
        P("row", "col", None, None, None, None),
        P("row", "col", None, None),
        P("row", "col", None, None),
    )
    out_specs = P("row", "col", None, None, None, None)
    return jax.shard_map(shards, mesh=mesh, in_specs=in_specs, out_specs=out_specs, check_vma=False)
```

```python
import functools

import jax
import jax.numpy as jnp
from jax import lax
from jax.experimental import pallas as pl
from jax.experimental.pallas import tpu as pltpu
from jax.sharding import PartitionSpec as P


F32 = jnp.float32
BF16 = jnp.bfloat16
NN = ((1,), (0,))
NT = ((1,), (1,))
TN = ((0,), (0,))
IN_PLANE = {"C": (0, 0), "N": (0, 1), "S": (1, -1), "E": (1, 0), "D": (1, 1)}


def offset_list():
    steps = (-1, 0, 1)
    return [(i, j, k) for i in steps for j in steps for k in steps if (i, j, k) > (0, 0, 0)]


def slot_number(offset):
    return offset_list().index(offset) + 1


def panel_blocks(name, layers):
    side = IN_PLANE[name]
    found = []
    for low in range(layers):
        for high in range(layers):
            step = high - low
            if abs(step) <= 1 and (*side, step) > (0, 0, 0):
                found.append((low, high, slot_number((*side, step))))
    return found


def sym_rows(layers, size):
    blocks = layers * (layers - 1) // 2 + (layers + 1) // 2
    return -(-blocks // layers) * size + 8


def rows_cols(size):
    return (
        lax.broadcasted_iota(jnp.int32, (size, size), 0),
        lax.broadcasted_iota(jnp.int32, (size, size), 1),
    )


def block_slices(k, layers, size):
    row, col = k // layers * size, k % layers * size
    return slice(row, row + size), slice(col, col + size)


def sym_places(layers):
    above = [(a, b) for a in range(layers) for b in range(a + 1, layers)]
    pairs = list(range(0, layers, 2))
    return list(enumerate(above)), [(len(above) + k, k, a) for k, a in enumerate(pairs)]


def put_sym(ref, get, layers, size, first=0):
    row, col = rows_cols(size)
    above, pairs = sym_places(layers)
    last = first + sym_rows(layers, size) - 8

    def put(k, value):
        rows, cols = block_slices(k, layers, size)
        ref[first + rows.start : first + rows.stop, cols] = value

    ref[last : last + 8, :] = jnp.zeros((8, layers * size), F32)
    if len(above) + len(pairs) < (last - first) // size * layers:
        ref[last - size : last, :] = jnp.zeros((size, layers * size), F32)
    for k, (a, b) in above:
        put(k, get(a, b))
    for k, mark, a in pairs:
        block = get(a, a)
        if a + 1 < layers:
            other = get(a + 1, a + 1)
            line = jnp.sum(jnp.where(row == col, other, 0.0), axis=0, keepdims=True)
            ref[last : last + 8, mark * size : (mark + 1) * size] = jnp.broadcast_to(line, (8, size))
            block = jnp.where(row <= col, block, other)
        put(k, block)


def take_sym(packed, layers, size):
    row, col = rows_cols(size)
    above, pairs = sym_places(layers)
    last = sym_rows(layers, size) - 8
    blocks = {}
    for k, (a, b) in above:
        rows, cols = block_slices(k, layers, size)
        blocks[a, b] = packed[rows, cols]
    for k, mark, a in pairs:
        rows, cols = block_slices(k, layers, size)
        block = packed[rows, cols]
        if a + 1 < layers:
            flipped = block.T
            line = packed[last : last + 1, mark * size : (mark + 1) * size]
            blocks[a, a] = jnp.where(row <= col, block, flipped)
            blocks[a + 1, a + 1] = jnp.where(row == col, line, jnp.where(row < col, flipped, block))
        else:
            blocks[a, a] = block
    return blocks


def whole_sym(blocks, layers):
    rows = []
    for a in range(layers):
        rows.append(
            jnp.concatenate(
                [blocks[a, b] if a <= b else blocks[b, a].T for b in range(layers)], axis=1
            )
        )
    return jnp.concatenate(rows, axis=0)


def split(value):
    high = value.astype(BF16)
    return high, (value - high.astype(F32)).astype(BF16)


def dot3(a, b, dims):
    go = functools.partial(lax.dot_general, dimension_numbers=(dims, ((), ())), preferred_element_type=F32)
    return go(a[0], b[0]) + (go(a[0], b[1]) + go(a[1], b[0]))


def cut(pair, at, size):
    return tuple(part[at : at + size, :] for part in pair)


def sym_product(pair, layers, size, dims):
    blocks = {}
    for a in range(layers):
        if dims == NT:
            left = tuple(part[a * size : (a + 1) * size, :] for part in pair)
            right = tuple(part[a * size :, :] for part in pair)
        else:
            left = tuple(part[:, a * size : (a + 1) * size] for part in pair)
            right = tuple(part[:, a * size :] for part in pair)
        strip = dot3(left, right, dims)
        for b in range(a, layers):
            blocks[a, b] = strip[:, (b - a) * size : (b - a + 1) * size]
    return blocks


def kept(mask_ref, layer, slot):
    return mask_ref[layer, slot - 1] > 0


def start_panel(stored_ref, out_ref, sems, first, name, layers, size, top=0):
    copies = []
    for k, (low, high, slot) in enumerate(panel_blocks(name, layers)):
        place = out_ref.at[pl.ds(top + low * size, size), pl.ds(high * size, size)]
        copies.append(pltpu.make_async_copy(stored_ref.at[low, slot], place, sems.at[first + k]))
        copies[-1].start()
    return copies


def end_panel(copies, out_ref, name, layers, size, mask_ref, top=0):
    blocks = panel_blocks(name, layers)
    for low in range(layers):
        for high in range(layers):
            if (low, high) not in [block[:2] for block in blocks]:
                out_ref[top + low * size : top + (low + 1) * size, high * size : (high + 1) * size] = jnp.zeros((size, size), F32)
    for copy, (low, high, slot) in zip(copies, blocks, strict=True):
        copy.wait()

        @pl.when(jnp.logical_not(kept(mask_ref, low, slot)))
        def _(low=low, high=high):
            out_ref[top + low * size : top + (low + 1) * size, high * size : (high + 1) * size] = jnp.zeros((size, size), F32)


def start_loads(stored_ref, held, sems, wanted):
    copies = [
        pltpu.make_async_copy(stored_ref.at[low, slot], held.at[k], sems.at[k])
        for k, (low, slot) in enumerate(wanted)
    ]
    for copy in copies:
        copy.start()
    return copies


def lanes(value):
    return jnp.sum(value.reshape(-1, 8, value.shape[-1]), axis=0)


def squares_of(value):
    return lanes(value * value)


def wanted(names, layers):
    return [(layer, 0) for layer in range(layers) if "C" in names] + [
        (low, slot) for name in names for low, _, slot in panel_blocks(name, layers)
    ]


def pack_body(
    layers, size, mask_ref, stored_ref, onsite_ref, t_ref, down_ref, held, sems, mask, mask_sem, onsite, onsite_sem
):
    n = layers * size
    small = [
        pltpu.make_async_copy(mask_ref, mask, mask_sem),
        pltpu.make_async_copy(onsite_ref, onsite, onsite_sem),
    ]
    for copy in small:
        copy.start()
    copies = start_loads(stored_ref, held, sems, wanted("C", layers))
    panels = []
    at = len(copies)
    for name, ref, top in (("N", t_ref, 0), ("S", down_ref, 0), ("E", down_ref, n)):
        panels.append((start_panel(stored_ref, ref, sems, at, name, layers, size, top=top), ref, name, top))
        at += len(panels[-1][0])
    for copy in small:
        copy.wait()
    row, col = rows_cols(size)
    blocks = {}
    for layer in range(layers):
        copies[layer].wait()
        block = held[layer]
        blocks[layer, layer] = 0.5 * (block + block.T) + jnp.where(row == col, onsite[layer : layer + 1, :], 0.0)
    for k, (low, high, slot) in enumerate(panel_blocks("C", layers), start=layers):
        copies[k].wait()
        blocks[low, high] = jnp.where(kept(mask, low, slot), held[k], 0.0)
    put_sym(t_ref, lambda a, b: blocks.get((a, b), jnp.zeros((size, size), F32)), layers, size, first=n)
    for started, ref, name, top in panels:
        end_panel(started, ref, name, layers, size, mask, top=top)


def pack_d_body(layers, size, mask_ref, stored_ref, _, d_ref, up_ref, sems, mask, mask_sem):
    small = pltpu.make_async_copy(mask_ref, mask, mask_sem)
    small.start()
    copies = start_panel(stored_ref, d_ref, sems, 0, "D", layers, size)
    small.wait()
    end_panel(copies, d_ref, "D", layers, size, mask)
    blocks = sym_product(split(d_ref[...]), layers, size, TN)
    put_sym(up_ref, lambda a, b: blocks[a, b], layers, size)


def sums_body(layers, size, mask_ref, _, down_ref, t_ref, d_ref, packed_ref, c_ref, keep_ref, sums_ref):
    n = layers * size
    packed_ref[...] = t_ref[n:, :]
    c_ref[...] = whole_sym(take_sym(t_ref[n:, :], layers, size), layers)
    keep_ref[...] = jnp.zeros(keep_ref.shape, F32)
    slots = keep_ref.shape[0] // layers
    for low, slot in wanted(IN_PLANE, layers):
        here = 1.0 if slot == 0 else jnp.where(kept(mask_ref, low, slot), 1.0, 0.0)
        keep_ref[low * slots + slot : low * slots + slot + 1, :] = jnp.full((1, size), here, F32)
    row, col = rows_cols(size)
    trace = 0.0
    for layer in range(layers):
        here = slice(layer * size, (layer + 1) * size)
        trace = trace + lanes(jnp.where(row == col, c_ref[here, here], 0.0))
    sums_ref[:8, :] = trace
    squares = squares_of(c_ref[...])
    for ref in (down_ref.at[:n, :], down_ref.at[n:, :], t_ref.at[:n, :], d_ref):
        squares = squares + 2.0 * squares_of(ref[...])
    sums_ref[8:, :] = sum(squares[:, at * size : (at + 1) * size] for at in range(layers))


def local_g_body(layers, size, _, sums_ref, more_ref, t_ref, down_ref, d_ref, total_ref, g_ref, r_ref, yc_up_ref):
    n = layers * size
    total_ref[...] = sums_ref[...] + more_ref[...]
    n_now, e, d = split(t_ref[:n, :]), split(down_ref[n:, :]), split(d_ref[...])
    blocks = sym_product(e, layers, size, TN)
    g_ref[:n, :] = dot3(e, d, TN)
    put_sym(g_ref, lambda a, b: blocks[a, b], layers, size, first=n)
    r_ref[:n, :] = dot3(n_now, e, TN)
    r_ref[n:, :] = dot3(n_now, d, TN)
    blocks = sym_product(n_now, layers, size, TN)
    put_sym(yc_up_ref, lambda a, b: blocks[a, b], layers, size)


def local_y_body(
    layers, size, _, sums_ref, more_ref, c_ref, t_ref, down_ref, d_ref,
    total_ref, out_ref, yc_ref, yn_ref, ys_ref, ye_ref, yd_ref, zero, sems,
):
    total_ref[...] = sums_ref[...] + more_ref[...]
    zero[...] = jnp.zeros(zero.shape, F32)
    written = set(wanted(IN_PLANE, layers))
    copies = []
    for layer in range(layers):
        for slot in range(out_ref.shape[1]):
            if (layer, slot) not in written:
                copies.append(pltpu.make_async_copy(zero, out_ref.at[layer, slot], sems.at[len(copies)]))
                copies[-1].start()
    at = layers * size
    parts = (c_ref[...], t_ref[:at, :], down_ref[:at, :], down_ref[at:, :], d_ref[...])
    c, n, s, e, d = (split(part) for part in parts)
    yn_ref[...] = dot3(c, n, NN)
    ys_ref[...] = dot3(c, s, NN)
    ye_ref[...] = dot3(c, e, NN)
    yd_ref[...] = dot3(c, d, NN)
    terms = [
        sym_product(pair, layers, size, dims)
        for pair, dims in ((c, NT), (n, NT), (s, NT), (e, NT), (d, NT))
    ]
    put_sym(yc_ref, lambda a, b: sum(term[a, b] for term in terms), layers, size)
    for copy in copies:
        copy.wait()


def copy_body(layers, size, _, __, from_ref, to_ref):
    to_ref[...] = from_ref[...]


def yc_body(layers, size, _, __, from_ref, to_ref):
    tall = from_ref.shape[0]
    to_ref[:tall, :] = from_ref[...]
    to_ref[tall:, :] = jnp.zeros((8, layers * size), F32)


def g_body(layers, size, _, sums_ref, more_ref, g0_ref, below_ref, up_ref, total_ref, g_ref):
    n, last = layers * size, g_ref.shape[0] - 8
    parts = sums_ref[...] + more_ref[...]
    line = lax.broadcasted_iota(jnp.int32, total_ref.shape, 0)
    total = jnp.where(line % 4 == 0, jnp.sum(parts[:8, :]), jnp.sum(parts[8:, :]))
    total_ref[...] = total
    stu, eu = split(below_ref[:n, :].T), split(below_ref[n:, :])
    g_ref[:n, :] = g0_ref[:n, :] + dot3(stu, eu, NN)
    blocks = sym_product(stu, layers, size, NT)
    put_sym(g_ref, lambda a, b: blocks[a, b], layers, size, first=n)
    g_ref[n:, :] += g0_ref[n:, :] + up_ref[...]
    for at in range(layers):
        cols = slice(at * size, (at + 1) * size)
        g_ref[last:, cols] = jnp.where(line < 4, g_ref[last:, cols], total)


def early_body(layers, size, _, t_ref, e_ref, d_ref, below_ref, cu_ref, yn0_ref, ye0_ref, yd0_ref, yn_ref, ye_ref, yd_ref):
    at = layers * size
    n, e, d = split(t_ref[:at, :]), split(e_ref[at:, :]), split(d_ref[...])
    su, eu = split(below_ref[:at, :]), split(below_ref[at:, :])
    cu = split(whole_sym(take_sym(cu_ref, layers, size), layers))
    yn_ref[...] = yn0_ref[...] + dot3(e, su, NT) + dot3(d, eu, NT) + dot3(n, cu, NN)
    ye_ref[...] = ye0_ref[...] + dot3(n, su, NN)
    yd_ref[...] = yd0_ref[...] + dot3(n, eu, NN)


def r_body(layers, size, _, r0_ref, below_ref, tx_ref, rs_ref, re_ref):
    n = layers * size
    su, eu, nx = split(below_ref[:n, :]), split(below_ref[n:, :]), split(tx_ref[:n, :])
    cx = split(whole_sym(take_sym(tx_ref[n:, :], layers, size), layers))
    rs_ref[...] = r0_ref[:n, :] + dot3(su, cx, NN) + dot3(eu, nx, NT)
    re_ref[...] = r0_ref[n:, :] + dot3(su, nx, NN)


def hand_body(layers, size, _, __, tx_ref, cx_ref):
    cx_ref[...] = tx_ref[layers * size :, :]


def middle_body(layers, size, _, e_ref, d_ref, tx_ref, ye0_ref, yd0_ref, ye_ref, yd_ref):
    at = layers * size
    e, d, nx = split(e_ref[at:, :]), split(d_ref[...]), split(tx_ref[:at, :])
    cx = split(whole_sym(take_sym(tx_ref[at:, :], layers, size), layers))
    ye_ref[...] = ye0_ref[...] + dot3(e, cx, NN) + dot3(d, nx, NT)
    yd_ref[...] = yd0_ref[...] + dot3(e, nx, NN)


def middle_c_body(layers, size, _, sums_ref, d_ref, cxu_ref, yd0_ref, total_ref, yd_ref):
    total_ref[...] = sums_ref[...]
    cxu = split(whole_sym(take_sym(cxu_ref, layers, size), layers))
    yd_ref[...] = yd0_ref[...] + dot3(split(d_ref[...]), cxu, NN)


def twice_h(target, size, sums):
    t1, t2 = sums[0:1, :], sums[1:2, :]
    return 2.0 * jax.nn.sigmoid((jnp.abs(t2 - target) - jnp.abs(2.0 * t1 - t2 - target)) / size)


class Sender:
    def __init__(self, twice, keep_ref, out_ref, held, sems):
        self.twice, self.keep_ref, self.out_ref, self.held, self.sems = twice, keep_ref, out_ref, held, sems
        self.copies = []

    def put(self, value, low, slot):
        k = len(self.copies)
        self.held[k] = value
        self.copies.append(pltpu.make_async_copy(self.held.at[k], self.out_ref.at[low, slot], self.sems.at[k]))
        self.copies[-1].start()

    def send(self, y, a, low, slot):
        at = low * self.out_ref.shape[1] + slot
        self.put(self.keep_ref[at : at + 1, :] * (y + self.twice * (a - y)), low, slot)

    def send_panel(self, name, a_ref, terms, layers, size):
        for low, high, slot in panel_blocks(name, layers):
            rows, cols = slice(low * size, (low + 1) * size), slice(high * size, (high + 1) * size)
            self.send(sum(ref[rows, cols] for ref in terms), a_ref[rows, cols], low, slot)

    def send_ready(self, name, y_ref, gap_ref, layers, size):
        for low, high, slot in panel_blocks(name, layers):
            rows, cols = slice(low * size, (low + 1) * size), slice(high * size, (high + 1) * size)
            self.put(y_ref[rows, cols] + self.twice * gap_ref[rows, cols], low, slot)

    def wait(self):
        for copy in self.copies:
            copy.wait()


def ready_body(layers, size, keep_ref, _, sums_ref, d_ref, e_ref, yd_ref, ye_ref, re_ref, total_ref, *outs):
    n, slots = layers * size, keep_ref.shape[0] // layers
    total_ref[...] = sums_ref[...]
    for name, a_ref, terms, y_out, gap_out in (
        ("D", d_ref, [yd_ref], *outs[:2]),
        ("E", e_ref.at[n:, :], [ye_ref, re_ref], *outs[2:]),
    ):
        for low, high, slot in panel_blocks(name, layers):
            rows, cols = slice(low * size, (low + 1) * size), slice(high * size, (high + 1) * size)
            at = low * slots + slot
            y = keep_ref[at : at + 1, :] * sum(ref[rows, cols] for ref in terms)
            y_out[rows, cols] = y
            gap_out[rows, cols] = a_ref[rows, cols] - y


def last_c_body(
    target, layers, size, keep_ref, _, c_ref, t_ref, yc_ref, yn_ref, yc_in_ref, g_ref, pd_ref, qd_ref, pe_ref, qe_ref, *rest
):
    *sums_refs, out_ref, twice_ref, held, sems = rest
    n, last = layers * size, g_ref.shape[0] - 8
    line = lax.broadcasted_iota(jnp.int32, (8, size), 0)
    beside = g_ref[last:, :size]
    sums = jnp.where(line == 0, beside[4:5, :], beside[5:6, :])
    twice = twice_h(target, size, sum((ref[...] for ref in sums_refs), start=sums))
    twice_ref[...] = jnp.broadcast_to(twice, twice_ref.shape)
    sender = Sender(twice, keep_ref, out_ref, held, sems)
    sender.send_ready("D", pd_ref, qd_ref, layers, size)
    sender.send_ready("E", pe_ref, qe_ref, layers, size)
    sender.send_panel("N", t_ref, [yn_ref, g_ref], layers, size)
    blocks = take_sym(yc_ref[...] + yc_in_ref[: yc_ref.shape[0], :] + g_ref[n:, :], layers, size)
    for low, high, slot in panel_blocks("C", layers) + [(layer, layer, 0) for layer in range(layers)]:
        rows, cols = slice(low * size, (low + 1) * size), slice(high * size, (high + 1) * size)
        sender.send(blocks[low, high], c_ref[rows, cols], low, slot)
    sender.wait()


def last_s_body(layers, size, keep_ref, _, twice_ref, down_ref, ys_ref, rs_ref, out_ref, held, sems):
    sender = Sender(twice_ref[0:1, :], keep_ref, out_ref, held, sems)
    sender.send_panel("S", down_ref, [ys_ref, rs_ref], layers, size)
    sender.wait()


def call(body, layers, size, outs, spaces, scratch=(), limit=24, out_spaces=None, aliases=None):
    return pl.pallas_call(
        functools.partial(body, layers, size),
        out_shape=[jax.ShapeDtypeStruct(shape, F32) for shape in outs],
        in_specs=[pl.BlockSpec(memory_space=space) for space in spaces],
        out_specs=[pl.BlockSpec(memory_space=space) for space in out_spaces or [pltpu.VMEM] * len(outs)],
        scratch_shapes=list(scratch),
        input_output_aliases=aliases or {},
        compiler_params=pltpu.CompilerParams(vmem_limit_bytes=limit << 20),
    )


def passed_along(value, axis, by):
    peers = lax.axis_size(axis)
    return lax.ppermute(value, axis, [(i, (i + by) % peers) for i in range(peers)])


def swapped(value, axis, bit):
    peers = lax.axis_size(axis)
    return lax.ppermute(value, axis, [(i, i ^ bit) for i in range(peers)])


def shards(stored_blocks, onsite, bond_mask):
    stored, onsite, mask = stored_blocks[0, 0], onsite[0, 0], bond_mask[0, 0]
    layers, slots, size = stored.shape[:3]
    n, tall = layers * size, sym_rows(layers, size)
    panel, packed, sums, total = (n, n), (tall, n), (16, size), (8, size)
    vmem, smem, hbm = pltpu.VMEM, pltpu.SMEM, pltpu.HBM

    def blocks(count):
        return [pltpu.VMEM((count, size, size), F32), pltpu.SemaphoreType.DMA((count,))]

    go = functools.partial(call, layers=layers, size=size)
    stored, onsite, mask_hbm = (pltpu.with_memory_space_constraint(value, hbm) for value in (stored, onsite, mask))

    peers = lax.axis_size("col")
    bits = [1 << k for k in range(peers.bit_length() - 1)]
    bits = bits[:1] + bits[2:] + bits[1:2]

    def arriving(value):
        return swapped(value, "col", bits.pop(0)) if bits else jnp.zeros_like(value)

    small = [pltpu.SMEM(mask.shape, mask.dtype), pltpu.SemaphoreType.DMA]
    count = {name: len(wanted(name, layers)) for name in IN_PLANE}
    T, down = go(
        pack_body, outs=[(n + tall, n), (2 * n, n)], spaces=[hbm] * 3,
        scratch=[pltpu.VMEM((count["C"], size, size), F32), pltpu.SemaphoreType.DMA((len(wanted("CNSE", layers)),))]
        + small + [pltpu.VMEM(onsite.shape, F32), pltpu.SemaphoreType.DMA],
    )(mask_hbm, stored, onsite)
    T_x = passed_along(T, "row", -1)
    below = passed_along(down, "col", -1)
    D, gc = go(
        pack_d_body, outs=[panel, packed], spaces=[hbm] * 3, scratch=[pltpu.SemaphoreType.DMA((count["D"],))] + small
    )(mask_hbm, stored, T)
    gc_in = passed_along(gc, "col", 1)
    Cp, C, keep, own = go(sums_body, outs=[packed, panel, (layers * slots, size), sums], spaces=[smem, hbm] + [vmem] * 3)(
        mask, gc, down, T, D
    )
    if peers.bit_count() > 1:
        own = own + sum(passed_along(own, "col", by) for by in range(1, peers))
        bits = []
    while len(bits) > 3:
        own = own + arriving(own)
    more = arriving(own)
    own, g0, r0, yc_up = go(local_g_body, outs=[sums, (n + tall, n), (2 * n, n), packed], spaces=[hbm] + [vmem] * 5)(
        gc, own, more, T, down, D
    )
    more = arriving(own)
    own, out, yc, yn, ys, ye, yd = go(
        local_y_body, outs=[sums, (layers, slots, size, size), packed] + [panel] * 4, spaces=[hbm] + [vmem] * 6,
        out_spaces=[vmem, hbm] + [vmem] * 5, scratch=[pltpu.VMEM((size, size), F32), pltpu.SemaphoreType.DMA((layers * slots,))],
    )(g0, own, more, C, T, down, D)
    more = arriving(own)
    (yc_up,) = go(yc_body, outs=[(tall + 8, n)], spaces=[hbm] * 2 + [vmem])(yc, below, yc_up)
    yc_in = passed_along(yc_up, "col", 1)
    own, g = go(g_body, outs=[total, (n + tall, n)], spaces=[hbm] + [vmem] * 5)(yc_up, own, more, g0, below, gc_in)
    g_in = passed_along(g, "row", 1)
    Cp_u = passed_along(Cp, "col", -1)
    rs, re = go(r_body, outs=[panel, panel], spaces=[hbm] + [vmem] * 3)(g, r0, below, T_x)
    (rs,) = go(copy_body, outs=[panel], spaces=[hbm] * 2 + [vmem])(yc_in, re, rs)
    rs_in, re_in = passed_along(rs, "col", 1), passed_along(re, "col", 1)
    (Cp_x,) = go(hand_body, outs=[packed], spaces=[hbm] * 2 + [vmem])(rs, Cp_u, T_x)
    Cp_xu = passed_along(Cp_x, "col", -1)
    yn, ye, yd = go(early_body, outs=[panel] * 3, spaces=[hbm] + [vmem] * 8)(Cp_x, T, down, D, below, Cp_u, yn, ye, yd)
    ye, yd = go(middle_body, outs=[panel, panel], spaces=[hbm] + [vmem] * 5)(yn, down, D, T_x, ye, yd)
    own, yd = go(middle_c_body, outs=[total, panel], spaces=[hbm] + [vmem] * 4)(ye, own, D, Cp_xu, yd)
    every = [own] + [passed_along(own, "row", -by) for by in range(1, lax.axis_size("row") - 1)]
    _, *ready = go(ready_body, outs=[total] + [panel] * 4, spaces=[vmem, hbm] + [vmem] * 6)(
        keep, yd, own, D, down, yd, ye, re_in
    )
    cells = lax.axis_size("row") * lax.axis_size("col") * layers
    target = float(cells * size // 2)
    out, twice = go(
        functools.partial(last_c_body, target), outs=[out.shape, total], out_spaces=[hbm, vmem],
        spaces=[vmem, hbm] + [vmem] * (10 + len(every)), scratch=blocks(len(wanted("CNED", layers))), aliases={1: 0},
    )(keep, out, C, T, yc, yn, yc_in, g_in, *ready, *every)
    (out,) = go(
        last_s_body, outs=[out.shape], out_spaces=[hbm], spaces=[vmem, hbm] + [vmem] * 4,
        scratch=blocks(count["S"]), aliases={1: 0},
    )(keep, out, twice, down, ys, rs_in)
    return out[None, None]


def solution(mesh):
    in_specs = (
        P("row", "col", None, None, None, None),
        P("row", "col", None, None),
        P("row", "col", None, None),
    )
    out_specs = P("row", "col", None, None, None, None)
    return jax.shard_map(shards, mesh=mesh, in_specs=in_specs, out_specs=out_specs, check_vma=False)
```

```python
import functools

import jax
import jax.numpy as jnp
from jax import lax
from jax.experimental import pallas as pl
from jax.experimental.pallas import tpu as pltpu
from jax.sharding import PartitionSpec as P


F32 = jnp.float32
BF16 = jnp.bfloat16
NN = ((1,), (0,))
NT = ((1,), (1,))
TN = ((0,), (0,))
IN_PLANE = {"C": (0, 0), "N": (0, 1), "S": (1, -1), "E": (1, 0), "D": (1, 1)}


def offset_list():
    steps = (-1, 0, 1)
    return [(i, j, k) for i in steps for j in steps for k in steps if (i, j, k) > (0, 0, 0)]


def slot_number(offset):
    return offset_list().index(offset) + 1


def panel_blocks(name, layers):
    side = IN_PLANE[name]
    found = []
    for low in range(layers):
        for high in range(layers):
            step = high - low
            if abs(step) <= 1 and (*side, step) > (0, 0, 0):
                found.append((low, high, slot_number((*side, step))))
    return found


def sym_rows(layers, size):
    blocks = layers * (layers - 1) // 2 + (layers + 1) // 2
    return -(-blocks // layers) * size + 8


def rows_cols(size):
    return (
        lax.broadcasted_iota(jnp.int32, (size, size), 0),
        lax.broadcasted_iota(jnp.int32, (size, size), 1),
    )


def block_slices(k, layers, size):
    row, col = k // layers * size, k % layers * size
    return slice(row, row + size), slice(col, col + size)


def sym_places(layers):
    above = [(a, b) for a in range(layers) for b in range(a + 1, layers)]
    pairs = list(range(0, layers, 2))
    return list(enumerate(above)), [(len(above) + k, k, a) for k, a in enumerate(pairs)]


def put_sym(ref, get, layers, size, first=0):
    row, col = rows_cols(size)
    above, pairs = sym_places(layers)
    last = first + sym_rows(layers, size) - 8

    def put(k, value):
        rows, cols = block_slices(k, layers, size)
        ref[first + rows.start : first + rows.stop, cols] = value

    ref[last : last + 8, :] = jnp.zeros((8, layers * size), F32)
    if len(above) + len(pairs) < (last - first) // size * layers:
        ref[last - size : last, :] = jnp.zeros((size, layers * size), F32)
    for k, (a, b) in above:
        put(k, get(a, b))
    for k, mark, a in pairs:
        block = get(a, a)
        if a + 1 < layers:
            other = get(a + 1, a + 1)
            line = jnp.sum(jnp.where(row == col, other, 0.0), axis=0, keepdims=True)
            ref[last : last + 8, mark * size : (mark + 1) * size] = jnp.broadcast_to(line, (8, size))
            block = jnp.where(row <= col, block, other)
        put(k, block)


def take_sym(packed, layers, size):
    row, col = rows_cols(size)
    above, pairs = sym_places(layers)
    last = sym_rows(layers, size) - 8
    blocks = {}
    for k, (a, b) in above:
        rows, cols = block_slices(k, layers, size)
        blocks[a, b] = packed[rows, cols]
    for k, mark, a in pairs:
        rows, cols = block_slices(k, layers, size)
        block = packed[rows, cols]
        if a + 1 < layers:
            flipped = block.T
            line = packed[last : last + 1, mark * size : (mark + 1) * size]
            blocks[a, a] = jnp.where(row <= col, block, flipped)
            blocks[a + 1, a + 1] = jnp.where(row == col, line, jnp.where(row < col, flipped, block))
        else:
            blocks[a, a] = block
    return blocks


def whole_sym(blocks, layers):
    rows = []
    for a in range(layers):
        rows.append(
            jnp.concatenate(
                [blocks[a, b] if a <= b else blocks[b, a].T for b in range(layers)], axis=1
            )
        )
    return jnp.concatenate(rows, axis=0)


def split(value):
    high = value.astype(BF16)
    return high, (value - high.astype(F32)).astype(BF16)


def dot3(a, b, dims):
    go = functools.partial(lax.dot_general, dimension_numbers=(dims, ((), ())), preferred_element_type=F32)
    return go(a[0], b[0]) + (go(a[0], b[1]) + go(a[1], b[0]))


def cut(pair, at, size):
    return tuple(part[at : at + size, :] for part in pair)


def sym_product(pair, layers, size, dims):
    blocks = {}
    for a in range(layers):
        if dims == NT:
            left = tuple(part[a * size : (a + 1) * size, :] for part in pair)
            right = tuple(part[a * size :, :] for part in pair)
        else:
            left = tuple(part[:, a * size : (a + 1) * size] for part in pair)
            right = tuple(part[:, a * size :] for part in pair)
        strip = dot3(left, right, dims)
        for b in range(a, layers):
            blocks[a, b] = strip[:, (b - a) * size : (b - a + 1) * size]
    return blocks


def kept(mask_ref, layer, slot):
    return mask_ref[layer, slot - 1] > 0


def start_panel(stored_ref, out_ref, sems, first, name, layers, size, top=0):
    copies = []
    for k, (low, high, slot) in enumerate(panel_blocks(name, layers)):
        place = out_ref.at[pl.ds(top + low * size, size), pl.ds(high * size, size)]
        copies.append(pltpu.make_async_copy(stored_ref.at[low, slot], place, sems.at[first + k]))
        copies[-1].start()
    return copies


def end_panel(copies, out_ref, name, layers, size, mask_ref, top=0):
    blocks = panel_blocks(name, layers)
    for low in range(layers):
        for high in range(layers):
            if (low, high) not in [block[:2] for block in blocks]:
                out_ref[top + low * size : top + (low + 1) * size, high * size : (high + 1) * size] = jnp.zeros((size, size), F32)
    for copy, (low, high, slot) in zip(copies, blocks, strict=True):
        copy.wait()

        @pl.when(jnp.logical_not(kept(mask_ref, low, slot)))
        def _(low=low, high=high):
            out_ref[top + low * size : top + (low + 1) * size, high * size : (high + 1) * size] = jnp.zeros((size, size), F32)


def start_loads(stored_ref, held, sems, wanted):
    copies = [
        pltpu.make_async_copy(stored_ref.at[low, slot], held.at[k], sems.at[k])
        for k, (low, slot) in enumerate(wanted)
    ]
    for copy in copies:
        copy.start()
    return copies


def lanes(value):
    return jnp.sum(value.reshape(-1, 8, value.shape[-1]), axis=0)


def squares_of(value):
    return lanes(value * value)


def wanted(names, layers):
    return [(layer, 0) for layer in range(layers) if "C" in names] + [
        (low, slot) for name in names for low, _, slot in panel_blocks(name, layers)
    ]


def pack_body(
    layers, size, mask_ref, stored_ref, onsite_ref, t_ref, down_ref, held, sems, mask, mask_sem, onsite, onsite_sem
):
    n = layers * size
    small = [
        pltpu.make_async_copy(mask_ref, mask, mask_sem),
        pltpu.make_async_copy(onsite_ref, onsite, onsite_sem),
    ]
    for copy in small:
        copy.start()
    copies = start_loads(stored_ref, held, sems, wanted("C", layers))
    panels = []
    at = len(copies)
    for name, ref, top in (("N", t_ref, 0), ("S", down_ref, 0), ("E", down_ref, n)):
        panels.append((start_panel(stored_ref, ref, sems, at, name, layers, size, top=top), ref, name, top))
        at += len(panels[-1][0])
    for copy in small:
        copy.wait()
    row, col = rows_cols(size)
    blocks = {}
    for layer in range(layers):
        copies[layer].wait()
        block = held[layer]
        blocks[layer, layer] = 0.5 * (block + block.T) + jnp.where(row == col, onsite[layer : layer + 1, :], 0.0)
    for k, (low, high, slot) in enumerate(panel_blocks("C", layers), start=layers):
        copies[k].wait()
        blocks[low, high] = jnp.where(kept(mask, low, slot), held[k], 0.0)
    put_sym(t_ref, lambda a, b: blocks.get((a, b), jnp.zeros((size, size), F32)), layers, size, first=n)
    for started, ref, name, top in panels:
        end_panel(started, ref, name, layers, size, mask, top=top)


def pack_d_body(layers, size, mask_ref, stored_ref, _, d_ref, up_ref, sems, mask, mask_sem):
    small = pltpu.make_async_copy(mask_ref, mask, mask_sem)
    small.start()
    copies = start_panel(stored_ref, d_ref, sems, 0, "D", layers, size)
    small.wait()
    end_panel(copies, d_ref, "D", layers, size, mask)
    blocks = sym_product(split(d_ref[...]), layers, size, TN)
    put_sym(up_ref, lambda a, b: blocks[a, b], layers, size)


def sums_body(layers, size, mask_ref, _, down_ref, t_ref, d_ref, packed_ref, c_ref, keep_ref, sums_ref):
    n = layers * size
    packed_ref[...] = t_ref[n:, :]
    c_ref[...] = whole_sym(take_sym(t_ref[n:, :], layers, size), layers)
    keep_ref[...] = jnp.zeros(keep_ref.shape, F32)
    slots = keep_ref.shape[0] // layers
    for low, slot in wanted(IN_PLANE, layers):
        here = 1.0 if slot == 0 else jnp.where(kept(mask_ref, low, slot), 1.0, 0.0)
        keep_ref[low * slots + slot : low * slots + slot + 1, :] = jnp.full((1, size), here, F32)
    row, col = rows_cols(size)
    trace = 0.0
    for layer in range(layers):
        here = slice(layer * size, (layer + 1) * size)
        trace = trace + lanes(jnp.where(row == col, c_ref[here, here], 0.0))
    sums_ref[:8, :] = trace
    squares = squares_of(c_ref[...])
    for ref in (down_ref.at[:n, :], down_ref.at[n:, :], t_ref.at[:n, :], d_ref):
        squares = squares + 2.0 * squares_of(ref[...])
    sums_ref[8:, :] = sum(squares[:, at * size : (at + 1) * size] for at in range(layers))


def local_g_body(layers, size, _, sums_ref, more_ref, t_ref, down_ref, d_ref, total_ref, g_ref, r_ref, yc_up_ref):
    n = layers * size
    total_ref[...] = sums_ref[...] + more_ref[...]
    n_now, e, d = split(t_ref[:n, :]), split(down_ref[n:, :]), split(d_ref[...])
    blocks = sym_product(e, layers, size, TN)
    g_ref[:n, :] = dot3(e, d, TN)
    put_sym(g_ref, lambda a, b: blocks[a, b], layers, size, first=n)
    r_ref[:n, :] = dot3(n_now, e, TN)
    r_ref[n:, :] = dot3(n_now, d, TN)
    blocks = sym_product(n_now, layers, size, TN)
    put_sym(yc_up_ref, lambda a, b: blocks[a, b], layers, size)


def local_y_body(
    layers, size, _, sums_ref, more_ref, c_ref, t_ref, down_ref, d_ref,
    total_ref, out_ref, yc_ref, yn_ref, ys_ref, ye_ref, yd_ref, zero, sems,
):
    total_ref[...] = sums_ref[...] + more_ref[...]
    zero[...] = jnp.zeros(zero.shape, F32)
    written = set(wanted(IN_PLANE, layers))
    copies = []
    for layer in range(layers):
        for slot in range(out_ref.shape[1]):
            if (layer, slot) not in written:
                copies.append(pltpu.make_async_copy(zero, out_ref.at[layer, slot], sems.at[len(copies)]))
                copies[-1].start()
    at = layers * size
    parts = (c_ref[...], t_ref[:at, :], down_ref[:at, :], down_ref[at:, :], d_ref[...])
    c, n, s, e, d = (split(part) for part in parts)
    yn_ref[...] = dot3(c, n, NN)
    ys_ref[...] = dot3(c, s, NN)
    ye_ref[...] = dot3(c, e, NN)
    yd_ref[...] = dot3(c, d, NN)
    terms = [
        sym_product(pair, layers, size, dims)
        for pair, dims in ((c, NT), (n, NT), (s, NT), (e, NT), (d, NT))
    ]
    put_sym(yc_ref, lambda a, b: sum(term[a, b] for term in terms), layers, size)
    for copy in copies:
        copy.wait()


def copy_body(layers, size, _, __, from_ref, to_ref):
    to_ref[...] = from_ref[...]


def yc_body(layers, size, _, __, from_ref, to_ref):
    tall = from_ref.shape[0]
    to_ref[:tall, :] = from_ref[...]
    to_ref[tall:, :] = jnp.zeros((8, layers * size), F32)


def g_body(layers, size, _, sums_ref, more_ref, g0_ref, below_ref, up_ref, total_ref, g_ref):
    n, last = layers * size, g_ref.shape[0] - 8
    parts = sums_ref[...] + more_ref[...]
    line = lax.broadcasted_iota(jnp.int32, total_ref.shape, 0)
    total = jnp.where(line % 4 == 0, jnp.sum(parts[:8, :]), jnp.sum(parts[8:, :]))
    total_ref[...] = total
    stu, eu = split(below_ref[:n, :].T), split(below_ref[n:, :])
    g_ref[:n, :] = g0_ref[:n, :] + dot3(stu, eu, NN)
    blocks = sym_product(stu, layers, size, NT)
    put_sym(g_ref, lambda a, b: blocks[a, b], layers, size, first=n)
    g_ref[n:, :] += g0_ref[n:, :] + up_ref[...]
    for at in range(layers):
        cols = slice(at * size, (at + 1) * size)
        g_ref[last:, cols] = jnp.where(line < 4, g_ref[last:, cols], total)


def early_body(layers, size, _, t_ref, e_ref, d_ref, below_ref, cu_ref, yn0_ref, ye0_ref, yd0_ref, yn_ref, ye_ref, yd_ref):
    at = layers * size
    n, e, d = split(t_ref[:at, :]), split(e_ref[at:, :]), split(d_ref[...])
    su, eu = split(below_ref[:at, :]), split(below_ref[at:, :])
    cu = split(whole_sym(take_sym(cu_ref, layers, size), layers))
    yn_ref[...] = yn0_ref[...] + dot3(e, su, NT) + dot3(d, eu, NT) + dot3(n, cu, NN)
    ye_ref[...] = ye0_ref[...] + dot3(n, su, NN)
    yd_ref[...] = yd0_ref[...] + dot3(n, eu, NN)


def r_e_body(layers, size, _, r0_ref, below_ref, tx_ref, re_ref):
    n = layers * size
    su, nx = split(below_ref[:n, :]), split(tx_ref[:n, :])
    re_ref[...] = r0_ref[n:, :] + dot3(su, nx, NN)


def r_s_body(layers, size, _, r0_ref, below_ref, tx_ref, rs_ref):
    n = layers * size
    su, eu, nx = split(below_ref[:n, :]), split(below_ref[n:, :]), split(tx_ref[:n, :])
    cx = split(whole_sym(take_sym(tx_ref[n:, :], layers, size), layers))
    rs_ref[...] = r0_ref[:n, :] + dot3(su, cx, NN) + dot3(eu, nx, NT)


def hand_body(layers, size, _, __, tx_ref, cx_ref):
    cx_ref[...] = tx_ref[layers * size :, :]


def middle_body(layers, size, _, e_ref, d_ref, tx_ref, ye0_ref, yd0_ref, ye_ref, yd_ref):
    at = layers * size
    e, d, nx = split(e_ref[at:, :]), split(d_ref[...]), split(tx_ref[:at, :])
    cx = split(whole_sym(take_sym(tx_ref[at:, :], layers, size), layers))
    ye_ref[...] = ye0_ref[...] + dot3(e, cx, NN) + dot3(d, nx, NT)
    yd_ref[...] = yd0_ref[...] + dot3(e, nx, NN)


def middle_c_body(layers, size, _, sums_ref, d_ref, cxu_ref, yd0_ref, total_ref, yd_ref):
    total_ref[...] = sums_ref[...]
    cxu = split(whole_sym(take_sym(cxu_ref, layers, size), layers))
    yd_ref[...] = yd0_ref[...] + dot3(split(d_ref[...]), cxu, NN)


def twice_h(target, size, sums):
    t1, t2 = sums[0:1, :], sums[1:2, :]
    return 2.0 * jax.nn.sigmoid((jnp.abs(t2 - target) - jnp.abs(2.0 * t1 - t2 - target)) / size)


class Sender:
    def __init__(self, twice, keep_ref, out_ref, held, sems):
        self.twice, self.keep_ref, self.out_ref, self.held, self.sems = twice, keep_ref, out_ref, held, sems
        self.copies, self.used = [], 0

    def put(self, values, low, slot):
        first = self.used
        for value in values:
            self.held[self.used] = value
            self.used += 1
        here = self.held.at[pl.ds(first, len(values))]
        there = self.out_ref.at[low, pl.ds(slot, len(values))]
        self.copies.append(pltpu.make_async_copy(here, there, self.sems.at[first]))
        self.copies[-1].start()

    def mixed(self, y, a, low, slot):
        at = low * self.out_ref.shape[1] + slot
        return self.keep_ref[at : at + 1, :] * (y + self.twice * (a - y))

    def send_rows(self, name, layers, make):
        for layer in range(layers):
            run = [block for block in panel_blocks(name, layers) if block[0] == layer]
            self.put([make(*block) for block in run], layer, run[0][2])

    def send_panel(self, name, a_ref, terms, layers, size):
        def make(low, high, slot):
            rows, cols = slice(low * size, (low + 1) * size), slice(high * size, (high + 1) * size)
            return self.mixed(sum(ref[rows, cols] for ref in terms), a_ref[rows, cols], low, slot)

        self.send_rows(name, layers, make)

    def send_ready(self, name, y_ref, gap_ref, layers, size):
        def make(low, high, slot):
            rows, cols = slice(low * size, (low + 1) * size), slice(high * size, (high + 1) * size)
            return y_ref[rows, cols] + self.twice * gap_ref[rows, cols]

        self.send_rows(name, layers, make)

    def wait(self):
        for copy in self.copies:
            copy.wait()


def ready_body(layers, size, keep_ref, _, sums_ref, d_ref, e_ref, yd_ref, ye_ref, re_ref, total_ref, *outs):
    n, slots = layers * size, keep_ref.shape[0] // layers
    total_ref[...] = sums_ref[...]
    for name, a_ref, terms, y_out, gap_out in (
        ("D", d_ref, [yd_ref], *outs[:2]),
        ("E", e_ref.at[n:, :], [ye_ref, re_ref], *outs[2:]),
    ):
        for low, high, slot in panel_blocks(name, layers):
            rows, cols = slice(low * size, (low + 1) * size), slice(high * size, (high + 1) * size)
            at = low * slots + slot
            y = keep_ref[at : at + 1, :] * sum(ref[rows, cols] for ref in terms)
            y_out[rows, cols] = y
            gap_out[rows, cols] = a_ref[rows, cols] - y


def last_c_body(
    target, layers, size, keep_ref, _, c_ref, t_ref, yc_ref, yn_ref, yc_in_ref, g_ref, pd_ref, qd_ref, pe_ref, qe_ref, *rest
):
    *sums_refs, out_ref, twice_ref, held, sems = rest
    n, last = layers * size, g_ref.shape[0] - 8
    line = lax.broadcasted_iota(jnp.int32, (8, size), 0)
    beside = g_ref[last:, :size]
    sums = jnp.where(line == 0, beside[4:5, :], beside[5:6, :])
    twice = twice_h(target, size, sum((ref[...] for ref in sums_refs), start=sums))
    twice_ref[...] = jnp.broadcast_to(twice, twice_ref.shape)
    sender = Sender(twice, keep_ref, out_ref, held, sems)
    sender.send_ready("D", pd_ref, qd_ref, layers, size)
    sender.send_ready("E", pe_ref, qe_ref, layers, size)
    sender.send_panel("N", t_ref, [yn_ref, g_ref], layers, size)
    blocks = take_sym(yc_ref[...] + yc_in_ref[: yc_ref.shape[0], :] + g_ref[n:, :], layers, size)
    for layer in range(layers):
        values = []
        for low, high, slot in [(layer, layer, 0)] + [block for block in panel_blocks("C", layers) if block[0] == layer]:
            rows, cols = slice(low * size, (low + 1) * size), slice(high * size, (high + 1) * size)
            values.append(sender.mixed(blocks[low, high], c_ref[rows, cols], low, slot))
        sender.put(values, layer, 0)
    sender.wait()


def last_s_body(layers, size, keep_ref, _, twice_ref, down_ref, ys_ref, rs_ref, out_ref, held, sems):
    sender = Sender(twice_ref[0:1, :], keep_ref, out_ref, held, sems)
    sender.send_panel("S", down_ref, [ys_ref, rs_ref], layers, size)
    sender.wait()


def call(body, layers, size, outs, spaces, scratch=(), limit=24, out_spaces=None, aliases=None):
    return pl.pallas_call(
        functools.partial(body, layers, size),
        out_shape=[jax.ShapeDtypeStruct(shape, F32) for shape in outs],
        in_specs=[pl.BlockSpec(memory_space=space) for space in spaces],
        out_specs=[pl.BlockSpec(memory_space=space) for space in out_spaces or [pltpu.VMEM] * len(outs)],
        scratch_shapes=list(scratch),
        input_output_aliases=aliases or {},
        compiler_params=pltpu.CompilerParams(vmem_limit_bytes=limit << 20),
    )


def passed_along(value, axis, by):
    peers = lax.axis_size(axis)
    return lax.ppermute(value, axis, [(i, (i + by) % peers) for i in range(peers)])


def swapped(value, axis, bit):
    peers = lax.axis_size(axis)
    return lax.ppermute(value, axis, [(i, i ^ bit) for i in range(peers)])


def shards(stored_blocks, onsite, bond_mask):
    stored, onsite, mask = stored_blocks[0, 0], onsite[0, 0], bond_mask[0, 0]
    layers, slots, size = stored.shape[:3]
    n, tall = layers * size, sym_rows(layers, size)
    panel, packed, sums, total = (n, n), (tall, n), (16, size), (8, size)
    vmem, smem, hbm = pltpu.VMEM, pltpu.SMEM, pltpu.HBM

    def blocks(count):
        return [pltpu.VMEM((count, size, size), F32), pltpu.SemaphoreType.DMA((count,))]

    go = functools.partial(call, layers=layers, size=size)
    stored, onsite, mask_hbm = (pltpu.with_memory_space_constraint(value, hbm) for value in (stored, onsite, mask))

    peers = lax.axis_size("col")
    bits = [1 << k for k in range(peers.bit_length() - 1)]
    bits = bits[:1] + bits[2:] + bits[1:2]

    def arriving(value):
        return swapped(value, "col", bits.pop(0)) if bits else jnp.zeros_like(value)

    small = [pltpu.SMEM(mask.shape, mask.dtype), pltpu.SemaphoreType.DMA]
    count = {name: len(wanted(name, layers)) for name in IN_PLANE}
    T, down = go(
        pack_body, outs=[(n + tall, n), (2 * n, n)], spaces=[hbm] * 3,
        scratch=[pltpu.VMEM((count["C"], size, size), F32), pltpu.SemaphoreType.DMA((len(wanted("CNSE", layers)),))]
        + small + [pltpu.VMEM(onsite.shape, F32), pltpu.SemaphoreType.DMA],
    )(mask_hbm, stored, onsite)
    T_x = passed_along(T, "row", -1)
    below = passed_along(down, "col", -1)
    D, gc = go(
        pack_d_body, outs=[panel, packed], spaces=[hbm] * 3, scratch=[pltpu.SemaphoreType.DMA((count["D"],))] + small
    )(mask_hbm, stored, T)
    gc_in = passed_along(gc, "col", 1)
    Cp, C, keep, own = go(sums_body, outs=[packed, panel, (layers * slots, size), sums], spaces=[smem, hbm] + [vmem] * 3)(
        mask, gc, down, T, D
    )
    if peers.bit_count() > 1:
        own = own + sum(passed_along(own, "col", by) for by in range(1, peers))
        bits = []
    while len(bits) > 3:
        own = own + arriving(own)
    more = arriving(own)
    own, g0, r0, yc_up = go(local_g_body, outs=[sums, (n + tall, n), (2 * n, n), packed], spaces=[hbm] + [vmem] * 5)(
        gc, own, more, T, down, D
    )
    more = arriving(own)
    own, out, yc, yn, ys, ye, yd = go(
        local_y_body, outs=[sums, (layers, slots, size, size), packed] + [panel] * 4, spaces=[hbm] + [vmem] * 6,
        out_spaces=[vmem, hbm] + [vmem] * 5, scratch=[pltpu.VMEM((size, size), F32), pltpu.SemaphoreType.DMA((layers * slots,))],
    )(g0, own, more, C, T, down, D)
    more = arriving(own)
    (yc_up,) = go(yc_body, outs=[(tall + 8, n)], spaces=[hbm] * 2 + [vmem])(yc, below, yc_up)
    yc_in = passed_along(yc_up, "col", 1)
    own, g = go(g_body, outs=[total, (n + tall, n)], spaces=[hbm] + [vmem] * 5)(yc_up, own, more, g0, below, gc_in)
    g_in = passed_along(g, "row", 1)
    Cp_u = passed_along(Cp, "col", -1)
    (re,) = go(r_e_body, outs=[panel], spaces=[hbm] + [vmem] * 3)(g, r0, below, T_x)
    (rs,) = go(r_s_body, outs=[panel], spaces=[hbm] + [vmem] * 3)(re, r0, below, T_x)
    (rs,) = go(copy_body, outs=[panel], spaces=[hbm] * 2 + [vmem])(yc_in, re, rs)
    rs_in, re_in = passed_along(rs, "col", 1), passed_along(re, "col", 1)
    (Cp_x,) = go(hand_body, outs=[packed], spaces=[hbm] * 2 + [vmem])(rs, Cp_u, T_x)
    Cp_xu = passed_along(Cp_x, "col", -1)
    yn, ye, yd = go(early_body, outs=[panel] * 3, spaces=[hbm] + [vmem] * 8)(Cp_x, T, down, D, below, Cp_u, yn, ye, yd)
    ye, yd = go(middle_body, outs=[panel, panel], spaces=[hbm] + [vmem] * 5)(yn, down, D, T_x, ye, yd)
    own, yd = go(middle_c_body, outs=[total, panel], spaces=[hbm] + [vmem] * 4)(ye, own, D, Cp_xu, yd)
    every = [own] + [passed_along(own, "row", -by) for by in range(1, lax.axis_size("row") - 1)]
    _, *ready = go(ready_body, outs=[total] + [panel] * 4, spaces=[vmem, hbm] + [vmem] * 6)(
        keep, yd, own, D, down, yd, ye, re_in
    )
    cells = lax.axis_size("row") * lax.axis_size("col") * layers
    target = float(cells * size // 2)
    out, twice = go(
        functools.partial(last_c_body, target), outs=[out.shape, total], out_spaces=[hbm, vmem],
        spaces=[vmem, hbm] + [vmem] * (10 + len(every)), scratch=blocks(len(wanted("CNED", layers))), aliases={1: 0},
    )(keep, out, C, T, yc, yn, yc_in, g_in, *ready, *every)
    (out,) = go(
        last_s_body, outs=[out.shape], out_spaces=[hbm], spaces=[vmem, hbm] + [vmem] * 4,
        scratch=blocks(count["S"]), aliases={1: 0},
    )(keep, out, twice, down, ys, rs_in)
    return out[None, None]


def solution(mesh):
    in_specs = (
        P("row", "col", None, None, None, None),
        P("row", "col", None, None),
        P("row", "col", None, None),
    )
    out_specs = P("row", "col", None, None, None, None)
    return jax.shard_map(shards, mesh=mesh, in_specs=in_specs, out_specs=out_specs, check_vma=False)
```

```python
import functools

import jax
import jax.numpy as jnp
from jax import lax
from jax.experimental import pallas as pl
from jax.experimental.pallas import tpu as pltpu
from jax.sharding import PartitionSpec as P


F32 = jnp.float32
BF16 = jnp.bfloat16
NN = ((1,), (0,))
NT = ((1,), (1,))
TN = ((0,), (0,))
IN_PLANE = {"C": (0, 0), "N": (0, 1), "S": (1, -1), "E": (1, 0), "D": (1, 1)}


def offset_list():
    steps = (-1, 0, 1)
    return [(i, j, k) for i in steps for j in steps for k in steps if (i, j, k) > (0, 0, 0)]


def slot_number(offset):
    return offset_list().index(offset) + 1


def panel_blocks(name, layers):
    side = IN_PLANE[name]
    found = []
    for low in range(layers):
        for high in range(layers):
            step = high - low
            if abs(step) <= 1 and (*side, step) > (0, 0, 0):
                found.append((low, high, slot_number((*side, step))))
    return found


def sym_rows(layers, size):
    blocks = layers * (layers - 1) // 2 + (layers + 1) // 2
    return -(-blocks // layers) * size + 8


def rows_cols(size):
    return (
        lax.broadcasted_iota(jnp.int32, (size, size), 0),
        lax.broadcasted_iota(jnp.int32, (size, size), 1),
    )


def block_slices(k, layers, size):
    row, col = k // layers * size, k % layers * size
    return slice(row, row + size), slice(col, col + size)


def sym_places(layers):
    above = [(a, b) for a in range(layers) for b in range(a + 1, layers)]
    pairs = list(range(0, layers, 2))
    return list(enumerate(above)), [(len(above) + k, k, a) for k, a in enumerate(pairs)]


def put_sym(ref, get, layers, size, first=0):
    row, col = rows_cols(size)
    above, pairs = sym_places(layers)
    last = first + sym_rows(layers, size) - 8

    def put(k, value):
        rows, cols = block_slices(k, layers, size)
        ref[first + rows.start : first + rows.stop, cols] = value

    ref[last : last + 8, :] = jnp.zeros((8, layers * size), F32)
    if len(above) + len(pairs) < (last - first) // size * layers:
        ref[last - size : last, :] = jnp.zeros((size, layers * size), F32)
    for k, (a, b) in above:
        put(k, get(a, b))
    for k, mark, a in pairs:
        block = get(a, a)
        if a + 1 < layers:
            other = get(a + 1, a + 1)
            line = jnp.sum(jnp.where(row == col, other, 0.0), axis=0, keepdims=True)
            ref[last : last + 8, mark * size : (mark + 1) * size] = jnp.broadcast_to(line, (8, size))
            block = jnp.where(row <= col, block, other)
        put(k, block)


def take_sym(packed, layers, size):
    row, col = rows_cols(size)
    above, pairs = sym_places(layers)
    last = sym_rows(layers, size) - 8
    blocks = {}
    for k, (a, b) in above:
        rows, cols = block_slices(k, layers, size)
        blocks[a, b] = packed[rows, cols]
    for k, mark, a in pairs:
        rows, cols = block_slices(k, layers, size)
        block = packed[rows, cols]
        if a + 1 < layers:
            flipped = block.T
            line = packed[last : last + 1, mark * size : (mark + 1) * size]
            blocks[a, a] = jnp.where(row <= col, block, flipped)
            blocks[a + 1, a + 1] = jnp.where(row == col, line, jnp.where(row < col, flipped, block))
        else:
            blocks[a, a] = block
    return blocks


def whole_sym(blocks, layers):
    rows = []
    for a in range(layers):
        rows.append(
            jnp.concatenate(
                [blocks[a, b] if a <= b else blocks[b, a].T for b in range(layers)], axis=1
            )
        )
    return jnp.concatenate(rows, axis=0)


def split(value):
    high = value.astype(BF16)
    return high, (value - high.astype(F32)).astype(BF16)


def dot3(a, b, dims):
    go = functools.partial(lax.dot_general, dimension_numbers=(dims, ((), ())), preferred_element_type=F32)
    return go(a[0], b[0]) + (go(a[0], b[1]) + go(a[1], b[0]))


def cut(pair, at, size):
    return tuple(part[at : at + size, :] for part in pair)


def sym_product(pair, layers, size, dims):
    blocks = {}
    for a in range(layers):
        if dims == NT:
            left = tuple(part[a * size : (a + 1) * size, :] for part in pair)
            right = tuple(part[a * size :, :] for part in pair)
        else:
            left = tuple(part[:, a * size : (a + 1) * size] for part in pair)
            right = tuple(part[:, a * size :] for part in pair)
        strip = dot3(left, right, dims)
        for b in range(a, layers):
            blocks[a, b] = strip[:, (b - a) * size : (b - a + 1) * size]
    return blocks


def kept(mask_ref, layer, slot):
    return mask_ref[layer, slot - 1] > 0


def start_panel(stored_ref, out_ref, sems, first, name, layers, size, top=0):
    copies = []
    for k, (low, high, slot) in enumerate(panel_blocks(name, layers)):
        place = out_ref.at[pl.ds(top + low * size, size), pl.ds(high * size, size)]
        copies.append(pltpu.make_async_copy(stored_ref.at[low, slot], place, sems.at[first + k]))
        copies[-1].start()
    return copies


def end_panel(copies, out_ref, name, layers, size, mask_ref, top=0):
    blocks = panel_blocks(name, layers)
    for low in range(layers):
        for high in range(layers):
            if (low, high) not in [block[:2] for block in blocks]:
                out_ref[top + low * size : top + (low + 1) * size, high * size : (high + 1) * size] = jnp.zeros((size, size), F32)
    for copy, (low, high, slot) in zip(copies, blocks, strict=True):
        copy.wait()

        @pl.when(jnp.logical_not(kept(mask_ref, low, slot)))
        def _(low=low, high=high):
            out_ref[top + low * size : top + (low + 1) * size, high * size : (high + 1) * size] = jnp.zeros((size, size), F32)


def start_loads(stored_ref, held, sems, wanted):
    copies = [
        pltpu.make_async_copy(stored_ref.at[low, slot], held.at[k], sems.at[k])
        for k, (low, slot) in enumerate(wanted)
    ]
    for copy in copies:
        copy.start()
    return copies


def lanes(value):
    return jnp.sum(value.reshape(-1, 8, value.shape[-1]), axis=0)


def squares_of(value):
    return lanes(value * value)


def wanted(names, layers):
    return [(layer, 0) for layer in range(layers) if "C" in names] + [
        (low, slot) for name in names for low, _, slot in panel_blocks(name, layers)
    ]


def pack_body(
    layers, size, mask_ref, stored_ref, onsite_ref, t_ref, down_ref, held, sems, mask, mask_sem, onsite, onsite_sem
):
    n = layers * size
    small = [
        pltpu.make_async_copy(mask_ref, mask, mask_sem),
        pltpu.make_async_copy(onsite_ref, onsite, onsite_sem),
    ]
    for copy in small:
        copy.start()
    copies = start_loads(stored_ref, held, sems, wanted("C", layers))
    panels = []
    at = len(copies)
    for name, ref, top in (("N", t_ref, 0), ("S", down_ref, 0), ("E", down_ref, n)):
        panels.append((start_panel(stored_ref, ref, sems, at, name, layers, size, top=top), ref, name, top))
        at += len(panels[-1][0])
    for copy in small:
        copy.wait()
    row, col = rows_cols(size)
    blocks = {}
    for layer in range(layers):
        copies[layer].wait()
        block = held[layer]
        blocks[layer, layer] = 0.5 * (block + block.T) + jnp.where(row == col, onsite[layer : layer + 1, :], 0.0)
    for k, (low, high, slot) in enumerate(panel_blocks("C", layers), start=layers):
        copies[k].wait()
        blocks[low, high] = jnp.where(kept(mask, low, slot), held[k], 0.0)
    put_sym(t_ref, lambda a, b: blocks.get((a, b), jnp.zeros((size, size), F32)), layers, size, first=n)
    for started, ref, name, top in panels:
        end_panel(started, ref, name, layers, size, mask, top=top)


def pack_d_body(layers, size, mask_ref, stored_ref, _, d_ref, up_ref, sems, mask, mask_sem):
    small = pltpu.make_async_copy(mask_ref, mask, mask_sem)
    small.start()
    copies = start_panel(stored_ref, d_ref, sems, 0, "D", layers, size)
    small.wait()
    end_panel(copies, d_ref, "D", layers, size, mask)
    blocks = sym_product(split(d_ref[...]), layers, size, TN)
    put_sym(up_ref, lambda a, b: blocks[a, b], layers, size)


def sums_body(layers, size, mask_ref, _, down_ref, t_ref, d_ref, packed_ref, c_ref, keep_ref, sums_ref):
    n = layers * size
    packed_ref[...] = t_ref[n:, :]
    c_ref[...] = whole_sym(take_sym(t_ref[n:, :], layers, size), layers)
    keep_ref[...] = jnp.zeros(keep_ref.shape, F32)
    slots = keep_ref.shape[0] // layers
    for low, slot in wanted(IN_PLANE, layers):
        here = 1.0 if slot == 0 else jnp.where(kept(mask_ref, low, slot), 1.0, 0.0)
        keep_ref[low * slots + slot : low * slots + slot + 1, :] = jnp.full((1, size), here, F32)
    row, col = rows_cols(size)
    trace = 0.0
    for layer in range(layers):
        here = slice(layer * size, (layer + 1) * size)
        trace = trace + lanes(jnp.where(row == col, c_ref[here, here], 0.0))
    sums_ref[:8, :] = trace
    squares = squares_of(c_ref[...])
    for ref in (down_ref.at[:n, :], down_ref.at[n:, :], t_ref.at[:n, :], d_ref):
        squares = squares + 2.0 * squares_of(ref[...])
    sums_ref[8:, :] = sum(squares[:, at * size : (at + 1) * size] for at in range(layers))


def local_g_body(layers, size, _, sums_ref, more_ref, t_ref, down_ref, d_ref, total_ref, g_ref, r_ref, yc_up_ref):
    n = layers * size
    total_ref[...] = sums_ref[...] + more_ref[...]
    n_now, e, d = split(t_ref[:n, :]), split(down_ref[n:, :]), split(d_ref[...])
    blocks = sym_product(e, layers, size, TN)
    g_ref[:n, :] = dot3(e, d, TN)
    put_sym(g_ref, lambda a, b: blocks[a, b], layers, size, first=n)
    r_ref[:n, :] = dot3(n_now, e, TN)
    r_ref[n:, :] = dot3(n_now, d, TN)
    blocks = sym_product(n_now, layers, size, TN)
    put_sym(yc_up_ref, lambda a, b: blocks[a, b], layers, size)


def local_y_body(
    layers, size, _, sums_ref, more_ref, c_ref, t_ref, down_ref, d_ref,
    total_ref, out_ref, yc_ref, yn_ref, ys_ref, ye_ref, yd_ref, zero, sems,
):
    total_ref[...] = sums_ref[...] + more_ref[...]
    zero[...] = jnp.zeros(zero.shape, F32)
    written = set(wanted(IN_PLANE, layers))
    copies = []
    for layer in range(layers):
        for slot in range(out_ref.shape[1]):
            if (layer, slot) not in written:
                copies.append(pltpu.make_async_copy(zero, out_ref.at[layer, slot], sems.at[len(copies)]))
                copies[-1].start()
    at = layers * size
    parts = (c_ref[...], t_ref[:at, :], down_ref[:at, :], down_ref[at:, :], d_ref[...])
    c, n, s, e, d = (split(part) for part in parts)
    yn_ref[...] = dot3(c, n, NN)
    ys_ref[...] = dot3(c, s, NN)
    ye_ref[...] = dot3(c, e, NN)
    yd_ref[...] = dot3(c, d, NN)
    terms = [
        sym_product(pair, layers, size, dims)
        for pair, dims in ((c, NT), (n, NT), (s, NT), (e, NT), (d, NT))
    ]
    put_sym(yc_ref, lambda a, b: sum(term[a, b] for term in terms), layers, size)
    for copy in copies:
        copy.wait()


def copy_body(layers, size, _, __, from_ref, to_ref):
    to_ref[...] = from_ref[...]


def yc_body(layers, size, _, __, from_ref, to_ref):
    tall = from_ref.shape[0]
    to_ref[:tall, :] = from_ref[...]
    to_ref[tall:, :] = jnp.zeros((8, layers * size), F32)


def g_body(layers, size, _, sums_ref, more_ref, g0_ref, below_ref, up_ref, total_ref, g_ref):
    n, last = layers * size, g_ref.shape[0] - 8
    parts = sums_ref[...] + more_ref[...]
    line = lax.broadcasted_iota(jnp.int32, total_ref.shape, 0)
    total = jnp.where(line % 4 == 0, jnp.sum(parts[:8, :]), jnp.sum(parts[8:, :]))
    total_ref[...] = total
    stu, eu = split(below_ref[:n, :].T), split(below_ref[n:, :])
    g_ref[:n, :] = g0_ref[:n, :] + dot3(stu, eu, NN)
    blocks = sym_product(stu, layers, size, NT)
    put_sym(g_ref, lambda a, b: blocks[a, b], layers, size, first=n)
    g_ref[n:, :] += g0_ref[n:, :] + up_ref[...]
    for at in range(layers):
        cols = slice(at * size, (at + 1) * size)
        g_ref[last:, cols] = jnp.where(line < 4, g_ref[last:, cols], total)


def early_body(layers, size, _, t_ref, e_ref, d_ref, below_ref, cu_ref, yn0_ref, ye0_ref, yd0_ref, yn_ref, ye_ref, yd_ref):
    at = layers * size
    n, e, d = split(t_ref[:at, :]), split(e_ref[at:, :]), split(d_ref[...])
    su, eu = split(below_ref[:at, :]), split(below_ref[at:, :])
    cu = split(whole_sym(take_sym(cu_ref, layers, size), layers))
    yn_ref[...] = yn0_ref[...] + dot3(e, su, NT) + dot3(d, eu, NT) + dot3(n, cu, NN)
    ye_ref[...] = ye0_ref[...] + dot3(n, su, NN)
    yd_ref[...] = yd0_ref[...] + dot3(n, eu, NN)


def r_body(layers, size, _, r0_ref, below_ref, tx_ref, rs_ref, re_ref):
    n = layers * size
    su, eu, nx = split(below_ref[:n, :]), split(below_ref[n:, :]), split(tx_ref[:n, :])
    cx = split(whole_sym(take_sym(tx_ref[n:, :], layers, size), layers))
    rs_ref[...] = r0_ref[:n, :] + dot3(su, cx, NN) + dot3(eu, nx, NT)
    re_ref[...] = r0_ref[n:, :] + dot3(su, nx, NN)


def hand_body(layers, size, _, __, tx_ref, cx_ref):
    cx_ref[...] = tx_ref[layers * size :, :]


def middle_body(layers, size, _, e_ref, d_ref, tx_ref, ye0_ref, yd0_ref, ye_ref, yd_ref):
    at = layers * size
    e, d, nx = split(e_ref[at:, :]), split(d_ref[...]), split(tx_ref[:at, :])
    cx = split(whole_sym(take_sym(tx_ref[at:, :], layers, size), layers))
    ye_ref[...] = ye0_ref[...] + dot3(e, cx, NN) + dot3(d, nx, NT)
    yd_ref[...] = yd0_ref[...] + dot3(e, nx, NN)


def middle_c_body(layers, size, _, sums_ref, d_ref, cxu_ref, yd0_ref, total_ref, yd_ref):
    total_ref[...] = sums_ref[...]
    cxu = split(whole_sym(take_sym(cxu_ref, layers, size), layers))
    yd_ref[...] = yd0_ref[...] + dot3(split(d_ref[...]), cxu, NN)


def twice_h(target, size, sums):
    t1, t2 = sums[0:1, :], sums[1:2, :]
    return 2.0 * jax.nn.sigmoid((jnp.abs(t2 - target) - jnp.abs(2.0 * t1 - t2 - target)) / size)


class Sender:
    def __init__(self, twice, keep_ref, out_ref, held, sems):
        self.twice, self.keep_ref, self.out_ref, self.held, self.sems = twice, keep_ref, out_ref, held, sems
        self.copies = []

    def put(self, value, low, slot):
        k = len(self.copies)
        self.held[k] = value
        self.copies.append(pltpu.make_async_copy(self.held.at[k], self.out_ref.at[low, slot], self.sems.at[k]))
        self.copies[-1].start()

    def send(self, y, a, low, slot):
        at = low * self.out_ref.shape[1] + slot
        self.put(self.keep_ref[at : at + 1, :] * (y + self.twice * (a - y)), low, slot)

    def send_panel(self, name, a_ref, terms, layers, size):
        for low, high, slot in panel_blocks(name, layers):
            rows, cols = slice(low * size, (low + 1) * size), slice(high * size, (high + 1) * size)
            self.send(sum(ref[rows, cols] for ref in terms), a_ref[rows, cols], low, slot)

    def send_ready(self, name, y_ref, gap_ref, layers, size):
        for low, high, slot in panel_blocks(name, layers):
            rows, cols = slice(low * size, (low + 1) * size), slice(high * size, (high + 1) * size)
            self.put(y_ref[rows, cols] + self.twice * gap_ref[rows, cols], low, slot)

    def wait(self):
        for copy in self.copies:
            copy.wait()


def ready_body(layers, size, keep_ref, _, sums_ref, d_ref, e_ref, yd_ref, ye_ref, re_ref, total_ref, *outs):
    n, slots = layers * size, keep_ref.shape[0] // layers
    total_ref[...] = sums_ref[...]
    for name, a_ref, terms, y_out, gap_out in (
        ("D", d_ref, [yd_ref], *outs[:2]),
        ("E", e_ref.at[n:, :], [ye_ref, re_ref], *outs[2:]),
    ):
        for low, high, slot in panel_blocks(name, layers):
            rows, cols = slice(low * size, (low + 1) * size), slice(high * size, (high + 1) * size)
            at = low * slots + slot
            y = keep_ref[at : at + 1, :] * sum(ref[rows, cols] for ref in terms)
            y_out[rows, cols] = y
            gap_out[rows, cols] = a_ref[rows, cols] - y


def last_c_body(
    target, layers, size, keep_ref, _, c_ref, t_ref, yc_ref, yn_ref, yc_in_ref, g_ref, pd_ref, qd_ref, pe_ref, qe_ref, *rest
):
    *sums_refs, out_ref, twice_ref, held, sems = rest
    n, last = layers * size, g_ref.shape[0] - 8
    line = lax.broadcasted_iota(jnp.int32, (8, size), 0)
    beside = g_ref[last:, :size]
    sums = jnp.where(line == 0, beside[4:5, :], beside[5:6, :])
    twice = twice_h(target, size, sum((ref[...] for ref in sums_refs), start=sums))
    twice_ref[...] = jnp.broadcast_to(twice, twice_ref.shape)
    sender = Sender(twice, keep_ref, out_ref, held, sems)
    sender.send_ready("D", pd_ref, qd_ref, layers, size)
    sender.send_ready("E", pe_ref, qe_ref, layers, size)
    sender.send_panel("N", t_ref, [yn_ref, g_ref], layers, size)
    blocks = take_sym(yc_ref[...] + yc_in_ref[: yc_ref.shape[0], :] + g_ref[n:, :], layers, size)
    for low, high, slot in panel_blocks("C", layers) + [(layer, layer, 0) for layer in range(layers)]:
        rows, cols = slice(low * size, (low + 1) * size), slice(high * size, (high + 1) * size)
        sender.send(blocks[low, high], c_ref[rows, cols], low, slot)
    sender.wait()


def last_s_body(layers, size, keep_ref, _, twice_ref, down_ref, ys_ref, rs_ref, out_ref, held, sems):
    sender = Sender(twice_ref[0:1, :], keep_ref, out_ref, held, sems)
    sender.send_panel("S", down_ref, [ys_ref, rs_ref], layers, size)
    sender.wait()


def call(body, layers, size, outs, spaces, scratch=(), limit=24, out_spaces=None, aliases=None):
    return pl.pallas_call(
        functools.partial(body, layers, size),
        out_shape=[jax.ShapeDtypeStruct(shape, F32) for shape in outs],
        in_specs=[pl.BlockSpec(memory_space=space) for space in spaces],
        out_specs=[pl.BlockSpec(memory_space=space) for space in out_spaces or [pltpu.VMEM] * len(outs)],
        scratch_shapes=list(scratch),
        input_output_aliases=aliases or {},
        compiler_params=pltpu.CompilerParams(vmem_limit_bytes=limit << 20),
    )


def passed_along(value, axis, by):
    peers = lax.axis_size(axis)
    return lax.ppermute(value, axis, [(i, (i + by) % peers) for i in range(peers)])


def swapped(value, axis, bit):
    peers = lax.axis_size(axis)
    return lax.ppermute(value, axis, [(i, i ^ bit) for i in range(peers)])


def shards(stored_blocks, onsite, bond_mask):
    stored, onsite, mask = stored_blocks[0, 0], onsite[0, 0], bond_mask[0, 0]
    layers, slots, size = stored.shape[:3]
    n, tall = layers * size, sym_rows(layers, size)
    panel, packed, sums, total = (n, n), (tall, n), (16, size), (8, size)
    vmem, smem, hbm = pltpu.VMEM, pltpu.SMEM, pltpu.HBM

    def blocks(count):
        return [pltpu.VMEM((count, size, size), F32), pltpu.SemaphoreType.DMA((count,))]

    go = functools.partial(call, layers=layers, size=size)
    stored, onsite, mask_hbm = (pltpu.with_memory_space_constraint(value, hbm) for value in (stored, onsite, mask))

    peers = lax.axis_size("col")
    bits = [1 << k for k in range(peers.bit_length() - 1)]
    bits = bits[:1] + bits[2:] + bits[1:2]

    def arriving(value):
        return swapped(value, "col", bits.pop(0)) if bits else jnp.zeros_like(value)

    small = [pltpu.SMEM(mask.shape, mask.dtype), pltpu.SemaphoreType.DMA]
    count = {name: len(wanted(name, layers)) for name in IN_PLANE}
    T, down = go(
        pack_body, outs=[(n + tall, n), (2 * n, n)], spaces=[hbm] * 3,
        scratch=[pltpu.VMEM((count["C"], size, size), F32), pltpu.SemaphoreType.DMA((len(wanted("CNSE", layers)),))]
        + small + [pltpu.VMEM(onsite.shape, F32), pltpu.SemaphoreType.DMA],
    )(mask_hbm, stored, onsite)
    T_x = passed_along(T, "row", -1)
    below = passed_along(down, "col", -1)
    D, gc = go(
        pack_d_body, outs=[panel, packed], spaces=[hbm] * 3, scratch=[pltpu.SemaphoreType.DMA((count["D"],))] + small
    )(mask_hbm, stored, T)
    gc_in = passed_along(gc, "col", 1)
    Cp, C, keep, own = go(sums_body, outs=[packed, panel, (layers * slots, size), sums], spaces=[smem, hbm] + [vmem] * 3)(
        mask, gc, down, T, D
    )
    if peers.bit_count() > 1:
        own = own + sum(passed_along(own, "col", by) for by in range(1, peers))
        bits = []
    while len(bits) > 3:
        own = own + arriving(own)
    more = arriving(own)
    own, g0, r0, yc_up = go(local_g_body, outs=[sums, (n + tall, n), (2 * n, n), packed], spaces=[hbm] + [vmem] * 5)(
        gc, own, more, T, down, D
    )
    more = arriving(own)
    own, out, yc, yn, ys, ye, yd = go(
        local_y_body, outs=[sums, (layers, slots, size, size), packed] + [panel] * 4, spaces=[hbm] + [vmem] * 6,
        out_spaces=[vmem, hbm] + [vmem] * 5, scratch=[pltpu.VMEM((size, size), F32), pltpu.SemaphoreType.DMA((layers * slots,))],
    )(g0, own, more, C, T, down, D)
    more = arriving(own)
    (yc_up,) = go(yc_body, outs=[(tall + 8, n)], spaces=[hbm] * 2 + [vmem])(yc, below, yc_up)
    yc_in = passed_along(yc_up, "col", 1)
    own, g = go(g_body, outs=[total, (n + tall, n)], spaces=[hbm] + [vmem] * 5)(yc_up, own, more, g0, below, gc_in)
    g_in = passed_along(g, "row", 1)
    Cp_u = passed_along(Cp, "col", -1)
    rs, re = go(r_body, outs=[panel, panel], spaces=[hbm] + [vmem] * 3)(g, r0, below, T_x)
    (rs,) = go(copy_body, outs=[panel], spaces=[hbm] * 2 + [vmem])(yc_in, re, rs)
    rs_in, re_in = passed_along(rs, "col", 1), passed_along(re, "col", 1)
    (Cp_x,) = go(hand_body, outs=[packed], spaces=[hbm] * 2 + [vmem])(rs, Cp_u, T_x)
    Cp_xu = passed_along(Cp_x, "col", -1)
    yn, ye, yd = go(early_body, outs=[panel] * 3, spaces=[hbm] + [vmem] * 8)(Cp_x, T, down, D, below, Cp_u, yn, ye, yd)
    ye, yd = go(middle_body, outs=[panel, panel], spaces=[hbm] + [vmem] * 5)(yn, down, D, T_x, ye, yd)
    early_sums = own
    own, yd = go(middle_c_body, outs=[total, panel], spaces=[hbm] + [vmem] * 4)(ye, own, D, Cp_xu, yd)
    every = [own] + [passed_along(own if by == 1 else early_sums, "row", -by) for by in range(1, lax.axis_size("row") - 1)]
    _, *ready = go(ready_body, outs=[total] + [panel] * 4, spaces=[vmem, hbm] + [vmem] * 6)(
        keep, yd, own, D, down, yd, ye, re_in
    )
    cells = lax.axis_size("row") * lax.axis_size("col") * layers
    target = float(cells * size // 2)
    out, twice = go(
        functools.partial(last_c_body, target), outs=[out.shape, total], out_spaces=[hbm, vmem],
        spaces=[vmem, hbm] + [vmem] * (10 + len(every)), scratch=blocks(len(wanted("CNED", layers))), aliases={1: 0},
    )(keep, out, C, T, yc, yn, yc_in, g_in, *ready, *every)
    (out,) = go(
        last_s_body, outs=[out.shape], out_spaces=[hbm], spaces=[vmem, hbm] + [vmem] * 4,
        scratch=blocks(count["S"]), aliases={1: 0},
    )(keep, out, twice, down, ys, rs_in)
    return out[None, None]


def solution(mesh):
    in_specs = (
        P("row", "col", None, None, None, None),
        P("row", "col", None, None),
        P("row", "col", None, None),
    )
    out_specs = P("row", "col", None, None, None, None)
    return jax.shard_map(shards, mesh=mesh, in_specs=in_specs, out_specs=out_specs, check_vma=False)
```

```python
import functools

import jax
import jax.numpy as jnp
from jax import lax
from jax.experimental import pallas as pl
from jax.experimental.pallas import tpu as pltpu
from jax.sharding import PartitionSpec as P


F32 = jnp.float32
BF16 = jnp.bfloat16
NN = ((1,), (0,))
NT = ((1,), (1,))
TN = ((0,), (0,))
IN_PLANE = {"C": (0, 0), "N": (0, 1), "S": (1, -1), "E": (1, 0), "D": (1, 1)}


def offset_list():
    steps = (-1, 0, 1)
    return [(i, j, k) for i in steps for j in steps for k in steps if (i, j, k) > (0, 0, 0)]


def slot_number(offset):
    return offset_list().index(offset) + 1


def panel_blocks(name, layers):
    side = IN_PLANE[name]
    found = []
    for low in range(layers):
        for high in range(layers):
            step = high - low
            if abs(step) <= 1 and (*side, step) > (0, 0, 0):
                found.append((low, high, slot_number((*side, step))))
    return found


def sym_rows(layers, size):
    blocks = layers * (layers - 1) // 2 + (layers + 1) // 2
    return -(-blocks // layers) * size + 8


def rows_cols(size):
    return (
        lax.broadcasted_iota(jnp.int32, (size, size), 0),
        lax.broadcasted_iota(jnp.int32, (size, size), 1),
    )


def block_slices(k, layers, size):
    row, col = k // layers * size, k % layers * size
    return slice(row, row + size), slice(col, col + size)


def sym_places(layers):
    above = [(a, b) for a in range(layers) for b in range(a + 1, layers)]
    pairs = list(range(0, layers, 2))
    return list(enumerate(above)), [(len(above) + k, k, a) for k, a in enumerate(pairs)]


def put_sym(ref, get, layers, size, first=0):
    row, col = rows_cols(size)
    above, pairs = sym_places(layers)
    last = first + sym_rows(layers, size) - 8

    def put(k, value):
        rows, cols = block_slices(k, layers, size)
        ref[first + rows.start : first + rows.stop, cols] = value

    ref[last : last + 8, :] = jnp.zeros((8, layers * size), F32)
    if len(above) + len(pairs) < (last - first) // size * layers:
        ref[last - size : last, :] = jnp.zeros((size, layers * size), F32)
    for k, (a, b) in above:
        put(k, get(a, b))
    for k, mark, a in pairs:
        block = get(a, a)
        if a + 1 < layers:
            other = get(a + 1, a + 1)
            line = jnp.sum(jnp.where(row == col, other, 0.0), axis=0, keepdims=True)
            ref[last : last + 8, mark * size : (mark + 1) * size] = jnp.broadcast_to(line, (8, size))
            block = jnp.where(row <= col, block, other)
        put(k, block)


def take_sym(packed, layers, size):
    row, col = rows_cols(size)
    above, pairs = sym_places(layers)
    last = sym_rows(layers, size) - 8
    blocks = {}
    for k, (a, b) in above:
        rows, cols = block_slices(k, layers, size)
        blocks[a, b] = packed[rows, cols]
    for k, mark, a in pairs:
        rows, cols = block_slices(k, layers, size)
        block = packed[rows, cols]
        if a + 1 < layers:
            flipped = block.T
            line = packed[last : last + 1, mark * size : (mark + 1) * size]
            blocks[a, a] = jnp.where(row <= col, block, flipped)
            blocks[a + 1, a + 1] = jnp.where(row == col, line, jnp.where(row < col, flipped, block))
        else:
            blocks[a, a] = block
    return blocks


def whole_sym(blocks, layers):
    rows = []
    for a in range(layers):
        rows.append(
            jnp.concatenate(
                [blocks[a, b] if a <= b else blocks[b, a].T for b in range(layers)], axis=1
            )
        )
    return jnp.concatenate(rows, axis=0)


def split(value):
    high = value.astype(BF16)
    return high, (value - high.astype(F32)).astype(BF16)


def dot3(a, b, dims):
    go = functools.partial(lax.dot_general, dimension_numbers=(dims, ((), ())), preferred_element_type=F32)
    return go(a[0], b[0]) + (go(a[0], b[1]) + go(a[1], b[0]))


def cut(pair, at, size):
    return tuple(part[at : at + size, :] for part in pair)


def sym_product(pair, layers, size, dims):
    blocks = {}
    for a in range(layers):
        if dims == NT:
            left = tuple(part[a * size : (a + 1) * size, :] for part in pair)
            right = tuple(part[a * size :, :] for part in pair)
        else:
            left = tuple(part[:, a * size : (a + 1) * size] for part in pair)
            right = tuple(part[:, a * size :] for part in pair)
        strip = dot3(left, right, dims)
        for b in range(a, layers):
            blocks[a, b] = strip[:, (b - a) * size : (b - a + 1) * size]
    return blocks


def kept(mask_ref, layer, slot):
    return mask_ref[layer, slot - 1] > 0


def start_panel(stored_ref, out_ref, sems, first, name, layers, size, top=0):
    copies = []
    for k, (low, high, slot) in enumerate(panel_blocks(name, layers)):
        place = out_ref.at[pl.ds(top + low * size, size), pl.ds(high * size, size)]
        copies.append(pltpu.make_async_copy(stored_ref.at[low, slot], place, sems.at[first + k]))
        copies[-1].start()
    return copies


def end_panel(copies, out_ref, name, layers, size, mask_ref, top=0):
    blocks = panel_blocks(name, layers)
    for low in range(layers):
        for high in range(layers):
            if (low, high) not in [block[:2] for block in blocks]:
                out_ref[top + low * size : top + (low + 1) * size, high * size : (high + 1) * size] = jnp.zeros((size, size), F32)
    for copy, (low, high, slot) in zip(copies, blocks, strict=True):
        copy.wait()

        @pl.when(jnp.logical_not(kept(mask_ref, low, slot)))
        def _(low=low, high=high):
            out_ref[top + low * size : top + (low + 1) * size, high * size : (high + 1) * size] = jnp.zeros((size, size), F32)


def start_loads(stored_ref, held, sems, wanted):
    copies = [
        pltpu.make_async_copy(stored_ref.at[low, slot], held.at[k], sems.at[k])
        for k, (low, slot) in enumerate(wanted)
    ]
    for copy in copies:
        copy.start()
    return copies


def lanes(value):
    return jnp.sum(value.reshape(-1, 8, value.shape[-1]), axis=0)


def squares_of(value):
    return lanes(value * value)


def wanted(names, layers):
    return [(layer, 0) for layer in range(layers) if "C" in names] + [
        (low, slot) for name in names for low, _, slot in panel_blocks(name, layers)
    ]


def pack_body(
    layers, size, mask_ref, stored_ref, onsite_ref, t_ref, down_ref, held, sems, mask, mask_sem, onsite, onsite_sem
):
    n = layers * size
    small = [
        pltpu.make_async_copy(mask_ref, mask, mask_sem),
        pltpu.make_async_copy(onsite_ref, onsite, onsite_sem),
    ]
    for copy in small:
        copy.start()
    copies = start_loads(stored_ref, held, sems, wanted("C", layers))
    panels = []
    at = len(copies)
    for name, ref, top in (("N", t_ref, 0), ("S", down_ref, 0), ("E", down_ref, n)):
        panels.append((start_panel(stored_ref, ref, sems, at, name, layers, size, top=top), ref, name, top))
        at += len(panels[-1][0])
    for copy in small:
        copy.wait()
    row, col = rows_cols(size)
    blocks = {}
    for layer in range(layers):
        copies[layer].wait()
        block = held[layer]
        blocks[layer, layer] = 0.5 * (block + block.T) + jnp.where(row == col, onsite[layer : layer + 1, :], 0.0)
    for k, (low, high, slot) in enumerate(panel_blocks("C", layers), start=layers):
        copies[k].wait()
        blocks[low, high] = jnp.where(kept(mask, low, slot), held[k], 0.0)
    put_sym(t_ref, lambda a, b: blocks.get((a, b), jnp.zeros((size, size), F32)), layers, size, first=n)
    for started, ref, name, top in panels:
        end_panel(started, ref, name, layers, size, mask, top=top)


def pack_d_body(layers, size, mask_ref, stored_ref, _, d_ref, up_ref, sems, mask, mask_sem):
    small = pltpu.make_async_copy(mask_ref, mask, mask_sem)
    small.start()
    copies = start_panel(stored_ref, d_ref, sems, 0, "D", layers, size)
    small.wait()
    end_panel(copies, d_ref, "D", layers, size, mask)
    blocks = sym_product(split(d_ref[...]), layers, size, TN)
    put_sym(up_ref, lambda a, b: blocks[a, b], layers, size)


def sums_body(layers, size, mask_ref, _, down_ref, t_ref, d_ref, packed_ref, c_ref, keep_ref, sums_ref):
    n = layers * size
    packed_ref[...] = t_ref[n:, :]
    c_ref[...] = whole_sym(take_sym(t_ref[n:, :], layers, size), layers)
    keep_ref[...] = jnp.zeros(keep_ref.shape, F32)
    slots = keep_ref.shape[0] // layers
    for low, slot in wanted(IN_PLANE, layers):
        here = 1.0 if slot == 0 else jnp.where(kept(mask_ref, low, slot), 1.0, 0.0)
        keep_ref[low * slots + slot : low * slots + slot + 1, :] = jnp.full((1, size), here, F32)
    row, col = rows_cols(size)
    trace = 0.0
    for layer in range(layers):
        here = slice(layer * size, (layer + 1) * size)
        trace = trace + lanes(jnp.where(row == col, c_ref[here, here], 0.0))
    sums_ref[:8, :] = trace
    squares = squares_of(c_ref[...])
    for ref in (down_ref.at[:n, :], down_ref.at[n:, :], t_ref.at[:n, :], d_ref):
        squares = squares + 2.0 * squares_of(ref[...])
    sums_ref[8:, :] = sum(squares[:, at * size : (at + 1) * size] for at in range(layers))


def local_g_body(layers, size, _, sums_ref, more_ref, t_ref, down_ref, d_ref, total_ref, g_ref, r_ref, yc_up_ref):
    n = layers * size
    total_ref[...] = sums_ref[...] + more_ref[...]
    n_now, e, d = split(t_ref[:n, :]), split(down_ref[n:, :]), split(d_ref[...])
    blocks = sym_product(e, layers, size, TN)
    g_ref[:n, :] = dot3(e, d, TN)
    put_sym(g_ref, lambda a, b: blocks[a, b], layers, size, first=n)
    r_ref[:n, :] = dot3(n_now, e, TN)
    r_ref[n:, :] = dot3(n_now, d, TN)
    blocks = sym_product(n_now, layers, size, TN)
    put_sym(yc_up_ref, lambda a, b: blocks[a, b], layers, size)


def local_y_body(
    layers, size, _, sums_ref, more_ref, c_ref, t_ref, down_ref, d_ref,
    total_ref, out_ref, yc_ref, yn_ref, ys_ref, ye_ref, yd_ref, zero, sems,
):
    total_ref[...] = sums_ref[...] + more_ref[...]
    zero[...] = jnp.zeros(zero.shape, F32)
    written = set(wanted(IN_PLANE, layers))
    copies = []
    for layer in range(layers):
        for slot in range(out_ref.shape[1]):
            if (layer, slot) not in written:
                copies.append(pltpu.make_async_copy(zero, out_ref.at[layer, slot], sems.at[len(copies)]))
                copies[-1].start()
    at = layers * size
    parts = (c_ref[...], t_ref[:at, :], down_ref[:at, :], down_ref[at:, :], d_ref[...])
    c, n, s, e, d = (split(part) for part in parts)
    yn_ref[...] = dot3(c, n, NN)
    ys_ref[...] = dot3(c, s, NN)
    ye_ref[...] = dot3(c, e, NN)
    yd_ref[...] = dot3(c, d, NN)
    terms = [
        sym_product(pair, layers, size, dims)
        for pair, dims in ((c, NT), (n, NT), (s, NT), (e, NT), (d, NT))
    ]
    put_sym(yc_ref, lambda a, b: sum(term[a, b] for term in terms), layers, size)
    for copy in copies:
        copy.wait()


def copy_body(layers, size, _, __, from_ref, to_ref):
    to_ref[...] = from_ref[...]


def yc_body(layers, size, _, __, from_ref, to_ref):
    tall = from_ref.shape[0]
    to_ref[:tall, :] = from_ref[...]
    to_ref[tall:, :] = jnp.zeros((8, layers * size), F32)


def g_body(layers, size, _, sums_ref, more_ref, g0_ref, below_ref, up_ref, total_ref, g_ref):
    n, last = layers * size, g_ref.shape[0] - 8
    parts = sums_ref[...] + more_ref[...]
    line = lax.broadcasted_iota(jnp.int32, total_ref.shape, 0)
    total = jnp.where(line % 4 == 0, jnp.sum(parts[:8, :]), jnp.sum(parts[8:, :]))
    total_ref[...] = total
    stu, eu = split(below_ref[:n, :].T), split(below_ref[n:, :])
    g_ref[:n, :] = g0_ref[:n, :] + dot3(stu, eu, NN)
    blocks = sym_product(stu, layers, size, NT)
    put_sym(g_ref, lambda a, b: blocks[a, b], layers, size, first=n)
    g_ref[n:, :] += g0_ref[n:, :] + up_ref[...]
    for at in range(layers):
        cols = slice(at * size, (at + 1) * size)
        g_ref[last:, cols] = jnp.where(line < 4, g_ref[last:, cols], total)


def early_body(layers, size, _, t_ref, e_ref, d_ref, below_ref, cu_ref, yn0_ref, ye0_ref, yd0_ref, yn_ref, ye_ref, yd_ref):
    at = layers * size
    n, e, d = split(t_ref[:at, :]), split(e_ref[at:, :]), split(d_ref[...])
    su, eu = split(below_ref[:at, :]), split(below_ref[at:, :])
    cu = split(whole_sym(take_sym(cu_ref, layers, size), layers))
    yn_ref[...] = yn0_ref[...] + dot3(e, su, NT) + dot3(d, eu, NT) + dot3(n, cu, NN)
    ye_ref[...] = ye0_ref[...] + dot3(n, su, NN)
    yd_ref[...] = yd0_ref[...] + dot3(n, eu, NN)


def r_e_body(layers, size, _, r0_ref, below_ref, tx_ref, re_ref):
    n = layers * size
    su, nx = split(below_ref[:n, :]), split(tx_ref[:n, :])
    re_ref[...] = r0_ref[n:, :] + dot3(su, nx, NN)


def r_s_body(layers, size, _, r0_ref, below_ref, tx_ref, rs_ref):
    n = layers * size
    su, eu, nx = split(below_ref[:n, :]), split(below_ref[n:, :]), split(tx_ref[:n, :])
    cx = split(whole_sym(take_sym(tx_ref[n:, :], layers, size), layers))
    rs_ref[...] = r0_ref[:n, :] + dot3(su, cx, NN) + dot3(eu, nx, NT)


def hand_body(layers, size, _, __, tx_ref, cx_ref):
    cx_ref[...] = tx_ref[layers * size :, :]


def middle_body(layers, size, _, e_ref, d_ref, tx_ref, ye0_ref, yd0_ref, ye_ref, yd_ref):
    at = layers * size
    e, d, nx = split(e_ref[at:, :]), split(d_ref[...]), split(tx_ref[:at, :])
    cx = split(whole_sym(take_sym(tx_ref[at:, :], layers, size), layers))
    ye_ref[...] = ye0_ref[...] + dot3(e, cx, NN) + dot3(d, nx, NT)
    yd_ref[...] = yd0_ref[...] + dot3(e, nx, NN)


def middle_c_body(layers, size, _, sums_ref, d_ref, cxu_ref, yd0_ref, total_ref, yd_ref):
    total_ref[...] = sums_ref[...]
    cxu = split(whole_sym(take_sym(cxu_ref, layers, size), layers))
    yd_ref[...] = yd0_ref[...] + dot3(split(d_ref[...]), cxu, NN)


def twice_h(target, size, sums):
    t1, t2 = sums[0:1, :], sums[1:2, :]
    return 2.0 * jax.nn.sigmoid((jnp.abs(t2 - target) - jnp.abs(2.0 * t1 - t2 - target)) / size)


class Sender:
    def __init__(self, twice, keep_ref, out_ref, held, sems):
        self.twice, self.keep_ref, self.out_ref, self.held, self.sems = twice, keep_ref, out_ref, held, sems
        self.copies = []

    def put(self, value, low, slot):
        k = len(self.copies)
        self.held[k] = value
        self.copies.append(pltpu.make_async_copy(self.held.at[k], self.out_ref.at[low, slot], self.sems.at[k]))
        self.copies[-1].start()

    def send(self, y, a, low, slot):
        at = low * self.out_ref.shape[1] + slot
        self.put(self.keep_ref[at : at + 1, :] * (y + self.twice * (a - y)), low, slot)

    def send_panel(self, name, a_ref, terms, layers, size):
        for low, high, slot in panel_blocks(name, layers):
            rows, cols = slice(low * size, (low + 1) * size), slice(high * size, (high + 1) * size)
            self.send(sum(ref[rows, cols] for ref in terms), a_ref[rows, cols], low, slot)

    def send_ready(self, name, y_ref, gap_ref, layers, size):
        for low, high, slot in panel_blocks(name, layers):
            rows, cols = slice(low * size, (low + 1) * size), slice(high * size, (high + 1) * size)
            self.put(y_ref[rows, cols] + self.twice * gap_ref[rows, cols], low, slot)

    def wait(self):
        for copy in self.copies:
            copy.wait()


def ready_body(layers, size, keep_ref, _, sums_ref, d_ref, e_ref, yd_ref, ye_ref, re_ref, total_ref, *outs):
    n, slots = layers * size, keep_ref.shape[0] // layers
    total_ref[...] = sums_ref[...]
    for name, a_ref, terms, y_out, gap_out in (
        ("D", d_ref, [yd_ref], *outs[:2]),
        ("E", e_ref.at[n:, :], [ye_ref, re_ref], *outs[2:]),
    ):
        for low, high, slot in panel_blocks(name, layers):
            rows, cols = slice(low * size, (low + 1) * size), slice(high * size, (high + 1) * size)
            at = low * slots + slot
            y = keep_ref[at : at + 1, :] * sum(ref[rows, cols] for ref in terms)
            y_out[rows, cols] = y
            gap_out[rows, cols] = a_ref[rows, cols] - y


def last_c_body(
    target, layers, size, keep_ref, _, c_ref, t_ref, yc_ref, yn_ref, yc_in_ref, g_ref, pd_ref, qd_ref, pe_ref, qe_ref, *rest
):
    *sums_refs, out_ref, twice_ref, held, sems = rest
    n, last = layers * size, g_ref.shape[0] - 8
    line = lax.broadcasted_iota(jnp.int32, (8, size), 0)
    beside = g_ref[last:, :size]
    sums = jnp.where(line == 0, beside[4:5, :], beside[5:6, :])
    twice = twice_h(target, size, sum((ref[...] for ref in sums_refs), start=sums))
    twice_ref[...] = jnp.broadcast_to(twice, twice_ref.shape)
    sender = Sender(twice, keep_ref, out_ref, held, sems)
    sender.send_ready("D", pd_ref, qd_ref, layers, size)
    sender.send_ready("E", pe_ref, qe_ref, layers, size)
    sender.send_panel("N", t_ref, [yn_ref, g_ref], layers, size)
    blocks = take_sym(yc_ref[...] + yc_in_ref[: yc_ref.shape[0], :] + g_ref[n:, :], layers, size)
    for low, high, slot in panel_blocks("C", layers) + [(layer, layer, 0) for layer in range(layers)]:
        rows, cols = slice(low * size, (low + 1) * size), slice(high * size, (high + 1) * size)
        sender.send(blocks[low, high], c_ref[rows, cols], low, slot)
    sender.wait()


def last_s_body(layers, size, keep_ref, _, twice_ref, down_ref, ys_ref, rs_ref, out_ref, held, sems):
    sender = Sender(twice_ref[0:1, :], keep_ref, out_ref, held, sems)
    sender.send_panel("S", down_ref, [ys_ref, rs_ref], layers, size)
    sender.wait()


def call(body, layers, size, outs, spaces, scratch=(), limit=24, out_spaces=None, aliases=None):
    return pl.pallas_call(
        functools.partial(body, layers, size),
        out_shape=[jax.ShapeDtypeStruct(shape, F32) for shape in outs],
        in_specs=[pl.BlockSpec(memory_space=space) for space in spaces],
        out_specs=[pl.BlockSpec(memory_space=space) for space in out_spaces or [pltpu.VMEM] * len(outs)],
        scratch_shapes=list(scratch),
        input_output_aliases=aliases or {},
        compiler_params=pltpu.CompilerParams(vmem_limit_bytes=limit << 20),
    )


def passed_along(value, axis, by):
    peers = lax.axis_size(axis)
    return lax.ppermute(value, axis, [(i, (i + by) % peers) for i in range(peers)])


def swapped(value, axis, bit):
    peers = lax.axis_size(axis)
    return lax.ppermute(value, axis, [(i, i ^ bit) for i in range(peers)])


def shards(stored_blocks, onsite, bond_mask):
    stored, onsite, mask = stored_blocks[0, 0], onsite[0, 0], bond_mask[0, 0]
    layers, slots, size = stored.shape[:3]
    n, tall = layers * size, sym_rows(layers, size)
    panel, packed, sums, total = (n, n), (tall, n), (16, size), (8, size)
    vmem, smem, hbm = pltpu.VMEM, pltpu.SMEM, pltpu.HBM

    def blocks(count):
        return [pltpu.VMEM((count, size, size), F32), pltpu.SemaphoreType.DMA((count,))]

    go = functools.partial(call, layers=layers, size=size)
    stored, onsite, mask_hbm = (pltpu.with_memory_space_constraint(value, hbm) for value in (stored, onsite, mask))

    peers = lax.axis_size("col")
    bits = [1 << k for k in range(peers.bit_length() - 1)]
    bits = bits[:1] + bits[2:] + bits[1:2]

    def arriving(value):
        return swapped(value, "col", bits.pop(0)) if bits else jnp.zeros_like(value)

    small = [pltpu.SMEM(mask.shape, mask.dtype), pltpu.SemaphoreType.DMA]
    count = {name: len(wanted(name, layers)) for name in IN_PLANE}
    T, down = go(
        pack_body, outs=[(n + tall, n), (2 * n, n)], spaces=[hbm] * 3,
        scratch=[pltpu.VMEM((count["C"], size, size), F32), pltpu.SemaphoreType.DMA((len(wanted("CNSE", layers)),))]
        + small + [pltpu.VMEM(onsite.shape, F32), pltpu.SemaphoreType.DMA],
    )(mask_hbm, stored, onsite)
    T_x = passed_along(T, "row", -1)
    below = passed_along(down, "col", -1)
    D, gc = go(
        pack_d_body, outs=[panel, packed], spaces=[hbm] * 3, scratch=[pltpu.SemaphoreType.DMA((count["D"],))] + small
    )(mask_hbm, stored, T)
    gc_in = passed_along(gc, "col", 1)
    Cp, C, keep, own = go(sums_body, outs=[packed, panel, (layers * slots, size), sums], spaces=[smem, hbm] + [vmem] * 3)(
        mask, gc, down, T, D
    )
    if peers.bit_count() > 1:
        own = own + sum(passed_along(own, "col", by) for by in range(1, peers))
        bits = []
    while len(bits) > 3:
        own = own + arriving(own)
    more = arriving(own)
    own, g0, r0, yc_up = go(local_g_body, outs=[sums, (n + tall, n), (2 * n, n), packed], spaces=[hbm] + [vmem] * 5)(
        gc, own, more, T, down, D
    )
    more = arriving(own)
    own, out, yc, yn, ys, ye, yd = go(
        local_y_body, outs=[sums, (layers, slots, size, size), packed] + [panel] * 4, spaces=[hbm] + [vmem] * 6,
        out_spaces=[vmem, hbm] + [vmem] * 5, scratch=[pltpu.VMEM((size, size), F32), pltpu.SemaphoreType.DMA((layers * slots,))],
    )(g0, own, more, C, T, down, D)
    more = arriving(own)
    (yc_up,) = go(yc_body, outs=[(tall + 8, n)], spaces=[hbm] * 2 + [vmem])(yc, below, yc_up)
    yc_in = passed_along(yc_up, "col", 1)
    own, g = go(g_body, outs=[total, (n + tall, n)], spaces=[hbm] + [vmem] * 5)(yc_up, own, more, g0, below, gc_in)
    g_in = passed_along(g, "row", 1)
    Cp_u = passed_along(Cp, "col", -1)
    (re,) = go(r_e_body, outs=[panel], spaces=[hbm] + [vmem] * 3)(g, r0, below, T_x)
    (rs,) = go(r_s_body, outs=[panel], spaces=[hbm] + [vmem] * 3)(re, r0, below, T_x)
    (rs,) = go(copy_body, outs=[panel], spaces=[hbm] * 2 + [vmem])(yc_in, re, rs)
    rs_in, re_in = passed_along(rs, "col", 1), passed_along(re, "col", 1)
    (Cp_x,) = go(hand_body, outs=[packed], spaces=[hbm] * 2 + [vmem])(rs, Cp_u, T_x)
    Cp_xu = passed_along(Cp_x, "col", -1)
    yn, ye, yd = go(early_body, outs=[panel] * 3, spaces=[hbm] + [vmem] * 8)(Cp_x, T, down, D, below, Cp_u, yn, ye, yd)
    ye, yd = go(middle_body, outs=[panel, panel], spaces=[hbm] + [vmem] * 5)(yn, down, D, T_x, ye, yd)
    early_sums = own
    own, yd = go(middle_c_body, outs=[total, panel], spaces=[hbm] + [vmem] * 4)(ye, own, D, Cp_xu, yd)
    every = [own] + [passed_along(own if by == 1 else early_sums, "row", -by) for by in range(1, lax.axis_size("row") - 1)]
    _, *ready = go(ready_body, outs=[total] + [panel] * 4, spaces=[vmem, hbm] + [vmem] * 6)(
        keep, yd, own, D, down, yd, ye, re_in
    )
    cells = lax.axis_size("row") * lax.axis_size("col") * layers
    target = float(cells * size // 2)
    out, twice = go(
        functools.partial(last_c_body, target), outs=[out.shape, total], out_spaces=[hbm, vmem],
        spaces=[vmem, hbm] + [vmem] * (10 + len(every)), scratch=blocks(len(wanted("CNED", layers))), aliases={1: 0},
    )(keep, out, C, T, yc, yn, yc_in, g_in, *ready, *every)
    (out,) = go(
        last_s_body, outs=[out.shape], out_spaces=[hbm], spaces=[vmem, hbm] + [vmem] * 4,
        scratch=blocks(count["S"]), aliases={1: 0},
    )(keep, out, twice, down, ys, rs_in)
    return out[None, None]


def solution(mesh):
    in_specs = (
        P("row", "col", None, None, None, None),
        P("row", "col", None, None),
        P("row", "col", None, None),
    )
    out_specs = P("row", "col", None, None, None, None)
    return jax.shard_map(shards, mesh=mesh, in_specs=in_specs, out_specs=out_specs, check_vma=False)
```
